32 devices in a mesh: pipe: 2 (over core), seq: 4 (over z), tensor: 4 (over y, x).
Axes of the slice: x: 2, y: 2, z: 4, core: 2. Of those that a mesh axis runs over, the one named last changes fastest.
Arguments:
- inputs: bfloat16 [2, 2048, 1024], P(None, 'seq'), may hold values from -6 to 6
- cotangent: bfloat16 [2, 2048, 1024], P(None, 'seq'), may hold values from -6 to 6
- doc_lengths: int32 [2, 8], replicated, may hold values from 1 to 1600, as said below
- norm_one: float32 [2, 1024], P('pipe'), may hold values from 0.5 to 1.5
- w_gate_z: bfloat16 [2, 1024, 1536], P('pipe', None, 'tensor'), may hold values from -0.1875 to 0.1875
- w_inner_x: bfloat16 [2, 1024, 1536], P('pipe', None, 'tensor'), may hold values from -0.1875 to 0.1875
- w_bc: bfloat16 [2, 1024, 256], P('pipe'), may hold values from -0.1875 to 0.1875
- w_step: bfloat16 [2, 1024, 24], P('pipe', None, 'tensor'), may hold values from -0.1875 to 0.1875
- conv_inner: float32 [2, 4, 1536], P('pipe', None, 'tensor'), may hold values from -4 to 4
- conv_bc: float32 [2, 4, 256], P('pipe'), may hold values from -4 to 4
- step_bias: float32 [2, 24], P('pipe', 'tensor'), may hold values from -8 to -4
- decay_log: float32 [2, 24], P('pipe', 'tensor'), may hold values from -1 to 1
- skip_gain: float32 [2, 24], P('pipe', 'tensor'), may hold values from 0.5 to 1.5
- w_mix_out: bfloat16 [2, 1536, 1024], P('pipe', 'tensor'), may hold values from -0.15625 to 0.15625
- w_query: bfloat16 [2, 1024, 512], P('pipe', None, 'tensor'), may hold values from -0.1875 to 0.1875
- keyval_weight: bfloat16 [2, 1024, 256], P('pipe'), may hold values from -0.1875 to 0.1875
- w_attn_out: bfloat16 [2, 512, 1024], P('pipe', 'tensor'), may hold values from -2 to 2
- norm_two: float32 [2, 1024], P('pipe'), may hold values from 0.5 to 1.5
- w_gate_up: bfloat16 [2, 2, 1024, 2048], P('pipe', None, None, 'tensor'), may hold values from -0.1875 to 0.1875
- w_down: bfloat16 [2, 2048, 1024], P('pipe', 'tensor'), may hold values from -0.125 to 0.125
Outputs:
- layer_out: bfloat16 [2, 2, 2048, 1024], P('pipe', None, 'seq')
- input_grad: bfloat16 [2, 2, 2048, 1024], P('pipe', None, 'seq')
- grad_norm_one: float32 [2, 1024], P('pipe')
- grad_w_gate_z: float32 [2, 1024, 1536], P('pipe', None, 'tensor')
- grad_w_inner_x: float32 [2, 1024, 1536], P('pipe', None, 'tensor')
- grad_w_bc: float32 [2, 1024, 256], P('pipe')
- grad_w_step: float32 [2, 1024, 24], P('pipe', None, 'tensor')
- grad_conv_inner: float32 [2, 4, 1536], P('pipe', None, 'tensor')
- grad_conv_bc: float32 [2, 4, 256], P('pipe')
- grad_step_bias: float32 [2, 24], P('pipe', 'tensor')
- grad_decay_log: float32 [2, 24], P('pipe', 'tensor')
- grad_skip_gain: float32 [2, 24], P('pipe', 'tensor')
- grad_w_mix_out: float32 [2, 1536, 1024], P('pipe', 'tensor')
- grad_w_query: float32 [2, 1024, 512], P('pipe', None, 'tensor')
- grad_w_keyval: float32 [2, 1024, 256], P('pipe')
- grad_w_attn_out: float32 [2, 512, 1024], P('pipe', 'tensor')
- grad_norm_two: float32 [2, 1024], P('pipe')
- grad_w_gate_up: float32 [2, 2, 1024, 2048], P('pipe', None, None, 'tensor')
- grad_w_down: float32 [2, 2048, 1024], P('pipe', 'tensor')
The draws below stay inside these ranges and needn't reach their ends.
Inputs may be any that keep to these rules, and one draw needn't show every extreme that they name: `doc_lengths`: each row holds 8 positive document lengths that sum to 2048; the first is never the longest, and the longest is the only one above 127.
All inputs are finite; a program needn't handle non-finite values.
Results may differ from the reference program's by a relative error of at most 0.04.
Values may be sent and summed in bfloat16 or wider, within the bound.
No kernel may reach another device: no remote copies, remote signals or barrier semaphores. Data moves between devices by JAX's collectives and lax.ppermute only.
A program may use at most 256 MiB of HBM per device.

```python
from functools import partial
import jax
import jax.numpy as jnp
from jax import lax

MODEL_WIDTH = 1024
HS = 24
P_SIZE = 64
N = 128
KC = 4
QUERY_HEADS = 8
KEY_HEADS = 2
HEAD_WIDTH = 64
FF = 2048
DI = 1536
TOK_DEV = 512
PACKED_LENGTH = 2048
MICRO = 2
DOCS = 8
BLOCK = 256
KBLK = 512
N_PIPE = 2


def one_pack(key):
    pick_key, size_key = jax.random.split(key)
    quarter = TOK_DEV // DOCS
    long_index = jax.random.randint(pick_key, (), 1, DOCS)
    spread = jax.random.randint(size_key, (DOCS - 1,), 0, quarter)
    spread = spread.at[0].set(0).at[1].set(quarter - 1)
    shorts = (quarter + spread - jnp.roll(spread, -1)).astype(jnp.int32)
    long_length = PACKED_LENGTH - (DOCS - 1) * quarter
    slots = jnp.arange(DOCS)
    short_index = jnp.clip(jnp.where(slots < long_index, slots, slots - 1), 0, DOCS - 2)
    picked = jnp.take(shorts, short_index)
    return jnp.where(slots == long_index, long_length, picked).astype(jnp.int32)


def draw_doc_lengths(key, part):
    key = jax.random.fold_in(key, 11)
    pack_keys = jax.random.split(key, MICRO)
    return jnp.stack([one_pack(pack_keys[micro_slot]) for micro_slot in range(MICRO)])


def block_scale(key, shape, cuts, smallest, top_value):
    def one(axis_at, shards_of):
        steps = jax.random.uniform(jax.random.fold_in(jax.random.fold_in(key, 6), axis_at), (shards_of,), jnp.float32, smallest / len(cuts), top_value / len(cuts))
        return jnp.repeat(jnp.exp(steps), shape[axis_at] // shards_of).reshape((-1,) + (1,) * (len(shape) - axis_at - 1))

    loudness = one(*cuts[0])
    for cut in cuts[1:]:
        loudness = loudness * one(*cut)
    return loudness


def normal_values(rng, shape, deviation, bound, cuts=(), kind=jnp.bfloat16):
    level = block_scale(rng, shape, cuts, -0.22, 0.18) if cuts else 1.0
    drawn = jax.random.normal(rng, shape, jnp.float32) * deviation * level
    return jnp.minimum(jnp.maximum(drawn, -bound), bound).astype(kind)


def setup_inputs(seed: int = 0) -> dict:
    key_list = jax.random.split(jax.random.key(seed), 21)
    inputs = normal_values(key_list[0], (MICRO, PACKED_LENGTH, MODEL_WIDTH), 1.0, 6.0, ((1, 4),))
    cotangent = normal_values(key_list[1], (MICRO, PACKED_LENGTH, MODEL_WIDTH), 1.0, 6.0, ((1, 4),))
    doc_lengths = draw_doc_lengths(jax.random.fold_in(key_list[20], 71), 0)
    norm_one = jnp.clip(1.0 + 0.1 * jax.random.normal(key_list[3], (N_PIPE, MODEL_WIDTH), jnp.float32), 0.5, 1.5)
    w_gate_z = normal_values(key_list[4], (N_PIPE, MODEL_WIDTH, DI), MODEL_WIDTH ** -0.5, 0.1875, ((0, 2), (2, 4)))
    w_inner_x = normal_values(key_list[5], (N_PIPE, MODEL_WIDTH, DI), MODEL_WIDTH ** -0.5, 0.1875, ((0, 2), (2, 4)))
    w_bc = normal_values(key_list[6], (N_PIPE, MODEL_WIDTH, 2 * N), MODEL_WIDTH ** -0.5, 0.1875, ((0, 2),))
    w_step = normal_values(key_list[7], (N_PIPE, MODEL_WIDTH, HS), MODEL_WIDTH ** -0.5, 0.1875, ((0, 2), (2, 4)))
    conv_inner = normal_values(key_list[8], (N_PIPE, KC, DI), 1.0, 4.0, ((0, 2), (2, 4)), jnp.float32)
    conv_bc = normal_values(key_list[9], (N_PIPE, KC, 2 * N), 1.0, 4.0, ((0, 2),), jnp.float32)
    step_bias = jnp.clip(-8.0 + 4.0 * jax.random.uniform(key_list[10], (N_PIPE, HS), jnp.float32) ** block_scale(key_list[10], (N_PIPE, HS), ((0, 2), (1, 4)), -0.2, 0.2), -8.0, -4.0)
    decay_log = jnp.clip(jax.random.uniform(key_list[11], (N_PIPE, HS), jnp.float32, -1.0, 1.0) * block_scale(key_list[11], (N_PIPE, HS), ((0, 2), (1, 4)), -0.4, 0.0), -1.0, 1.0)
    skip_gain = jnp.clip(0.5 + 1.0 * jax.random.uniform(key_list[12], (N_PIPE, HS), jnp.float32) ** block_scale(key_list[12], (N_PIPE, HS), ((0, 2), (1, 4)), -0.2, 0.2), 0.5, 1.5)
    w_mix_out = normal_values(key_list[13], (N_PIPE, DI, MODEL_WIDTH), DI ** -0.5, 0.15625, ((0, 2), (1, 4)))
    w_query = normal_values(key_list[14], (N_PIPE, MODEL_WIDTH, QUERY_HEADS * HEAD_WIDTH), MODEL_WIDTH ** -0.5, 0.1875, ((0, 2), (2, 4)))
    keyval_weight = normal_values(key_list[15], (N_PIPE, MODEL_WIDTH, 2 * KEY_HEADS * HEAD_WIDTH), MODEL_WIDTH ** -0.5, 0.1875, ((0, 2),))
    w_attn_out = normal_values(key_list[16], (N_PIPE, QUERY_HEADS * HEAD_WIDTH, MODEL_WIDTH), 8 ** -0.5, 2.0, ((0, 2), (1, 4)))
    norm_two = jnp.clip(1.0 + 0.1 * jax.random.normal(key_list[17], (N_PIPE, MODEL_WIDTH), jnp.float32), 0.5, 1.5)
    w_gate_up = normal_values(key_list[18], (N_PIPE, 2, MODEL_WIDTH, FF), MODEL_WIDTH ** -0.5, 0.1875, ((0, 2), (3, 4)))
    w_down = normal_values(key_list[19], (N_PIPE, FF, MODEL_WIDTH), FF ** -0.5, 0.125, ((0, 2), (1, 4)))
    return {"inputs": inputs, "cotangent": cotangent, "doc_lengths": doc_lengths, "norm_one": norm_one, "w_gate_z": w_gate_z, "w_inner_x": w_inner_x, "w_bc": w_bc, "w_step": w_step, "conv_inner": conv_inner, "conv_bc": conv_bc, "step_bias": step_bias, "decay_log": decay_log, "skip_gain": skip_gain, "w_mix_out": w_mix_out, "w_query": w_query, "keyval_weight": keyval_weight, "w_attn_out": w_attn_out, "norm_two": norm_two, "w_gate_up": w_gate_up, "w_down": w_down}


@jax.custom_vjp
def lower_bound(v):
    return lax.optimization_barrier(v.astype(jnp.bfloat16)).astype(jnp.float32)

@jax.custom_vjp
def low_back(v):
    return v

def low_keep(v):
    return (lower_bound(v), None)

def low_pass(kept, grad):
    return (grad,)

def back_keep(v):
    return (v, None)

def back_low(kept, grad):
    return (lower_bound(grad),)
lower_bound.defvjp(low_keep, low_pass)
low_back.defvjp(back_keep, back_low)
highest = lax.Precision.HIGHEST
eps_norm = 1e-05
rope_base = 100000000000.0
masked_score = -1e+30

def matmul(left_side, right_side):
    return jnp.dot(left_side, right_side, precision=highest)

def rms_norm(value_matrix, gain):
    return value_matrix * lax.rsqrt(lax.optimization_barrier(jnp.mean(value_matrix * value_matrix, axis=-1, keepdims=True)) + eps_norm) * gain

def documents(lengths_row, positions):
    doc_ends = jnp.cumsum(lengths_row).astype(jnp.int32)
    before = doc_ends[None, :] <= positions[:, None]
    segment = lax.optimization_barrier(jnp.sum(before.astype(jnp.int32), axis=1)).astype(jnp.int32)
    doc_starts = lax.optimization_barrier(jnp.sum(jnp.where(before, lengths_row[None, :], 0), axis=1)).astype(jnp.int32)
    return (segment, (positions - doc_starts).astype(jnp.int32))

def rotary_embed(value_matrix, position_offsets):
    half_size = value_matrix.shape[-1] // 2
    frequency = rope_base ** (-2.0 * jnp.arange(half_size, dtype=jnp.float32) / value_matrix.shape[-1])
    angles = position_offsets.astype(jnp.float32)[:, None] * frequency[None, :]
    cosine = jnp.cos(angles)[:, None, :]
    sine = jnp.sin(angles)[:, None, :]
    first_half = value_matrix[..., :half_size]
    second_half = value_matrix[..., half_size:]
    return jnp.concatenate([first_half * cosine - second_half * sine, second_half * cosine + first_half * sine], axis=-1)

def conv_silu(extended, kernel, segment_ext, valid_ext):
    row_count = extended.shape[0] - (KC - 1)
    own_segment = segment_ext[KC - 1:]
    summed = jnp.zeros((row_count, extended.shape[1]), jnp.float32)
    for tap_index in range(KC):
        window = extended[tap_index:tap_index + row_count]
        keep_tap = (segment_ext[tap_index:tap_index + row_count] == own_segment) & valid_ext[tap_index:tap_index + row_count]
        summed = summed + jnp.where(keep_tap[:, None], window, 0.0) * kernel[tap_index]
    return jax.nn.silu(summed)

def ssm_block(carried, block):
    state, previous = carried
    inner_u, step_size, log_decay, input_map, output_map, segment = block
    cumulative = jnp.cumsum(log_decay, axis=0)
    positions = jnp.arange(segment.shape[0])
    allowed = (segment[:, None] == segment[None, :]) & (positions[:, None] >= positions[None, :])
    gaps = jnp.where(allowed[:, :, None], cumulative[:, None, :] - cumulative[None, :, :], 0.0)
    decays = jnp.where(allowed[:, :, None], jnp.exp(gaps), 0.0)
    intersection = jnp.dot(output_map, input_map.T, precision=highest)
    weights = decays * intersection[:, :, None] * step_size[None, :, :]
    inner_part = jnp.einsum('tsh,shp->thp', weights, inner_u, precision=highest)
    linked = jnp.where((segment == previous)[:, None], jnp.exp(cumulative), 0.0)
    outer_part = jnp.einsum('tn,hpn->thp', output_map, state, precision=highest) * linked[:, :, None]
    at_tail = (segment == segment[-1])[:, None]
    towards_end = jnp.where(at_tail, jnp.exp(cumulative[-1][None, :] - cumulative), 0.0) * step_size
    carried_keep = jnp.where(segment[-1] == previous, jnp.exp(cumulative[-1]), 0.0)
    fresh = jnp.einsum('sh,shp,sn->hpn', towards_end, inner_u, input_map, precision=highest)
    return ((carried_keep[:, None, None] * state + fresh, segment[-1]), inner_part + outer_part)

def ssm(inner_u, step_size, log_decay, input_map, output_map, segment):
    block_count = PACKED_LENGTH // BLOCK
    start_state = (jnp.zeros((HS, P_SIZE, N), jnp.float32), jnp.array(-1, dtype=jnp.int32))
    pieces = (inner_u.reshape(block_count, BLOCK, HS, P_SIZE), step_size.reshape(block_count, BLOCK, HS), log_decay.reshape(block_count, BLOCK, HS), input_map.reshape(block_count, BLOCK, N), output_map.reshape(block_count, BLOCK, N), segment.reshape(block_count, BLOCK))
    unused_state, outputs = lax.scan(jax.checkpoint(ssm_block), start_state, pieces)
    return outputs.reshape(PACKED_LENGTH, HS, P_SIZE)

def attention(queries, key_matrix, value_matrix, segment):
    positions = jnp.arange(PACKED_LENGTH, dtype=jnp.int32)
    query_group_width = QUERY_HEADS // KEY_HEADS
    keys_wide = jnp.repeat(key_matrix, query_group_width, axis=1)
    values_wide = jnp.repeat(value_matrix, query_group_width, axis=1)
    block_count = PACKED_LENGTH // KBLK

    def one_block(pieces):
        query_rows, query_segment, query_places = pieces
        raw_scores = low_back(jnp.einsum('qhd,khd->hqk', query_rows, keys_wide, precision=highest))
        allowed = (query_segment[:, None] == segment[None, :]) & (query_places[:, None] >= positions[None, :])
        scores = jnp.where(allowed[None], raw_scores * HEAD_WIDTH ** (-0.5), masked_score)
        shifted = jnp.exp(scores - lax.optimization_barrier(jnp.max(scores, axis=-1, keepdims=True)))
        probs = lower_bound(shifted / lax.optimization_barrier(jnp.sum(shifted, axis=-1, keepdims=True)))
        return jnp.einsum('hqk,khd->qhd', probs, values_wide, precision=highest).reshape(KBLK, QUERY_HEADS * HEAD_WIDTH)
    outputs = lax.map(jax.checkpoint(one_block), (queries.reshape(block_count, KBLK, QUERY_HEADS, HEAD_WIDTH), segment.reshape(block_count, KBLK), positions.reshape(block_count, KBLK)))
    return outputs.reshape(PACKED_LENGTH, QUERY_HEADS * HEAD_WIDTH)

def layer(section_input, params, lengths_row):
    gain_one, proj_gate, proj_inner, proj_maps, proj_step, kernel_inner, kernel_maps, shift_step, rate_log, skip_term, proj_mixout, proj_query, proj_keyval, proj_attnout, gain_two, proj_gateup, proj_down = params
    ext_places = jnp.arange(PACKED_LENGTH + KC - 1, dtype=jnp.int32) - (KC - 1)
    segment_ext, offsets_ext = documents(lengths_row, ext_places)
    valid_ext = ext_places >= 0
    segment = segment_ext[KC - 1:]
    position_offsets = offsets_ext[KC - 1:]
    normed_one = lower_bound(rms_norm(section_input, gain_one))
    gate_raw = low_back(matmul(normed_one, proj_gate))
    inner = lower_bound(low_back(matmul(normed_one, proj_inner)))
    maps = lower_bound(low_back(matmul(normed_one, proj_maps)))
    step_raw = low_back(matmul(normed_one, proj_step))
    inner_u = conv_silu(jnp.concatenate([jnp.zeros((KC - 1, DI), jnp.float32), inner], axis=0), kernel_inner, segment_ext, valid_ext).reshape(PACKED_LENGTH, HS, P_SIZE)
    maps_out = conv_silu(jnp.concatenate([jnp.zeros((KC - 1, 2 * N), jnp.float32), maps], axis=0), kernel_maps, segment_ext, valid_ext)
    step_size = jax.nn.softplus(step_raw + shift_step)
    log_decay = -step_size * jnp.exp(rate_log)
    mixed = ssm(inner_u, step_size, log_decay, maps_out[:, :N], maps_out[:, N:], segment) + skip_term[None, :, None] * inner_u
    gated = lower_bound((mixed * jax.nn.silu(gate_raw).reshape(PACKED_LENGTH, HS, P_SIZE)).reshape(PACKED_LENGTH, DI))
    queries = lower_bound(rotary_embed(low_back(matmul(normed_one, proj_query)).reshape(PACKED_LENGTH, QUERY_HEADS, HEAD_WIDTH), position_offsets))
    keyval_projected = low_back(matmul(normed_one, proj_keyval))
    key_matrix = lower_bound(rotary_embed(keyval_projected[:, :KEY_HEADS * HEAD_WIDTH].reshape(PACKED_LENGTH, KEY_HEADS, HEAD_WIDTH), position_offsets))
    value_matrix = lower_bound(keyval_projected[:, KEY_HEADS * HEAD_WIDTH:].reshape(PACKED_LENGTH, KEY_HEADS, HEAD_WIDTH))
    attn = lower_bound(low_back(attention(queries, key_matrix, value_matrix, segment)))
    branch = low_back(matmul(gated, proj_mixout) + matmul(attn, proj_attnout))
    resid = section_input + branch
    normed_two = lower_bound(rms_norm(resid, gain_two))
    gate = low_back(matmul(normed_two, proj_gateup[0]))
    up_value = low_back(matmul(normed_two, proj_gateup[1]))
    hidden = lower_bound(jax.nn.silu(gate) * up_value)
    return resid + low_back(matmul(hidden, proj_down))

def section_run(section_input, params, doc_lengths):
    return jnp.stack([layer(section_input[micro_slot], params, doc_lengths[micro_slot]) for micro_slot in range(MICRO)])

def reference(inputs, cotangent, doc_lengths, norm_one, w_gate_z, w_inner_x, w_bc, w_step, conv_inner, conv_bc, step_bias, decay_log, skip_gain, w_mix_out, w_query, keyval_weight, w_attn_out, norm_two, w_gate_up, w_down):
    stacked = [weight.astype(jnp.float32) for weight in (norm_one, w_gate_z, w_inner_x, w_bc, w_step, conv_inner, conv_bc, step_bias, decay_log, skip_gain, w_mix_out, w_query, keyval_weight, w_attn_out, norm_two, w_gate_up, w_down)]
    first_section = [weight[0] for weight in stacked]
    second_section = [weight[1] for weight in stacked]
    runner = partial(section_run, doc_lengths=doc_lengths)
    out_first, back_first = jax.vjp(runner, inputs.astype(jnp.float32), first_section)
    sent = lower_bound(out_first)
    out_second, back_second = jax.vjp(runner, sent, second_section)
    d_sent, grads_second = back_second(cotangent.astype(jnp.float32))
    d_inputs, grads_first = back_first(lower_bound(d_sent))
    layer_out = jnp.stack([sent, out_second]).astype(jnp.bfloat16)
    input_grad = jnp.stack([d_inputs, d_sent]).astype(jnp.bfloat16)
    grads = [jnp.stack([first_grad, second_grad]) for first_grad, second_grad in zip(grads_first, grads_second)]
    return (layer_out, input_grad, grads[0], grads[1], grads[2], grads[3], grads[4], grads[5], grads[6], grads[7], grads[8], grads[9], grads[10], grads[11], grads[12], grads[13], grads[14], grads[15], grads[16])
```

```python
from functools import partial

import jax
import jax.numpy as jnp
from jax import lax
from jax.experimental import pallas as pl
from jax.experimental.pallas import tpu as pltpu
from jax.sharding import PartitionSpec as P

P_SIZE = 64
N = 128
KC = 4
KEY_HEADS = 2
QUERY_HEADS = 8
HEAD_WIDTH = 64
CHUNK = 128
LANES = 128
HALO = 16

f32 = jnp.float32
bf16 = jnp.bfloat16
highest = lax.Precision.HIGHEST
eps_norm = 1e-05
rope_base = 100000000000.0
masked_score = -1e30
score_scale = HEAD_WIDTH ** (-0.5)


def nn(a, b, precision=None):
    return lax.dot_general(
        a, b, (((1,), (0,)), ((), ())), precision=precision, preferred_element_type=f32
    )


def nt(a, b, precision=None):
    return lax.dot_general(
        a, b, (((1,), (1,)), ((), ())), precision=precision, preferred_element_type=f32
    )


def tn(a, b, precision=None):
    return lax.dot_general(
        a, b, (((0,), (0,)), ((), ())), precision=precision, preferred_element_type=f32
    )


def iota(shape, axis):
    return lax.broadcasted_iota(jnp.int32, shape, axis)


def sds(shape, kind):
    return jax.ShapeDtypeStruct(shape, kind)


def call(kernel, outs, args, scratch=(), mib=40, name=None):
    specs = [pl.BlockSpec(memory_space=pltpu.SMEM)] + [
        pl.BlockSpec(memory_space=pltpu.VMEM) for _ in args[1:]
    ]
    return pl.pallas_call(
        kernel,
        out_shape=outs,
        in_specs=specs,
        out_specs=[pl.BlockSpec(memory_space=pltpu.VMEM) for _ in outs],
        scratch_shapes=list(scratch),
        compiler_params=pltpu.CompilerParams(vmem_limit_bytes=mib * 1024 * 1024),
        name=name,
    )(*args)


def block_rows(me_ref, k, size):
    return pl.ds(pl.multiple_of((me_ref[0] ^ k) * size, size), size)


def rms_scale(x):
    return lax.rsqrt(jnp.mean(x * x, axis=-1, keepdims=True) + eps_norm)


def swap_halves(x):
    lane = iota(x.shape, 1) % HEAD_WIDTH
    ahead = pltpu.roll(x, LANES - HEAD_WIDTH // 2, 1)
    behind = pltpu.roll(x, HEAD_WIDTH // 2, 1)
    return jnp.where(lane < HEAD_WIDTH // 2, ahead, behind)


def low_lanes(shape):
    return iota(shape, 1) < HEAD_WIDTH


def project_kernel(pieces, di, me_ref, *refs):
    xs = refs[:pieces]
    gain_ref, w_ref, cos_ref, sin_ref, h_ref, z_ref, im_ref, step_ref, q_ref, kv_ref = refs[pieces:]
    tokens = h_ref.shape[0]
    size = tokens // 4
    for k in range(4):
        rows = block_rows(me_ref, k, size)
        x = (xs[0][rows, :] if pieces == 1 else xs[k][...]).astype(f32)
        h = (x * rms_scale(x) * gain_ref[...]).astype(bf16)
        h_ref[rows, :] = h
        p = nn(h, w_ref[...])
        z_ref[rows, :] = p[:, :di]
        im_ref[rows, :di] = p[:, di : 2 * di].astype(bf16)
        at = 2 * di
        cos, sin = cos_ref[rows, :], sin_ref[rows, :]
        q = p[:, at : at + LANES]
        q_ref[rows, :] = (q * cos + swap_halves(q) * sin).astype(bf16)
        step_ref[rows, :] = p[:, at + LANES : at + 2 * LANES]
        im_ref[rows, di:] = p[:, at + 2 * LANES : at + 4 * LANES].astype(bf16)
        kv = p[:, at + 4 * LANES :]
        turned = kv * cos + swap_halves(kv) * sin
        kv_ref[rows, :] = jnp.where(low_lanes(kv.shape), turned, kv).astype(bf16)


def fill_ext(ext, halo_ref, im_ref):
    ext[:HALO, :] = halo_ref[...].astype(f32)
    ext[HALO:, :] = im_ref[...].astype(f32)


def triangle(lower):
    r, c = iota((CHUNK, CHUNK), 0), iota((CHUNK, CHUNK), 1)
    return jnp.where((c <= r) if lower else (c >= r), 1.0, 0.0).astype(f32)


def expand(cols, i):
    shape = (cols.shape[0], LANES)
    return jnp.where(
        low_lanes(shape),
        jnp.broadcast_to(cols[:, 2 * i : 2 * i + 1], shape),
        jnp.broadcast_to(cols[:, 2 * i + 1 : 2 * i + 2], shape),
    )


def expand_all(cols, tiles):
    return jnp.concatenate([expand(cols, i) for i in range(tiles)], axis=1)


def per_state_row(row, heads):
    return jnp.concatenate(
        [jnp.broadcast_to(row[:, h : h + 1], (P_SIZE, N)) for h in range(heads)], axis=0
    )


def chunk_steps(c, step_ref, dsl_ref, par_ref):
    r0 = c * CHUNK
    rows = slice(r0, r0 + CHUNK)
    raw = step_ref[rows, :] + par_ref[0:1, :]
    dt = jnp.maximum(raw, 0.0) + jnp.log1p(jnp.exp(-jnp.abs(raw)))
    ld = -dt * par_ref[1:2, :]
    cum = nn(triangle(True), ld, highest)
    dsl = dsl_ref[rows, :]
    place = r0 + iota((CHUNK, LANES), 0)
    end = cum[CHUNK - 1 : CHUNK, :]
    dsl_end = dsl[CHUNK - 1 : CHUNK, :]
    to_end = jnp.where(place >= dsl_end, jnp.exp(end - cum), 0.0)
    link = jnp.where(dsl < r0, jnp.exp(cum), 0.0)
    keep = jnp.where(dsl_end < r0, jnp.exp(end), 0.0)
    allowed = (iota((CHUNK, CHUNK), 1) <= iota((CHUNK, CHUNK), 0)) & (
        r0 + iota((CHUNK, CHUNK), 1) >= dsl
    )
    return raw, dt, ld, cum, dsl, place - dsl, end, to_end, link, keep, allowed


def chunk_conv(c, off, ext, kern_ref, tiles):
    r0 = c * CHUNK
    keeps = [jnp.where(off >= KC - 1 - j, 1.0, 0.0) for j in range(KC)]
    outs = []
    for i in range(tiles):
        cols = slice(i * LANES, (i + 1) * LANES)
        acc = None
        for j in range(KC):
            at = r0 + HALO - (KC - 1) + j
            term = ext[at : at + CHUNK, cols] * keeps[j] * kern_ref[j : j + 1, cols]
            acc = term if acc is None else acc + term
        outs.append(acc)
    return outs


def decays(cum, cum_t, allowed, h):
    gap = cum[:, h : h + 1] - cum_t[h : h + 1, :]
    return jnp.exp(jnp.where(allowed, gap, masked_score))


def both(a0, a1, axis):
    return jnp.concatenate([a0, a1], axis=axis)


def split_pair(x):
    low = low_lanes(x.shape)
    return both(jnp.where(low, x, 0.0), jnp.where(low, 0.0, x), 0)


def ssm_forward_kernel(
    heads, me_ref, im_ref, halo_ref, step_ref, dsl_ref, kern_ref, par_ref,
    mix_ref, cmap_ref, lfac_ref, packet_ref, ext, state,
):
    tokens = im_ref.shape[0]
    pairs = heads // 2
    fill_ext(ext, halo_ref, im_ref)
    state[...] = jnp.zeros_like(state)
    base = jnp.zeros((1, LANES), f32)
    for c in range(tokens // CHUNK):
        rows = slice(c * CHUNK, (c + 1) * CHUNK)
        raw, dt, ld, cum, dsl, off, end, to_end, link, keep, allowed = chunk_steps(
            c, step_ref, dsl_ref, par_ref
        )
        acts = [a * jax.nn.sigmoid(a) for a in chunk_conv(c, off, ext, kern_ref, pairs + 2)]
        bmap, cmap = acts[pairs].astype(bf16), acts[pairs + 1].astype(bf16)
        cum_t, dt_t = cum.T, dt.T
        cross = nt(cmap, bmap)
        carried = nt(cmap, state[...].astype(bf16)) if c else None
        ins = to_end * dt
        fed = []
        for i in range(pairs):
            u = acts[i]
            weights = [
                (decays(cum, cum_t, allowed, h) * cross * dt_t[h : h + 1, :]).astype(bf16)
                for h in (2 * i, 2 * i + 1)
            ]
            cols = slice(i * LANES, (i + 1) * LANES)
            y = nn(both(*weights, 1), split_pair(u).astype(bf16))
            if c:
                y = y + carried[:, cols] * expand(link, i)
            mix_ref[rows, cols] = y + kern_ref[KC : KC + 1, cols] * u
            fed.append((u * expand(ins, i)).astype(bf16))
        fresh = tn(jnp.concatenate(fed, axis=1), bmap)
        state[...] = per_state_row(keep, heads) * state[...] + fresh
        cmap_ref[rows, :] = cmap
        lfac = jnp.where(dsl < 0, jnp.exp(base + cum), 0.0)
        lfac_ref[rows, :] = lfac
        base = base + end
    packet_ref[: heads * P_SIZE, :] = state[...].astype(bf16)
    packet_ref[heads * P_SIZE :, :] = jnp.broadcast_to(
        lfac[CHUNK - 1 : CHUNK, :], (HALO, LANES)
    ).astype(bf16)


def arriving(packets, heads):
    total = None
    for ref in packets[::-1]:
        own = ref[: heads * P_SIZE, :].astype(f32)
        if total is not None:
            row = ref[heads * P_SIZE : heads * P_SIZE + 1, :].astype(f32)
            own = own + per_state_row(row, heads) * total
        total = own
    return total


def mix_kernel(heads, packets, me_ref, *refs):
    ins = refs[:packets]
    (mix_ref, cmap_ref, lfac_ref, z_ref, attn_ref, w_ref,
     mixed_ref, ga_ref, state_ref, own_ref, *part_refs) = refs[packets:]
    tokens = mix_ref.shape[0]
    size = tokens // 4
    pairs = heads // 2
    di = heads * P_SIZE
    if packets:
        state = arriving(ins, heads)
    else:
        state = jnp.zeros(state_ref.shape, f32)
    state_ref[...] = state
    state = state.astype(bf16)
    for k in (1, 2, 3, 0):
        rows = block_rows(me_ref, k, size)
        carried = nt(cmap_ref[rows, :], state)
        mixed = mix_ref[rows, :] + carried * expand_all(lfac_ref[rows, :], pairs)
        mixed_ref[rows, :] = mixed
        z = z_ref[rows, :]
        ga_ref[rows, :di] = (mixed * z * jax.nn.sigmoid(z)).astype(bf16)
        ga_ref[rows, di:] = attn_ref[rows, :].astype(bf16)
        part = nn(ga_ref[rows, :], w_ref[...])
        if k:
            part_refs[k - 1][...] = part.astype(bf16)
        else:
            own_ref[...] = part


def spread_keyval(ref):
    kv = ref[...].astype(f32)
    other = pltpu.roll(kv, HEAD_WIDTH, 1)
    low = low_lanes(kv.shape)
    return (
        jnp.where(low, kv, other).astype(bf16),
        jnp.where(low, other, kv).astype(bf16),
    )


def pair_mask(r0, d, tokens, dsl):
    shape = (CHUNK, tokens)
    key = iota(shape, 1) - d * tokens
    ok = key >= jnp.broadcast_to(dsl[:, 0:1], shape)
    if d == 0:
        ok = ok & (key <= r0 + iota(shape, 0))
    return both(ok, ok, 0)


def attention_kernel(blocks, me_ref, q_ref, dsl_ref, *refs):
    kvs = refs[:blocks]
    attn_ref, lse_ref, keys, values = refs[blocks:]
    tokens = q_ref.shape[0]
    for d in range(blocks):
        keys[d], values[d] = spread_keyval(kvs[d])
    for c in range(tokens // CHUNK):
        r0 = c * CHUNK
        rows = slice(r0, r0 + CHUNK)
        q = split_pair(q_ref[rows, :].astype(f32)).astype(bf16)
        dsl = dsl_ref[rows, :]
        top = total = acc = None
        for d in range(blocks):
            ok = pair_mask(r0, d, tokens, dsl)
            scores = jnp.where(ok, nt(q, keys[d]) * score_scale, masked_score)
            block_top = jnp.max(scores, axis=1, keepdims=True)
            if d == 0:
                top = block_top
                weights = jnp.exp(scores - top)
                total = jnp.sum(weights, axis=1, keepdims=True)
                acc = nn(weights.astype(bf16), values[d])
            else:
                new_top = jnp.maximum(top, block_top)
                factor = jnp.exp(top - new_top)
                weights = jnp.exp(scores - new_top)
                total = total * factor + jnp.sum(weights, axis=1, keepdims=True)
                acc = acc * factor + nn(weights.astype(bf16), values[d])
                top = new_top
        out = acc / total
        low = low_lanes((CHUNK, LANES))
        attn_ref[rows, :] = jnp.where(low, out[:CHUNK], out[CHUNK:])
        lse = jnp.broadcast_to(top + jnp.log(total), (2 * CHUNK, LANES))
        lse_ref[rows, :] = jnp.where(low, lse[:CHUNK], lse[CHUNK:])


def attention_back_kernel(blocks, me_ref, q_ref, dsl_ref, attn_ref, lse_ref, dattn_ref, *refs):
    kvs = refs[:blocks]
    dq_ref = refs[blocks]
    outs = refs[blocks + 1 : 2 * blocks + 1]
    keys, values, dkeys, dvalues = refs[2 * blocks + 1 :]
    tokens = q_ref.shape[0]
    low = low_lanes((CHUNK, LANES))
    for d in range(blocks):
        keys[d], values[d] = spread_keyval(kvs[d])
    for c in range(tokens // CHUNK):
        r0 = c * CHUNK
        rows = slice(r0, r0 + CHUNK)
        q = split_pair(q_ref[rows, :].astype(f32)).astype(bf16)
        dout = dattn_ref[rows, :].astype(f32)
        prod = split_pair(dout * attn_ref[rows, :])
        delta = jnp.sum(prod, axis=1, keepdims=True)
        dout = split_pair(dout).astype(bf16)
        lse = lse_ref[rows, :]
        lse = both(lse[:, 0:1], lse[:, HEAD_WIDTH : HEAD_WIDTH + 1], 0)
        dsl = dsl_ref[rows, :]
        dq = None
        for d in range(blocks):
            ok = pair_mask(r0, d, tokens, dsl)
            scores = jnp.where(ok, nt(q, keys[d]) * score_scale - lse, masked_score)
            probs = jnp.exp(scores)
            dprobs = nt(dout, values[d])
            dscores = (probs * (dprobs - delta) * score_scale).astype(bf16)
            probs = probs.astype(bf16)
            part = nn(dscores, keys[d])
            dq = part if dq is None else dq + part
            dk, dv = tn(dscores, q), tn(probs, dout)
            if c:
                dkeys[d] += dk
                dvalues[d] += dv
            else:
                dkeys[d] = dk
                dvalues[d] = dv
        dq_ref[rows, :] = jnp.where(low, dq[:CHUNK], dq[CHUNK:])
    wide = low_lanes((tokens, LANES))
    for d in range(blocks):
        dk, dv = dkeys[d], dvalues[d]
        dk = dk + pltpu.roll(dk, HEAD_WIDTH, 1)
        dv = dv + pltpu.roll(dv, HEAD_WIDTH, 1)
        outs[d][...] = jnp.where(wide, dk, dv).astype(outs[d].dtype)


def norm_two_kernel(me_ref, x_ref, own_ref, r1, r2, r3, gain_ref, resid_ref, h_ref):
    resid = x_ref[...].astype(f32) + own_ref[...]
    for r in (r1, r2, r3):
        resid = resid + r[...].astype(f32)
    resid_ref[...] = resid
    h_ref[...] = (resid * rms_scale(resid) * gain_ref[...]).astype(bf16)


def mlp_kernel(me_ref, h0, h1, h2, h3, gu_ref, down_ref, h_ref, gate_ref, up_ref, hid_ref, own_ref, *parts):
    size = h0.shape[0]
    for k, ref in ((1, h1), (2, h2), (3, h3), (0, h0)):
        rows = slice(k * size, (k + 1) * size)
        h = ref[...]
        h_ref[rows, :] = h
        gate = nn(h, gu_ref[0])
        up = nn(h, gu_ref[1])
        gate_ref[rows, :] = gate.astype(bf16)
        up_ref[rows, :] = up.astype(bf16)
        hidden = (gate * jax.nn.sigmoid(gate) * up).astype(bf16)
        hid_ref[rows, :] = hidden
        part = nn(hidden, down_ref[...])
        if k:
            parts[k - 1][...] = part.astype(bf16)
        else:
            own_ref[...] = part


def out_kernel(me_ref, resid_ref, own_ref, r1, r2, r3, out_ref):
    out = resid_ref[...] + own_ref[...]
    for r in (r1, r2, r3):
        out = out + r[...].astype(f32)
    out_ref[...] = out.astype(bf16)


def mlp_back_kernel(pieces, me_ref, *refs):
    gs = refs[:pieces]
    gate_ref, up_ref, gu_ref, down_ref, dgu_ref, g_ref, own_ref, *parts = refs[pieces:]
    ff = gate_ref.shape[1]
    size = gate_ref.shape[0] // 4
    for k in (1, 2, 3, 0):
        rows = slice(k * size, (k + 1) * size)
        g = gs[0][block_rows(me_ref, k, size), :] if pieces == 1 else gs[k][...]
        g_ref[rows, :] = g
        dhid = nt(g, down_ref[...])
        gate, up = gate_ref[rows, :].astype(f32), up_ref[rows, :].astype(f32)
        sig = jax.nn.sigmoid(gate)
        dgate = (dhid * up * sig * (1.0 + gate * (1.0 - sig))).astype(bf16)
        dup = (dhid * gate * sig).astype(bf16)
        dgu_ref[rows, :ff] = dgate
        dgu_ref[rows, ff:] = dup
        part = nt(dgate, gu_ref[0]) + nt(dup, gu_ref[1])
        if k:
            parts[k - 1][...] = part.astype(bf16)
        else:
            own_ref[...] = part


def norm_back_kernel(me_ref, base_ref, own_ref, r1, r2, r3, x_ref, gain_ref, *outs):
    low_ref, gain_grad_ref = outs[-2:]
    dh = own_ref[...]
    for r in (r1, r2, r3):
        dh = dh + r[...].astype(f32)
    x = x_ref[...].astype(f32)
    r = rms_scale(x)
    n = x * r
    gain_grad_ref[...] = jnp.broadcast_to(
        jnp.sum(dh * n, axis=0, keepdims=True), gain_grad_ref.shape
    )
    dn = dh * gain_ref[...]
    dx = base_ref[...].astype(f32) + r * (dn - n * jnp.mean(dn * n, axis=-1, keepdims=True))
    if len(outs) == 3:
        outs[0][...] = dx
    low_ref[...] = dx.astype(bf16)


def mixer_back_kernel(
    heads, me_ref, d0, d1, d2, d3, w_ref, z_ref, mixed_ref, cmap_ref, lfac_ref, passing_ref,
    dbr_ref, dmixed_ref, dz_ref, dattn_ref, packet_ref,
):
    size = d0.shape[0]
    di = heads * P_SIZE
    pairs = heads // 2
    own = None
    for k, ref in ((0, d0), (1, d1), (2, d2), (3, d3)):
        rows = block_rows(me_ref, k, size)
        d = ref[...]
        dbr_ref[rows, :] = d
        p = nt(d, w_ref[...])
        dgated = p[:, :di]
        z = z_ref[rows, :]
        sig = jax.nn.sigmoid(z)
        act = z * sig
        dmixed = dgated * act
        dmixed_ref[rows, :] = dmixed
        dz_ref[rows, :] = (dgated * mixed_ref[rows, :] * sig * (1.0 + z * (1.0 - sig))).astype(bf16)
        dattn_ref[rows, :] = p[:, di:].astype(bf16)
        linked = (dmixed * expand_all(lfac_ref[rows, :], pairs)).astype(bf16)
        part = tn(linked, cmap_ref[rows, :])
        own = part if own is None else own + part
    packet_ref[:di, :] = own.astype(bf16)
    packet_ref[di:, :] = passing_ref[di:, :]


def ssm_back_kernel(heads, packets, me_ref, *refs):
    ins = refs[:packets]
    (im_ref, halo_ref, step_ref, dsl_ref, kern_ref, par_ref, dmixed_ref, state_in_ref,
     dim_ref, dhalo_ref, dstep_ref, dkern_ref, dpar_ref,
     ext, dcs, dsl_pad, states, dstate, rows_acc) = refs[packets:]
    tokens = im_ref.shape[0]
    chunks = tokens // CHUNK
    pairs = heads // 2
    di = heads * P_SIZE
    tiles = pairs + 2
    fill_ext(ext, halo_ref, im_ref)
    pick = jnp.where(
        iota((di, LANES), 0) // P_SIZE == iota((di, LANES), 1), 1.0, 0.0
    ).astype(f32)

    states[0] = state_in_ref[...]
    for c in range(chunks - 1):
        raw, dt, ld, cum, dsl, off, end, to_end, link, keep, allowed = chunk_steps(
            c, step_ref, dsl_ref, par_ref
        )
        acts = [a * jax.nn.sigmoid(a) for a in chunk_conv(c, off, ext, kern_ref, pairs + 1)]
        ins_ = to_end * dt
        fed = jnp.concatenate([(acts[i] * expand(ins_, i)).astype(bf16) for i in range(pairs)], 1)
        states[c + 1] = per_state_row(keep, heads) * states[c] + tn(fed, acts[pairs].astype(bf16))

    if packets:
        dstate[...] = arriving(ins, heads)
    else:
        dstate[...] = jnp.zeros_like(dstate)
    dcs[:HALO, :] = jnp.zeros((HALO, tiles * LANES), f32)
    dcs[HALO + tokens :, :] = jnp.zeros((HALO, tiles * LANES), f32)
    drate = jnp.zeros((1, LANES), f32)
    dbias = jnp.zeros((1, LANES), f32)
    dskip = [jnp.zeros((1, LANES), f32) for _ in range(pairs)]
    dkern = [[jnp.zeros((1, LANES), f32) for _ in range(tiles)] for _ in range(KC)]
    rows_acc[...] = jnp.zeros_like(rows_acc)
    lane = iota((CHUNK, LANES), 1)
    for c in range(chunks - 1, -1, -1):
        r0 = c * CHUNK
        rows = slice(r0, r0 + CHUNK)
        raw, dt, ld, cum, dsl, off, end, to_end, link, keep, allowed = chunk_steps(
            c, step_ref, dsl_ref, par_ref
        )
        pre = chunk_conv(c, off, ext, kern_ref, tiles)
        sigs = [jax.nn.sigmoid(a) for a in pre]
        acts = [a * s for a, s in zip(pre, sigs)]
        bmap, cmap = acts[pairs].astype(bf16), acts[pairs + 1].astype(bf16)
        cum_t, dt_t = cum.T, dt.T
        cross = nt(cmap, bmap)
        state = states[c]
        state_low = state.astype(bf16)
        ds = dstate[...]
        ds_low = ds.astype(bf16)
        carried = nt(cmap, state_low)
        towards = nt(bmap, ds_low)
        ins_ = to_end * dt
        cross_grad = jnp.zeros((CHUNK, CHUNK), f32)
        row_sums = jnp.zeros((CHUNK, LANES), f32)
        linked, fed, link_prod, end_prod, dus = [], [], [], [], []
        for i in range(pairs):
            cols = slice(i * LANES, (i + 1) * LANES)
            u = acts[i]
            dy = dmixed_ref[rows, cols]
            dy2 = split_pair(dy).astype(bf16)
            dw2 = nt(dy2, u.astype(bf16))
            weights = []
            for s in range(2):
                h = 2 * i + s
                dw = dw2[s * CHUNK : (s + 1) * CHUNK]
                low = decays(cum, cum_t, allowed, h)
                dt_row = dt_t[h : h + 1, :]
                scaled = low * dt_row
                cross_grad = cross_grad + dw * scaled
                g = low * cross
                weights.append((g * dt_row).astype(bf16))
                r = dw * g
                rows_acc[h : h + 1, :] = jnp.sum(r, axis=0, keepdims=True)
                row_sums = jnp.where(
                    lane == h, jnp.sum(r * dt_row, axis=1, keepdims=True), row_sums
                )
            du = tn(both(*weights, 0), dy2)
            x_link = dy * expand(link, i)
            linked.append(x_link.astype(bf16))
            link_prod.append(x_link * carried[:, cols])
            x_in = expand(ins_, i)
            fed.append((u * x_in).astype(bf16))
            x_to = towards[:, cols]
            end_prod.append(u * x_to * expand(to_end, i))
            skip = kern_ref[KC : KC + 1, cols]
            du = du + x_in * x_to + skip * dy
            dskip[i] = dskip[i] + jnp.sum(dy * u, axis=0, keepdims=True)
            dus.append(du)
        linked = jnp.concatenate(linked, axis=1)
        fed = jnp.concatenate(fed, axis=1)
        cross_low = cross_grad.astype(bf16)
        dc_map = nn(linked, state_low) + nn(cross_low, bmap)
        db_map = nn(fed, ds_low) + tn(cross_low, cmap)
        y_sum = nn(jnp.concatenate(link_prod, axis=1), pick, highest)
        v = nn(jnp.concatenate(end_prod, axis=1), pick, highest)
        col_sums = rows_acc[...].T
        keep_sum = nn(nt(jnp.ones((8, N), f32), ds * state, highest), pick, highest)[0:1, :]
        d_end = keep * keep_sum + jnp.sum(v * dt, axis=0, keepdims=True)
        dcum = row_sums - col_sums * dt + y_sum - v * dt
        dcum = dcum + jnp.where(iota((CHUNK, LANES), 0) == CHUNK - 1, d_end, 0.0)
        dld = nn(triangle(False), dcum, highest)
        ddt = col_sums + v - dld * par_ref[1:2, :]
        dstep = ddt * jax.nn.sigmoid(raw)
        dstep_ref[rows, :] = dstep.astype(bf16)
        dbias = dbias + jnp.sum(dstep, axis=0, keepdims=True)
        drate = drate + jnp.sum(dld * ld, axis=0, keepdims=True)
        dstate[...] = per_state_row(keep, heads) * ds + tn(linked, cmap)
        grads = dus + [db_map, dc_map]
        for i in range(tiles):
            cols = slice(i * LANES, (i + 1) * LANES)
            dpre = grads[i] * sigs[i] * (1.0 + pre[i] * (1.0 - sigs[i]))
            dcs[HALO + r0 : HALO + r0 + CHUNK, cols] = dpre
            for j in range(KC):
                at = r0 + HALO - (KC - 1) + j
                term = jnp.where(off >= KC - 1 - j, ext[at : at + CHUNK, cols] * dpre, 0.0)
                dkern[j][i] = dkern[j][i] + jnp.sum(term, axis=0, keepdims=True)
    for i in range(tiles):
        cols = slice(i * LANES, (i + 1) * LANES)
        for j in range(KC):
            dkern_ref[j : j + 1, cols] = dkern[j][i]
        dkern_ref[KC : KC + 1, cols] = dskip[i] if i < pairs else jnp.zeros((1, LANES), f32)
        dkern_ref[KC + 1 :, cols] = jnp.zeros((8 - KC - 1, LANES), f32)
    dpar_ref[...] = jnp.zeros_like(dpar_ref)
    dpar_ref[0:1, :] = dbias
    dpar_ref[1:2, :] = drate

    dsl_pad[:HALO, :] = jnp.full((HALO, LANES), 1 << 20, jnp.int32)
    dsl_pad[HALO : HALO + tokens, :] = dsl_ref[...]
    dsl_pad[HALO + tokens :, :] = jnp.full((HALO, LANES), 1 << 20, jnp.int32)
    for start, count in [(-HALO, HALO)] + [(c * CHUNK, CHUNK) for c in range(chunks)]:
        keeps = []
        for q in range(KC):
            at = start + q
            place = at + iota((count, LANES), 0)
            reach = place - dsl_pad[HALO + at : HALO + at + count, :]
            keeps.append(jnp.where(reach >= q, 1.0, 0.0))
        for i in range(tiles):
            cols = slice(i * LANES, (i + 1) * LANES)
            acc = None
            for q in range(KC):
                at = HALO + start + q
                term = dcs[at : at + count, cols] * keeps[q] * kern_ref[KC - 1 - q : KC - q, cols]
                acc = term if acc is None else acc + term
            if start < 0:
                dhalo_ref[:, cols] = acc
            else:
                dim_ref[start : start + count, cols] = acc.astype(bf16)


def project_back_kernel(received, me_ref, *refs):
    gots = refs[:received]
    (dz_ref, dim_ref, dhalo_ref, dq_ref, dkv_ref, dstep_ref, cos_ref, sin_ref, w_ref,
     dcat_ref, own_ref, *parts) = refs[received:]
    tokens, di = dz_ref.shape
    size = tokens // 4
    at = 2 * di
    tail = slice(tokens - HALO, tokens)
    dcat_ref[:, :di] = dz_ref[...]
    dcat_ref[:, di:at] = dim_ref[:, :di]
    dcat_ref[tail, di:at] = (dim_ref[tail, :di].astype(f32) + dhalo_ref[:, :di]).astype(bf16)
    cos, sin = cos_ref[...], sin_ref[...]
    dq = dq_ref[...]
    dcat_ref[:, at : at + LANES] = (dq * cos - swap_halves(dq) * sin).astype(bf16)
    dcat_ref[:, at + LANES : at + 2 * LANES] = dstep_ref[...]
    maps = slice(at + 2 * LANES, at + 4 * LANES)
    dcat_ref[:, maps] = dim_ref[:, di:]
    dcat_ref[tail, maps] = (dim_ref[tail, di:].astype(f32) + dhalo_ref[:, di:]).astype(bf16)
    dkv = dkv_ref[...]
    for got in gots:
        dkv = dkv + got[...].astype(f32)
    turned = dkv * cos - swap_halves(dkv) * sin
    dcat_ref[:, at + 4 * LANES :] = jnp.where(low_lanes(dkv.shape), turned, dkv).astype(bf16)
    for k in (1, 2, 3, 0):
        part = nt(dcat_ref[block_rows(me_ref, k, size), :], w_ref[...])
        if k:
            parts[k - 1][...] = part.astype(bf16)
        else:
            own_ref[...] = part


def trade(array, k):
    places = range(lax.axis_size("tensor"))
    return lax.ppermute(array, "tensor", [(i, i ^ k) for i in places])


def trades(arrays):
    return [trade(array, k + 1) for k, array in enumerate(arrays)]


def from_shard(array, distance):
    places = range(lax.axis_size("seq"))
    route = [(i - distance, i) for i in places if i - distance in places]
    return lax.ppermute(array, "seq", route)


def from_shards(array, sign):
    return [from_shard(array, sign * d) for d in range(1, lax.axis_size("seq"))]


def other_core(array):
    return lax.ppermute(array, "pipe", [(0, 1), (1, 0)])


def forward(x, x_own, wt, geo):
    w_cat, w_out, w_gu, w_down, gain_one, gain_two, kern, par = wt
    me, dsl, cos, sin, di = geo
    heads = di // P_SIZE
    tokens = dsl.shape[0]
    size, width = x_own.shape
    ff = w_down.shape[0]
    seqs = lax.axis_size("seq")
    wide = di + 2 * N
    low_parts = [sds((size, width), bf16)] * 3
    h, z, im, step, q, kv = call(
        partial(project_kernel, len(x), di),
        [
            sds((tokens, width), bf16),
            sds((tokens, di), f32),
            sds((tokens, wide), bf16),
            sds((tokens, LANES), f32),
            sds((tokens, LANES), bf16),
            sds((tokens, LANES), bf16),
        ],
        [me, *x, gain_one, w_cat, cos, sin],
        name="project",
    )
    halo = from_shard(im[tokens - HALO :], 1)
    kvs = [kv] + from_shards(kv, 1)
    mix0, cmap, lfac, packet = call(
        partial(ssm_forward_kernel, heads),
        [
            sds((tokens, di), f32),
            sds((tokens, N), bf16),
            sds((tokens, LANES), f32),
            sds((di + HALO, N), bf16),
        ],
        [me, im, halo, step, dsl, kern, par],
        [pltpu.VMEM((tokens + HALO, wide), f32), pltpu.VMEM((di, N), f32)],
        name="ssm_forward",
    )
    packets = from_shards(packet, 1)
    attn, lse = call(
        partial(attention_kernel, seqs),
        [sds((tokens, LANES), f32), sds((tokens, LANES), f32)],
        [me, q, dsl, *kvs],
        [pltpu.VMEM((seqs, tokens, LANES), bf16)] * 2,
        name="attention",
    )
    mixed, ga, state_in, own, *parts = call(
        partial(mix_kernel, heads, len(packets)),
        [
            sds((tokens, di), f32),
            sds((tokens, di + LANES), bf16),
            sds((di, N), f32),
            sds((size, width), f32),
            *low_parts,
        ],
        [me, *packets, mix0, cmap, lfac, z, attn, w_out],
        name="mix",
    )
    resid, h_own = call(
        norm_two_kernel,
        [sds((size, width), f32), sds((size, width), bf16)],
        [me, x_own, own, *trades(parts), gain_two],
        name="norm_two",
    )
    h_two, gate, up, hidden, own, *parts = call(
        mlp_kernel,
        [
            sds((tokens, width), bf16),
            sds((tokens, ff), bf16),
            sds((tokens, ff), bf16),
            sds((tokens, ff), bf16),
            sds((size, width), f32),
            *low_parts,
        ],
        [me, h_own, *trades([h_own] * 3), w_gu, w_down],
        name="mlp",
    )
    (out_own,) = call(
        out_kernel, [sds((size, width), bf16)], [me, resid, own, *trades(parts)], name="layer_out"
    )
    out = [out_own] + trades([out_own] * 3)
    saved = (
        x_own, h, z, im, step, q, halo, kvs, cmap, lfac, packet, attn, lse, mixed, ga, state_in,
        resid, h_two, gate, up, hidden,
    )
    return out, saved


def backward(g, g_own, saved, wt, geo):
    (
        x_own, h, z, im, step, q, halo, kvs, cmap, lfac, packet, attn, lse, mixed, ga, state_in,
        resid, h_two, gate, up, hidden,
    ) = saved
    w_cat, w_out, w_gu, w_down, gain_one, gain_two, kern, par = wt
    me, dsl, cos, sin, di = geo
    heads = di // P_SIZE
    tokens = dsl.shape[0]
    size, width = x_own.shape
    ff = w_down.shape[0]
    seqs = lax.axis_size("seq")
    wide = di + 2 * N
    low_parts = [sds((size, width), bf16)] * 3
    dgu, g_cat, own, *parts = call(
        partial(mlp_back_kernel, len(g)),
        [
            sds((tokens, 2 * ff), bf16),
            sds((tokens, width), bf16),
            sds((size, width), f32),
            *low_parts,
        ],
        [me, *g, gate, up, w_gu, w_down],
        name="mlp_back",
    )
    got = trades(parts)
    grad_down = tn(hidden, g_cat).astype(bf16)
    grad_gu = tn(h_two, dgu).astype(bf16)
    d_resid, d_own, grad_gain_two = call(
        norm_back_kernel,
        [sds((size, width), f32), sds((size, width), bf16), sds((8, width), f32)],
        [me, g_own, own, *got, resid, gain_two],
        name="norm_two_back",
    )
    d_branch, d_mixed, dz, d_attn, packet_back = call(
        partial(mixer_back_kernel, heads),
        [
            sds((tokens, width), bf16),
            sds((tokens, di), f32),
            sds((tokens, di), bf16),
            sds((tokens, LANES), bf16),
            sds((di + HALO, N), bf16),
        ],
        [me, d_own, *trades([d_own] * 3), w_out, z, mixed, cmap, lfac, packet],
        name="mixer_back",
    )
    packets = from_shards(packet_back, -1)
    grad_out = tn(ga, d_branch).astype(bf16)
    dq, *dkvs = call(
        partial(attention_back_kernel, seqs),
        [sds((tokens, LANES), f32), sds((tokens, LANES), f32)]
        + [sds((tokens, LANES), bf16)] * (seqs - 1),
        [me, q, dsl, attn, lse, d_attn, *kvs],
        [pltpu.VMEM((seqs, tokens, LANES), bf16)] * 2
        + [pltpu.VMEM((seqs, tokens, LANES), f32)] * 2,
        name="attention_back",
    )
    got_kv = [from_shard(dkvs[d], -d) for d in range(1, seqs)]
    d_im, d_halo, d_step, grad_kern, grad_par = call(
        partial(ssm_back_kernel, heads, len(packets)),
        [
            sds((tokens, wide), bf16),
            sds((HALO, wide), f32),
            sds((tokens, LANES), bf16),
            sds((8, wide), f32),
            sds((8, LANES), f32),
        ],
        [me, *packets, im, halo, step, dsl, kern, par, d_mixed, state_in],
        [
            pltpu.VMEM((tokens + HALO, wide), f32),
            pltpu.VMEM((tokens + 2 * HALO, wide), f32),
            pltpu.VMEM((tokens + 2 * HALO, LANES), jnp.int32),
            pltpu.VMEM((tokens // CHUNK, di, N), f32),
            pltpu.VMEM((di, N), f32),
            pltpu.VMEM((LANES, LANES), f32),
        ],
        name="ssm_back",
    )
    back_halo = from_shard(d_halo, -1)
    d_cat, own, *parts = call(
        partial(project_back_kernel, len(got_kv)),
        [
            sds((tokens, w_cat.shape[1]), bf16),
            sds((size, width), f32),
            *low_parts,
        ],
        [me, *got_kv, dz, d_im, back_halo, dq, dkvs[0], d_step, cos, sin, w_cat],
        name="project_back",
    )
    got = trades(parts)
    grad_cat = tn(h, d_cat).astype(bf16)
    dx_own, grad_gain_one = call(
        norm_back_kernel,
        [sds((size, width), bf16), sds((8, width), f32)],
        [me, d_resid, own, *got, x_own, gain_one],
        name="norm_one_back",
    )
    dx = [dx_own] + trades([dx_own] * 3)
    grads = (grad_cat, grad_out, grad_gu, grad_down)
    small = (grad_gain_one[0], grad_gain_two[0], grad_kern, grad_par)
    return dx, grads, small


def in_order(pieces, me):
    size = pieces[0].shape[0]
    whole = jnp.zeros((size * len(pieces), pieces[0].shape[1]), pieces[0].dtype)
    for k, piece in enumerate(pieces):
        whole = lax.dynamic_update_slice_in_dim(whole, piece, (me ^ k) * size, 0)
    return whole


def body(
    inputs,
    cotangent,
    doc_lengths,
    norm_one,
    w_gate_z,
    w_inner_x,
    w_bc,
    w_step,
    conv_inner,
    conv_bc,
    step_bias,
    decay_log,
    skip_gain,
    w_mix_out,
    w_query,
    keyval_weight,
    w_attn_out,
    norm_two,
    w_gate_up,
    w_down,
):
    core = lax.axis_index("pipe")
    place = lax.axis_index("tensor")
    me = place.astype(jnp.int32).reshape(1)
    tokens, width = inputs.shape[1:]
    di = w_gate_z.shape[2]
    heads = di // P_SIZE
    size = tokens // lax.axis_size("tensor")

    keyval_head = place * (w_query.shape[2] // HEAD_WIDTH) // (QUERY_HEADS // KEY_HEADS)
    key_at = keyval_head * HEAD_WIDTH
    value_at = KEY_HEADS * HEAD_WIDTH + key_at
    own_cat = jnp.concatenate(
        [
            w_gate_z[0],
            w_inner_x[0],
            w_query[0],
            jnp.pad(w_step[0], ((0, 0), (0, LANES - heads))),
            w_bc[0],
            lax.dynamic_slice_in_dim(keyval_weight[0], key_at, HEAD_WIDTH, 1),
            lax.dynamic_slice_in_dim(keyval_weight[0], value_at, HEAD_WIDTH, 1),
        ],
        axis=1,
    )
    own_out = jnp.concatenate([w_mix_out[0], w_attn_out[0]], axis=0)
    wide = di + 2 * N
    own_kern = jnp.concatenate(
        [
            jnp.concatenate([conv_inner[0], conv_bc[0]], axis=1),
            jnp.pad(jnp.repeat(skip_gain, P_SIZE, axis=1), ((0, KC - 1), (0, 2 * N))),
        ],
        axis=0,
    )
    own_par = jnp.pad(
        jnp.concatenate([step_bias, jnp.exp(decay_log)], axis=0), ((0, 6), (0, LANES - heads))
    )
    own_small = jnp.concatenate(
        [
            jnp.pad(jnp.concatenate([norm_one, norm_two], axis=0), ((0, 6), (0, 0))),
            jnp.pad(
                jnp.concatenate([own_kern, own_par], axis=1),
                ((0, 0), (0, width - wide - LANES)),
            ),
        ],
        axis=0,
    )
    mine = (own_cat, own_out, w_gate_up[0], w_down[0], own_small)
    theirs = [other_core(w) for w in mine]

    def weights(layer):
        cat, out, gu, down, small = [
            jnp.where(core == layer, a, b) for a, b in zip(mine, theirs)
        ]
        return (
            cat, out, gu, down, small[0:1], small[1:2],
            small[8:, :wide], small[8:, wide : wide + LANES],
        )

    layers = [weights(0), weights(1)]

    x = lax.dynamic_index_in_dim(inputs, core, 0, keepdims=False)
    top = lax.dynamic_index_in_dim(cotangent, core, 0, keepdims=False)
    lengths = lax.dynamic_index_in_dim(doc_lengths, core, 0, keepdims=False)
    first = lax.axis_index("seq") * tokens
    spots = first + jnp.arange(tokens, dtype=jnp.int32)
    before = jnp.cumsum(lengths)[None, :] <= spots[:, None]
    starts = jnp.sum(jnp.where(before, lengths[None, :], 0), axis=1)
    dsl = jnp.broadcast_to((starts - first)[:, None], (tokens, LANES)).astype(jnp.int32)
    half = HEAD_WIDTH // 2
    frequency = rope_base ** (-2.0 * jnp.arange(half, dtype=f32) / HEAD_WIDTH)
    angles = (spots - starts).astype(f32)[:, None] * frequency[None, :]
    cos, sin = jnp.cos(angles), jnp.sin(angles)
    cos = jnp.concatenate([cos] * 4, axis=1)
    sin = jnp.concatenate([-sin, sin] * 2, axis=1)
    geo = (me, dsl, cos, sin, di)

    def share(whole):
        return lax.dynamic_slice_in_dim(whole, place * size, size, 0)

    out_0, saved_0 = forward([x], share(x), layers[0], geo)
    out_1, saved_1 = forward(out_0, out_0[0], layers[1], geo)
    dx_1, grads_1, small_1 = backward([top], share(top), saved_1, layers[1], geo)

    def half_sums(grads):
        halves = []
        for g in grads:
            rows = g.shape[0] // 2
            keep = lax.dynamic_slice_in_dim(g, core * rows, rows, 0)
            send = lax.dynamic_slice_in_dim(g, (1 - core) * rows, rows, 0)
            halves.append((keep.astype(f32) + other_core(send).astype(f32)).astype(bf16))
        cat = halves[0]
        split = 2 * di + 2 * LANES
        kv = cat[:, split + 2 * N :]
        placed = jnp.zeros((kv.shape[0], 2 * KEY_HEADS * HEAD_WIDTH), bf16)
        placed = lax.dynamic_update_slice_in_dim(placed, kv[:, :HEAD_WIDTH], key_at, 1)
        placed = lax.dynamic_update_slice_in_dim(placed, kv[:, HEAD_WIDTH:], value_at, 1)
        shared = jnp.concatenate([cat[:, split : split + 2 * N], placed], axis=1)
        shared = lax.psum(shared, ("seq", "tensor"))
        return (shared,) + lax.psum((cat[:, :split],) + tuple(halves[1:]), "seq")

    sums_1 = half_sums(grads_1)
    dx_0, grads_0, small_0 = backward(dx_1, dx_1[0], saved_0, layers[0], geo)
    sums_0 = half_sums(grads_0)

    whole = []
    for a, b in zip(sums_0, sums_1):
        rows = a.shape[0]
        keep = jnp.where(core == 0, a, b)
        got = other_core(jnp.where(core == 0, b, a))
        first_half = jnp.where(core == 0, keep, got)
        second_half = jnp.where(core == 0, got, keep)
        whole.append(jnp.concatenate([first_half, second_half], axis=0).astype(f32))
    shared, cat, out, gu, down = whole

    def flat_small(small):
        gain_one, gain_two, kern, par = small
        every = jnp.concatenate([gain_one, gain_two, kern[:KC, di:].reshape(-1)])
        skip = jnp.sum(kern[KC, :di].reshape(heads, P_SIZE), axis=1)
        sharded = jnp.concatenate([kern[:KC, :di].reshape(-1), par[0, :heads], par[1, :heads], skip])
        return every, sharded

    smalls = [flat_small(small_0), flat_small(small_1)]
    every = lax.psum(jnp.stack([s[0] for s in smalls]), ("pipe", "seq", "tensor"))
    sharded = lax.psum(jnp.stack([s[1] for s in smalls]), ("pipe", "seq"))
    every = lax.dynamic_index_in_dim(every, core, 0, keepdims=False)
    sharded = lax.dynamic_index_in_dim(sharded, core, 0, keepdims=False)
    at = KC * di

    def both_micros(first_layer, second_layer):
        a, b = in_order(first_layer, place), in_order(second_layer, place)
        keep = jnp.where(core == 0, a, b)
        got = other_core(jnp.where(core == 0, b, a))
        return jnp.stack([jnp.where(core == 0, keep, got), jnp.where(core == 0, got, keep)])

    layer_out = both_micros(out_0, out_1)
    input_grad = both_micros(dx_0, dx_1)
    ff = w_down.shape[1]
    results = (
        layer_out,
        input_grad,
        every[:width],
        cat[:, :di],
        cat[:, di : 2 * di],
        shared[:, : 2 * N],
        cat[:, 2 * di + LANES : 2 * di + LANES + heads],
        sharded[:at].reshape(KC, di),
        every[2 * width :].reshape(KC, 2 * N),
        sharded[at : at + heads],
        sharded[at + heads : at + 2 * heads],
        sharded[at + 2 * heads :],
        out[:di],
        cat[:, 2 * di : 2 * di + LANES],
        shared[:, 2 * N :],
        out[di:],
        every[width : 2 * width],
        jnp.stack([gu[:, :ff], gu[:, ff:]]),
        down,
    )
    return tuple(r[None] for r in results)


def solution(mesh):
    token_spec = P(None, "seq", None)
    columns = P("pipe", None, "tensor")
    rows = P("pipe", "tensor", None)
    layer = P("pipe", None, None)
    vector = P("pipe", None)
    heads = P("pipe", "tensor")
    outs = P("pipe", None, "seq", None)
    gate_up = P("pipe", None, None, "tensor")
    return jax.shard_map(
        body,
        mesh=mesh,
        in_specs=(
            token_spec, token_spec, P(), vector, columns, columns, layer, columns, columns, layer,
            heads, heads, heads, rows, columns, layer, rows, vector, gate_up, rows,
        ),
        out_specs=(
            outs, outs, vector, columns, columns, layer, columns, columns, layer,
            heads, heads, heads, rows, columns, layer, rows, vector, gate_up, rows,
        ),
        check_vma=False,
    )
```

```python
from functools import partial

import jax
import jax.numpy as jnp
from jax import lax
from jax.experimental import pallas as pl
from jax.experimental.pallas import tpu as pltpu
from jax.sharding import PartitionSpec as P

P_SIZE = 64
N = 128
KC = 4
KEY_HEADS = 2
QUERY_HEADS = 8
HEAD_WIDTH = 64
CHUNK = 128
LANES = 128
HALO = 16

f32 = jnp.float32
bf16 = jnp.bfloat16
highest = lax.Precision.HIGHEST
eps_norm = 1e-05
rope_base = 100000000000.0
masked_score = -1e30
score_scale = HEAD_WIDTH ** (-0.5)


def nn(a, b, precision=None):
    return lax.dot_general(
        a, b, (((1,), (0,)), ((), ())), precision=precision, preferred_element_type=f32
    )


def nt(a, b, precision=None):
    return lax.dot_general(
        a, b, (((1,), (1,)), ((), ())), precision=precision, preferred_element_type=f32
    )


def tn(a, b, precision=None):
    return lax.dot_general(
        a, b, (((0,), (0,)), ((), ())), precision=precision, preferred_element_type=f32
    )


def iota(shape, axis):
    return lax.broadcasted_iota(jnp.int32, shape, axis)


def sds(shape, kind):
    return jax.ShapeDtypeStruct(shape, kind)


MICROSECONDS = {
    "project": 3.0,
    "ssm_forward": 3.8,
    "attention": 5.5,
    "mix": 1.6,
    "norm_two": 1.0,
    "mlp": 2.3,
    "layer_out": 1.0,
    "last_down": 1.0,
    "mlp_back": 0.46,
    "norm_two_back": 0.12,
    "mixer_back": 0.21,
    "attention_back": 0.82,
    "ssm_back": 1.38,
    "project_back": 0.39,
    "norm_one_back": 0.12,
    "products": 0.20,
    "last_products": 0.22,
    "share_sum": 0.09,
}


class Far:
    def __init__(self, value):
        self.value = value


def fars(*values):
    return [Far(value) for value in values]


def in_hbm(array):
    return pltpu.with_memory_space_constraint(array, pltpu.HBM)


def call(kernel, outs, args, scratch=(), name=None, after=()):
    count, wait = len(args), len(after)
    far_in = [i for i, a in enumerate(args) if isinstance(a, Far)]
    far_out = [i for i, o in enumerate(outs) if isinstance(o, Far)]
    args = [in_hbm(a.value) if isinstance(a, Far) else a for a in args]
    after = [in_hbm(a) for a in after]
    outs = [pltpu.HBM(o.value.shape, o.value.dtype) if isinstance(o, Far) else o for o in outs]

    def run(*refs):
        ins = list(refs[:count])
        results = list(refs[count + wait : count + wait + len(outs)])
        rest = list(refs[count + wait + len(outs) :])
        own = rest[: len(scratch)]
        near = rest[len(scratch) : len(scratch) + len(far_in) + len(far_out)]
        copies = []
        for k, i in enumerate(far_in):
            copies.append(pltpu.make_async_copy(ins[i], near[k], rest[-1].at[k]))
            ins[i] = near[k]
        for copy in copies:
            copy.start()
        for copy in copies:
            copy.wait()
        copies = []
        for k, i in enumerate(far_out):
            k = k + len(far_in)
            copies.append(pltpu.make_async_copy(near[k], results[i], rest[-1].at[k]))
            results[i] = near[k]
        kernel(*ins, *results, *own)
        for copy in copies:
            copy.start()
        for copy in copies:
            copy.wait()

    def spec(far):
        return pl.BlockSpec(memory_space=pltpu.HBM if far else pltpu.VMEM)

    specs = [pl.BlockSpec(memory_space=pltpu.SMEM)]
    specs += [spec(i in far_in) for i in range(1, count)]
    specs += [spec(True) for _ in after]
    scratch = list(scratch)
    extra = [pltpu.VMEM(args[i].shape, args[i].dtype) for i in far_in]
    extra += [pltpu.VMEM(outs[i].shape, outs[i].dtype) for i in far_out]
    if extra:
        extra.append(pltpu.SemaphoreType.DMA((len(extra),)))
    return pl.pallas_call(
        run,
        out_shape=outs,
        in_specs=specs,
        out_specs=[spec(i in far_out) for i in range(len(outs))],
        scratch_shapes=scratch + extra,
        compiler_params=pltpu.CompilerParams(
            vmem_limit_bytes=(14 + 2 * lax.axis_size("seq")) * 1024 * 1024
        ),
        cost_estimate=pl.CostEstimate(
            flops=int(MICROSECONDS[name] * 1.1e9), bytes_accessed=0, transcendentals=0
        ),
        name=name,
    )(*args, *after)


def block_rows(me_ref, k, size):
    return pl.ds(pl.multiple_of((me_ref[0] ^ k) * size, size), size)


def rms_scale(x):
    return lax.rsqrt(jnp.mean(x * x, axis=-1, keepdims=True) + eps_norm)


def swap_halves(x):
    lane = iota(x.shape, 1) % HEAD_WIDTH
    ahead = pltpu.roll(x, LANES - HEAD_WIDTH // 2, 1)
    behind = pltpu.roll(x, HEAD_WIDTH // 2, 1)
    return jnp.where(lane < HEAD_WIDTH // 2, ahead, behind)


def low_lanes(shape):
    return iota(shape, 1) < HEAD_WIDTH


def project_kernel(pieces, di, me_ref, *refs):
    xs = refs[:pieces]
    (gain_ref, w_ref, cos_ref, sin_ref,
     h_ref, z_ref, im_ref, step_ref, q_ref, kv_ref, *held) = refs[pieces:]
    tokens = h_ref.shape[0]
    size = tokens // 4
    source = xs[0]
    if pieces > 1:
        (source,) = held
        for k in range(4):
            source[block_rows(me_ref, k, size), :] = xs[k][...]

    def block(k, nothing):
        rows = pl.ds(pl.multiple_of(k * size, size), size)
        x = source[rows, :].astype(f32)
        h = (x * rms_scale(x) * gain_ref[...]).astype(bf16)
        h_ref[rows, :] = h
        p = nn(h, w_ref[...])
        z_ref[rows, :] = p[:, :di]
        cos, sin = cos_ref[rows, :], sin_ref[rows, :]
        q = p[:, di : di + LANES]
        q_ref[rows, :] = (q * cos + swap_halves(q) * sin).astype(bf16)
        im_ref[rows, :di] = p[:, di + LANES : 2 * di + LANES].astype(bf16)
        at = 2 * di
        step_ref[rows, :] = p[:, at + LANES : at + 2 * LANES]
        im_ref[rows, di:] = p[:, at + 2 * LANES : at + 4 * LANES].astype(bf16)
        kv = p[:, at + 4 * LANES :]
        turned = kv * cos + swap_halves(kv) * sin
        kv_ref[rows, :] = jnp.where(low_lanes(kv.shape), turned, kv).astype(bf16)
        return nothing

    lax.fori_loop(0, 4, block, 0)


def fill_ext(ext, halo_ref, im_ref):
    ext[:HALO, :] = halo_ref[...].astype(f32)
    ext[HALO:, :] = im_ref[...].astype(f32)


def triangle(lower):
    r, c = iota((CHUNK, CHUNK), 0), iota((CHUNK, CHUNK), 1)
    return jnp.where((c <= r) if lower else (c >= r), 1.0, 0.0).astype(f32)


def expand(cols, i):
    shape = (cols.shape[0], LANES)
    return jnp.where(
        low_lanes(shape),
        jnp.broadcast_to(cols[:, 2 * i : 2 * i + 1], shape),
        jnp.broadcast_to(cols[:, 2 * i + 1 : 2 * i + 2], shape),
    )


def expand_all(cols, tiles):
    return jnp.concatenate([expand(cols, i) for i in range(tiles)], axis=1)


def per_state_row(row, heads):
    return jnp.concatenate(
        [jnp.broadcast_to(row[:, h : h + 1], (P_SIZE, N)) for h in range(heads)], axis=0
    )


def chunk_steps(c, step_ref, dsl_ref, par_ref):
    r0 = c * CHUNK
    rows = slice(r0, r0 + CHUNK)
    raw = step_ref[rows, :] + par_ref[0:1, :]
    dt = jnp.maximum(raw, 0.0) + jnp.log1p(jnp.exp(-jnp.abs(raw)))
    ld = -dt * par_ref[1:2, :]
    cum = nn(triangle(True), ld, highest)
    dsl = dsl_ref[rows, :]
    place = r0 + iota((CHUNK, LANES), 0)
    end = cum[CHUNK - 1 : CHUNK, :]
    dsl_end = dsl[CHUNK - 1 : CHUNK, :]
    to_end = jnp.where(place >= dsl_end, jnp.exp(end - cum), 0.0)
    link = jnp.where(dsl < r0, jnp.exp(cum), 0.0)
    keep = jnp.where(dsl_end < r0, jnp.exp(end), 0.0)
    allowed = (iota((CHUNK, CHUNK), 1) <= iota((CHUNK, CHUNK), 0)) & (
        r0 + iota((CHUNK, CHUNK), 1) >= dsl
    )
    return raw, dt, ld, cum, dsl, place - dsl, end, to_end, link, keep, allowed


def chunk_conv(c, off, ext, kern_ref, tiles):
    r0 = c * CHUNK
    keeps = [jnp.where(off >= KC - 1 - j, 1.0, 0.0) for j in range(KC)]
    outs = []
    for i in range(tiles):
        cols = slice(i * LANES, (i + 1) * LANES)
        acc = None
        for j in range(KC):
            at = r0 + HALO - (KC - 1) + j
            term = ext[at : at + CHUNK, cols] * keeps[j] * kern_ref[j : j + 1, cols]
            acc = term if acc is None else acc + term
        outs.append(acc)
    return outs


def decays(cum, cum_t, allowed, h):
    gap = cum[:, h : h + 1] - cum_t[h : h + 1, :]
    return jnp.exp(jnp.where(allowed, gap, masked_score))


def both(a0, a1, axis):
    return jnp.concatenate([a0, a1], axis=axis)


def split_pair(x):
    low = low_lanes(x.shape)
    return both(jnp.where(low, x, 0.0), jnp.where(low, 0.0, x), 0)


def ssm_forward_kernel(
    heads, me_ref, im_ref, halo_ref, step_ref, dsl_ref, kern_ref, par_ref,
    mix_ref, cmap_ref, lfac_ref, packet_ref, ext, state,
):
    tokens = im_ref.shape[0]
    pairs = heads // 2
    fill_ext(ext, halo_ref, im_ref)
    state[...] = jnp.zeros_like(state)
    base = jnp.zeros((1, LANES), f32)
    for c in range(tokens // CHUNK):
        rows = slice(c * CHUNK, (c + 1) * CHUNK)
        raw, dt, ld, cum, dsl, off, end, to_end, link, keep, allowed = chunk_steps(
            c, step_ref, dsl_ref, par_ref
        )
        acts = [a * jax.nn.sigmoid(a) for a in chunk_conv(c, off, ext, kern_ref, pairs + 2)]
        bmap, cmap = acts[pairs].astype(bf16), acts[pairs + 1].astype(bf16)
        cum_t, dt_t = cum.T, dt.T
        cross = nt(cmap, bmap)
        carried = nt(cmap, state[...].astype(bf16)) if c else None
        ins = to_end * dt
        fed = []
        for i in range(pairs):
            u = acts[i]
            weights = [
                (decays(cum, cum_t, allowed, h) * cross * dt_t[h : h + 1, :]).astype(bf16)
                for h in (2 * i, 2 * i + 1)
            ]
            cols = slice(i * LANES, (i + 1) * LANES)
            y = nn(both(*weights, 1), split_pair(u).astype(bf16))
            if c:
                y = y + carried[:, cols] * expand(link, i)
            mix_ref[rows, cols] = y + kern_ref[KC : KC + 1, cols] * u
            fed.append((u * expand(ins, i)).astype(bf16))
        fresh = tn(jnp.concatenate(fed, axis=1), bmap)
        state[...] = per_state_row(keep, heads) * state[...] + fresh
        cmap_ref[rows, :] = cmap
        lfac = jnp.where(dsl < 0, jnp.exp(base + cum), 0.0)
        lfac_ref[rows, :] = lfac
        base = base + end
    packet_ref[: heads * P_SIZE, :] = state[...].astype(bf16)
    packet_ref[heads * P_SIZE :, :] = jnp.broadcast_to(
        lfac[CHUNK - 1 : CHUNK, :], (HALO, LANES)
    ).astype(bf16)


def arriving(packets, heads):
    total = None
    for ref in packets[::-1]:
        own = ref[: heads * P_SIZE, :].astype(f32)
        if total is not None:
            row = ref[heads * P_SIZE : heads * P_SIZE + 1, :].astype(f32)
            own = own + per_state_row(row, heads) * total
        total = own
    return total


def mix_kernel(heads, packets, me_ref, *refs):
    ins = refs[:packets]
    (mix_ref, cmap_ref, lfac_ref, z_ref, attn_ref, w_ref,
     mixed_ref, ga_ref, state_ref, own_ref, *part_refs) = refs[packets:]
    tokens = mix_ref.shape[0]
    size = tokens // 4
    pairs = heads // 2
    di = heads * P_SIZE
    if packets:
        state = arriving(ins, heads)
    else:
        state = jnp.zeros(state_ref.shape, f32)
    state_ref[...] = state
    state = state.astype(bf16)
    for k in (1, 2, 3, 0):
        rows = block_rows(me_ref, k, size)
        carried = nt(cmap_ref[rows, :], state)
        mixed = mix_ref[rows, :] + carried * expand_all(lfac_ref[rows, :], pairs)
        mixed_ref[rows, :] = mixed
        z = z_ref[rows, :]
        ga_ref[rows, :di] = (mixed * z * jax.nn.sigmoid(z)).astype(bf16)
        ga_ref[rows, di:] = attn_ref[rows, :].astype(bf16)
        part = nn(ga_ref[rows, :], w_ref[...])
        if k:
            part_refs[k - 1][...] = part.astype(bf16)
        else:
            own_ref[...] = part


def spread_keyval(ref):
    kv = ref[...].astype(f32)
    other = pltpu.roll(kv, HEAD_WIDTH, 1)
    low = low_lanes(kv.shape)
    return (
        jnp.where(low, kv, other).astype(bf16),
        jnp.where(low, other, kv).astype(bf16),
    )


def pair_mask(r0, d, tokens, dsl):
    shape = (CHUNK, tokens)
    key = iota(shape, 1) - d * tokens
    ok = key >= jnp.broadcast_to(dsl[:, 0:1], shape)
    if d == 0:
        ok = ok & (key <= r0 + iota(shape, 0))
    return both(ok, ok, 0)


def attention_kernel(blocks, me_ref, q_ref, dsl_ref, *refs):
    kvs = refs[:blocks]
    attn_ref, lse_ref, keys, values = refs[blocks:]
    tokens = q_ref.shape[0]
    for d in range(blocks):
        keys[d], values[d] = spread_keyval(kvs[d])
    for c in range(tokens // CHUNK):
        r0 = c * CHUNK
        rows = slice(r0, r0 + CHUNK)
        q = split_pair(q_ref[rows, :].astype(f32)).astype(bf16)
        dsl = dsl_ref[rows, :]
        top = total = acc = None
        for d in range(blocks):
            ok = pair_mask(r0, d, tokens, dsl)
            scores = jnp.where(ok, nt(q, keys[d]) * score_scale, masked_score)
            block_top = jnp.max(scores, axis=1, keepdims=True)
            if d == 0:
                top = block_top
                weights = jnp.exp(scores - top)
                total = jnp.sum(weights, axis=1, keepdims=True)
                acc = nn(weights.astype(bf16), values[d])
            else:
                new_top = jnp.maximum(top, block_top)
                factor = jnp.exp(top - new_top)
                weights = jnp.exp(scores - new_top)
                total = total * factor + jnp.sum(weights, axis=1, keepdims=True)
                acc = acc * factor + nn(weights.astype(bf16), values[d])
                top = new_top
        out = acc / total
        low = low_lanes((CHUNK, LANES))
        attn_ref[rows, :] = jnp.where(low, out[:CHUNK], out[CHUNK:])
        lse = jnp.broadcast_to(top + jnp.log(total), (2 * CHUNK, LANES))
        lse_ref[rows, :] = jnp.where(low, lse[:CHUNK], lse[CHUNK:])


def attention_back_kernel(
    blocks, me_ref, q_ref, dsl_ref, attn_ref, lse_ref, dattn_ref, dz_ref, cos_ref, sin_ref, *refs
):
    kvs = refs[:blocks]
    zq_ref = refs[blocks]
    outs = refs[blocks + 1 : 2 * blocks + 1]
    keys, values, dkeys, dvalues = refs[2 * blocks + 1 :]
    tokens = q_ref.shape[0]
    low = low_lanes((CHUNK, LANES))
    zq_ref[:, : dz_ref.shape[1]] = dz_ref[...]
    for d in range(blocks):
        keys[d], values[d] = spread_keyval(kvs[d])
    for c in range(tokens // CHUNK):
        r0 = c * CHUNK
        rows = slice(r0, r0 + CHUNK)
        q = split_pair(q_ref[rows, :].astype(f32)).astype(bf16)
        dout = dattn_ref[rows, :].astype(f32)
        prod = split_pair(dout * attn_ref[rows, :])
        delta = jnp.sum(prod, axis=1, keepdims=True)
        dout = split_pair(dout).astype(bf16)
        lse = lse_ref[rows, :]
        lse = both(lse[:, 0:1], lse[:, HEAD_WIDTH : HEAD_WIDTH + 1], 0)
        dsl = dsl_ref[rows, :]
        dq = None
        for d in range(blocks):
            ok = pair_mask(r0, d, tokens, dsl)
            scores = jnp.where(ok, nt(q, keys[d]) * score_scale - lse, masked_score)
            probs = jnp.exp(scores)
            dprobs = nt(dout, values[d])
            dscores = (probs * (dprobs - delta) * score_scale).astype(bf16)
            probs = probs.astype(bf16)
            part = nn(dscores, keys[d])
            dq = part if dq is None else dq + part
            dk, dv = tn(dscores, q), tn(probs, dout)
            if c:
                dkeys[d] += dk
                dvalues[d] += dv
            else:
                dkeys[d] = dk
                dvalues[d] = dv
        dq = jnp.where(low, dq[:CHUNK], dq[CHUNK:])
        dq = dq * cos_ref[rows, :] - swap_halves(dq) * sin_ref[rows, :]
        zq_ref[rows, dz_ref.shape[1] :] = dq.astype(bf16)
    wide = low_lanes((tokens, LANES))
    for d in range(blocks):
        dk, dv = dkeys[d], dvalues[d]
        dk = dk + pltpu.roll(dk, HEAD_WIDTH, 1)
        dv = dv + pltpu.roll(dv, HEAD_WIDTH, 1)
        outs[d][...] = jnp.where(wide, dk, dv).astype(outs[d].dtype)


def norm_two_kernel(me_ref, x_ref, own_ref, r1, r2, r3, gain_ref, resid_ref, h_ref):
    resid = x_ref[...].astype(f32) + own_ref[...]
    for r in (r1, r2, r3):
        resid = resid + r[...].astype(f32)
    resid_ref[...] = resid
    h_ref[...] = (resid * rms_scale(resid) * gain_ref[...]).astype(bf16)


def mlp_kernel(
    me_ref, h0, h1, h2, h3, gu_ref, down_ref, h_ref, gate_ref, up_ref, hid_ref, *rest
):
    size = h0.shape[0]
    for k, ref in ((1, h1), (2, h2), (3, h3), (0, h0)):
        rows = slice(k * size, (k + 1) * size)
        h = ref[...]
        h_ref[rows, :] = h
        gate = nn(h, gu_ref[0])
        up = nn(h, gu_ref[1])
        gate_ref[rows, :] = gate.astype(bf16)
        up_ref[rows, :] = up.astype(bf16)
        hidden = (gate * jax.nn.sigmoid(gate) * up).astype(bf16)
        hid_ref[rows, :] = hidden
        if rest:
            own_ref, *parts = rest
            part = nn(hidden, down_ref[...])
            if k:
                parts[k - 1][...] = part.astype(bf16)
            else:
                own_ref[...] = part


def down_kernel(me_ref, hid_ref, down_ref, own_ref, *parts):
    size = own_ref.shape[0]
    for k in (1, 2, 3, 0):
        part = nn(hid_ref[k * size : (k + 1) * size, :], down_ref[...])
        if k:
            parts[k - 1][...] = part.astype(bf16)
        else:
            own_ref[...] = part


def out_kernel(me_ref, resid_ref, own_ref, r1, r2, r3, out_ref):
    out = resid_ref[...] + own_ref[...]
    for r in (r1, r2, r3):
        out = out + r[...].astype(f32)
    out_ref[...] = out.astype(bf16)


def mlp_back_kernel(pieces, me_ref, *refs):
    gs = refs[:pieces]
    gate_ref, up_ref, gu_ref, down_ref, dgate_ref, dup_ref, g_ref, own_ref, *parts = refs[pieces:]
    size = gate_ref.shape[0] // 4
    for k in (1, 2, 3, 0):
        rows = slice(k * size, (k + 1) * size)
        g = gs[0][block_rows(me_ref, k, size), :] if pieces == 1 else gs[k][...]
        g_ref[rows, :] = g
        dhid = nt(g, down_ref[...])
        gate, up = gate_ref[rows, :].astype(f32), up_ref[rows, :].astype(f32)
        sig = jax.nn.sigmoid(gate)
        dgate = (dhid * up * sig * (1.0 + gate * (1.0 - sig))).astype(bf16)
        dup = (dhid * gate * sig).astype(bf16)
        dgate_ref[rows, :] = dgate
        dup_ref[rows, :] = dup
        part = nt(dgate, gu_ref[0]) + nt(dup, gu_ref[1])
        if k:
            parts[k - 1][...] = part.astype(bf16)
        else:
            own_ref[...] = part


def norm_back_kernel(me_ref, base_ref, own_ref, r1, r2, r3, x_ref, gain_ref, *outs):
    low_ref, gain_grad_ref = outs[-2:]
    dh = own_ref[...]
    for r in (r1, r2, r3):
        dh = dh + r[...].astype(f32)
    x = x_ref[...].astype(f32)
    r = rms_scale(x)
    n = x * r
    gain_grad_ref[...] = jnp.broadcast_to(
        jnp.sum(dh * n, axis=0, keepdims=True), gain_grad_ref.shape
    )
    dn = dh * gain_ref[...]
    dx = base_ref[...].astype(f32) + r * (dn - n * jnp.mean(dn * n, axis=-1, keepdims=True))
    if len(outs) == 3:
        outs[0][...] = dx
    low_ref[...] = dx.astype(bf16)


def mixer_back_kernel(
    heads, me_ref, d0, d1, d2, d3, w_ref, z_ref, mixed_ref, cmap_ref, lfac_ref, passing_ref,
    dbr_ref, dmixed_ref, dz_ref, dattn_ref, packet_ref,
):
    size = d0.shape[0]
    di = heads * P_SIZE
    pairs = heads // 2
    own = None
    for k, ref in ((0, d0), (1, d1), (2, d2), (3, d3)):
        rows = block_rows(me_ref, k, size)
        d = ref[...]
        dbr_ref[rows, :] = d
        p = nt(d, w_ref[...])
        dgated = p[:, :di]
        z = z_ref[rows, :]
        sig = jax.nn.sigmoid(z)
        act = z * sig
        dmixed = dgated * act
        dmixed_ref[rows, :] = dmixed
        dz_ref[rows, :] = (dgated * mixed_ref[rows, :] * sig * (1.0 + z * (1.0 - sig))).astype(bf16)
        dattn_ref[rows, :] = p[:, di:].astype(bf16)
        linked = (dmixed * expand_all(lfac_ref[rows, :], pairs)).astype(bf16)
        part = tn(linked, cmap_ref[rows, :])
        own = part if own is None else own + part
    packet_ref[:di, :] = own.astype(bf16)
    packet_ref[di:, :] = passing_ref[di:, :]


def ssm_back_kernel(heads, packets, me_ref, *refs):
    ins = refs[:packets]
    (im_ref, halo_ref, step_ref, dsl_ref, kern_ref, par_ref, dmixed_ref, state_in_ref,
     dim_ref, dhalo_ref, dstep_ref, dkern_ref, dpar_ref,
     ext, dcs, dsl_pad, states, dstate, rows_acc) = refs[packets:]
    tokens = im_ref.shape[0]
    chunks = tokens // CHUNK
    pairs = heads // 2
    di = heads * P_SIZE
    tiles = pairs + 2
    fill_ext(ext, halo_ref, im_ref)
    pick = jnp.where(
        iota((di, LANES), 0) // P_SIZE == iota((di, LANES), 1), 1.0, 0.0
    ).astype(f32)

    states[0] = state_in_ref[...]
    for c in range(chunks - 1):
        raw, dt, ld, cum, dsl, off, end, to_end, link, keep, allowed = chunk_steps(
            c, step_ref, dsl_ref, par_ref
        )
        acts = [a * jax.nn.sigmoid(a) for a in chunk_conv(c, off, ext, kern_ref, pairs + 1)]
        ins_ = to_end * dt
        fed = jnp.concatenate([(acts[i] * expand(ins_, i)).astype(bf16) for i in range(pairs)], 1)
        states[c + 1] = per_state_row(keep, heads) * states[c] + tn(fed, acts[pairs].astype(bf16))

    if packets:
        dstate[...] = arriving(ins, heads)
    else:
        dstate[...] = jnp.zeros_like(dstate)
    dcs[:HALO, :] = jnp.zeros((HALO, tiles * LANES), f32)
    dcs[HALO + tokens :, :] = jnp.zeros((HALO, tiles * LANES), f32)
    drate = jnp.zeros((1, LANES), f32)
    dbias = jnp.zeros((1, LANES), f32)
    dskip = [jnp.zeros((1, LANES), f32) for _ in range(pairs)]
    dkern = [[jnp.zeros((1, LANES), f32) for _ in range(tiles)] for _ in range(KC)]
    rows_acc[...] = jnp.zeros_like(rows_acc)
    lane = iota((CHUNK, LANES), 1)
    for c in range(chunks - 1, -1, -1):
        r0 = c * CHUNK
        rows = slice(r0, r0 + CHUNK)
        raw, dt, ld, cum, dsl, off, end, to_end, link, keep, allowed = chunk_steps(
            c, step_ref, dsl_ref, par_ref
        )
        pre = chunk_conv(c, off, ext, kern_ref, tiles)
        sigs = [jax.nn.sigmoid(a) for a in pre]
        acts = [a * s for a, s in zip(pre, sigs)]
        bmap, cmap = acts[pairs].astype(bf16), acts[pairs + 1].astype(bf16)
        cum_t, dt_t = cum.T, dt.T
        cross = nt(cmap, bmap)
        state = states[c]
        state_low = state.astype(bf16)
        ds = dstate[...]
        ds_low = ds.astype(bf16)
        carried = nt(cmap, state_low)
        towards = nt(bmap, ds_low)
        ins_ = to_end * dt
        cross_grad = jnp.zeros((CHUNK, CHUNK), f32)
        row_sums = jnp.zeros((CHUNK, LANES), f32)
        linked, fed, link_prod, end_prod, dus = [], [], [], [], []
        for i in range(pairs):
            cols = slice(i * LANES, (i + 1) * LANES)
            u = acts[i]
            dy = dmixed_ref[rows, cols]
            dy2 = split_pair(dy).astype(bf16)
            dw2 = nt(dy2, u.astype(bf16))
            weights = []
            for s in range(2):
                h = 2 * i + s
                dw = dw2[s * CHUNK : (s + 1) * CHUNK]
                low = decays(cum, cum_t, allowed, h)
                dt_row = dt_t[h : h + 1, :]
                scaled = low * dt_row
                cross_grad = cross_grad + dw * scaled
                g = low * cross
                weights.append((g * dt_row).astype(bf16))
                r = dw * g
                rows_acc[h : h + 1, :] = jnp.sum(r, axis=0, keepdims=True)
                row_sums = jnp.where(
                    lane == h, jnp.sum(r * dt_row, axis=1, keepdims=True), row_sums
                )
            du = tn(both(*weights, 0), dy2)
            x_link = dy * expand(link, i)
            linked.append(x_link.astype(bf16))
            link_prod.append(x_link * carried[:, cols])
            x_in = expand(ins_, i)
            fed.append((u * x_in).astype(bf16))
            x_to = towards[:, cols]
            end_prod.append(u * x_to * expand(to_end, i))
            skip = kern_ref[KC : KC + 1, cols]
            du = du + x_in * x_to + skip * dy
            dskip[i] = dskip[i] + jnp.sum(dy * u, axis=0, keepdims=True)
            dus.append(du)
        linked = jnp.concatenate(linked, axis=1)
        fed = jnp.concatenate(fed, axis=1)
        cross_low = cross_grad.astype(bf16)
        dc_map = nn(linked, state_low) + nn(cross_low, bmap)
        db_map = nn(fed, ds_low) + tn(cross_low, cmap)
        y_sum = nn(jnp.concatenate(link_prod, axis=1), pick, highest)
        v = nn(jnp.concatenate(end_prod, axis=1), pick, highest)
        col_sums = rows_acc[...].T
        keep_sum = nn(nt(jnp.ones((8, N), f32), ds * state, highest), pick, highest)[0:1, :]
        d_end = keep * keep_sum + jnp.sum(v * dt, axis=0, keepdims=True)
        dcum = row_sums - col_sums * dt + y_sum - v * dt
        dcum = dcum + jnp.where(iota((CHUNK, LANES), 0) == CHUNK - 1, d_end, 0.0)
        dld = nn(triangle(False), dcum, highest)
        ddt = col_sums + v - dld * par_ref[1:2, :]
        dstep = ddt * jax.nn.sigmoid(raw)
        dstep_ref[rows, :] = dstep.astype(bf16)
        dbias = dbias + jnp.sum(dstep, axis=0, keepdims=True)
        drate = drate + jnp.sum(dld * ld, axis=0, keepdims=True)
        dstate[...] = per_state_row(keep, heads) * ds + tn(linked, cmap)
        grads = dus + [db_map, dc_map]
        for i in range(tiles):
            cols = slice(i * LANES, (i + 1) * LANES)
            dpre = grads[i] * sigs[i] * (1.0 + pre[i] * (1.0 - sigs[i]))
            dcs[HALO + r0 : HALO + r0 + CHUNK, cols] = dpre
            for j in range(KC):
                at = r0 + HALO - (KC - 1) + j
                term = jnp.where(off >= KC - 1 - j, ext[at : at + CHUNK, cols] * dpre, 0.0)
                dkern[j][i] = dkern[j][i] + jnp.sum(term, axis=0, keepdims=True)
    for i in range(tiles):
        cols = slice(i * LANES, (i + 1) * LANES)
        for j in range(KC):
            dkern_ref[j : j + 1, cols] = dkern[j][i]
        dkern_ref[KC : KC + 1, cols] = dskip[i] if i < pairs else jnp.zeros((1, LANES), f32)
        dkern_ref[KC + 1 :, cols] = jnp.zeros((8 - KC - 1, LANES), f32)
    dpar_ref[...] = jnp.zeros_like(dpar_ref)
    dpar_ref[0:1, :] = dbias
    dpar_ref[1:2, :] = drate

    dsl_pad[:HALO, :] = jnp.full((HALO, LANES), 1 << 20, jnp.int32)
    dsl_pad[HALO : HALO + tokens, :] = dsl_ref[...]
    dsl_pad[HALO + tokens :, :] = jnp.full((HALO, LANES), 1 << 20, jnp.int32)
    for start, count in [(-HALO, HALO)] + [(c * CHUNK, CHUNK) for c in range(chunks)]:
        keeps = []
        for q in range(KC):
            at = start + q
            place = at + iota((count, LANES), 0)
            reach = place - dsl_pad[HALO + at : HALO + at + count, :]
            keeps.append(jnp.where(reach >= q, 1.0, 0.0))
        for i in range(tiles):
            cols = slice(i * LANES, (i + 1) * LANES)
            acc = None
            for q in range(KC):
                at = HALO + start + q
                term = dcs[at : at + count, cols] * keeps[q] * kern_ref[KC - 1 - q : KC - q, cols]
                acc = term if acc is None else acc + term
            if start < 0:
                dhalo_ref[:, cols] = acc
            else:
                dim_ref[start : start + count, cols] = acc.astype(bf16)


def project_back_kernel(received, me_ref, *refs):
    gots = refs[:received]
    (zq_ref, dim_ref, dhalo_ref, dkv_ref, dstep_ref, cos_ref, sin_ref, w_ref,
     dis_ref, dmk_ref, own_ref, *parts) = refs[received:]
    tokens = zq_ref.shape[0]
    di = zq_ref.shape[1] - LANES
    size = tokens // 4
    tail = slice(tokens - HALO, tokens)
    dis_ref[:, :di] = dim_ref[:, :di]
    dis_ref[tail, :di] = (dim_ref[tail, :di].astype(f32) + dhalo_ref[:, :di]).astype(bf16)
    dis_ref[:, di:] = dstep_ref[...]
    dmk_ref[:, : 2 * N] = dim_ref[:, di:]
    dmk_ref[tail, : 2 * N] = (dim_ref[tail, di:].astype(f32) + dhalo_ref[:, di:]).astype(bf16)
    dkv = dkv_ref[...]
    for got in gots:
        dkv = dkv + got[...].astype(f32)
    turned = dkv * cos_ref[...] - swap_halves(dkv) * sin_ref[...]
    dmk_ref[:, 2 * N :] = jnp.where(low_lanes(dkv.shape), turned, dkv).astype(bf16)
    first, second = di + LANES, 2 * di + 2 * LANES
    for k in (1, 2, 3, 0):
        rows = block_rows(me_ref, k, size)
        part = nt(zq_ref[rows, :], w_ref[:, :first])
        part = part + nt(dis_ref[rows, :], w_ref[:, first:second])
        part = part + nt(dmk_ref[rows, :], w_ref[:, second:])
        if k:
            parts[k - 1][...] = part.astype(bf16)
        else:
            own_ref[...] = part


def products_kernel(count, me_ref, *refs):
    for i in range(count):
        refs[2 * count + i][...] = tn(refs[2 * i][...], refs[2 * i + 1][...]).astype(bf16)


def last_products_kernel(
    me_ref, h_ref, dis_ref, dmk_ref, kern_ref, par_ref, one_ref, two_ref, is_ref, own_ref, *parts
):
    di = dis_ref.shape[1] - LANES
    rows = h_ref.shape[1]
    size = rows // 4
    width = one_ref.shape[1]
    wide = dmk_ref.shape[1]
    is_ref[:rows, :] = tn(h_ref[...], dis_ref[...]).astype(bf16)
    small = jnp.concatenate([kern_ref[:, :di], par_ref[...]], axis=1)
    is_ref[rows:, :] = both(small, jnp.zeros_like(small), 0).astype(bf16)
    pieces = []
    for ref in (one_ref, two_ref):
        for at in range(0, width, wide):
            piece = ref[0:1, at : at + wide]
            if piece.shape[1] < wide:
                piece = both(piece, jnp.zeros((1, wide - piece.shape[1]), f32), 1)
            pieces.append(piece)
    taps = both(kern_ref[:KC, di:], jnp.zeros((KC, wide - 2 * N), f32), 1)
    pieces.append(taps)
    pieces.append(jnp.zeros((HALO - KC - len(pieces) + 1, wide), f32))
    extra = jnp.concatenate(pieces, axis=0)
    for k in range(4):
        at = pl.ds(pl.multiple_of((me_ref[0] ^ k) * size, size), size)
        block = tn(h_ref[:, at], dmk_ref[...])
        out = parts[k - 1] if k else own_ref
        out[:size, :] = block.astype(out.dtype)
        out[size:, :] = extra.astype(out.dtype)


def share_sum_kernel(me_ref, own_ref, r1, r2, r3, out_ref):
    size = own_ref.shape[0] - HALO
    wide = own_ref.shape[1]
    near = own_ref[...] + r1[...].astype(f32)
    far = r2[...].astype(f32) + r3[...].astype(f32)
    total = near + far
    out_ref[:, : 2 * N] = total[:, : 2 * N].astype(bf16)
    first = me_ref[0] // 2 == 0
    mine, other = near[:size, 2 * N :], far[:size, 2 * N :]
    a, b = jnp.where(first, mine, other), jnp.where(first, other, mine)
    low = low_lanes(a.shape)
    out_ref[:size, 2 * N : 2 * N + LANES] = jnp.where(low, a, pltpu.roll(b, HEAD_WIDTH, 1)).astype(bf16)
    out_ref[:size, 2 * N + LANES :] = jnp.where(low, pltpu.roll(a, HEAD_WIDTH, 1), b).astype(bf16)
    out_ref[size:, 2 * N : wide] = total[size:, 2 * N :].astype(bf16)
    out_ref[size:, wide:] = jnp.zeros((HALO, out_ref.shape[1] - wide), bf16)


def trade(array, k):
    places = range(lax.axis_size("tensor"))
    return lax.ppermute(array, "tensor", [(i, i ^ k) for i in places])


def trades(arrays):
    return [trade(array, k + 1) for k, array in enumerate(arrays)]


def from_shard(array, distance):
    places = range(lax.axis_size("seq"))
    route = [(i - distance, i) for i in places if i - distance in places]
    return lax.ppermute(array, "seq", route)


def from_shards(array, sign):
    return [from_shard(array, sign * d) for d in range(1, lax.axis_size("seq"))]


def other_core(array):
    return lax.ppermute(array, "pipe", [(0, 1), (1, 0)])


def finish(me, resid, own, *parts):
    (out_own,) = call(
        out_kernel, [sds(resid.shape, bf16)], [me, resid, own, *trades(parts)], name="layer_out"
    )
    return [out_own] + trades([out_own] * 3)


def last_out(saved, wt, me, after):
    resid, hidden = saved[-5], saved[-1]
    parts = call(
        down_kernel,
        [sds(resid.shape, f32)] + [sds(resid.shape, bf16)] * 3,
        [me, *fars(hidden, wt[3])],
        name="last_down",
        after=after,
    )
    return finish(me, resid, *parts)


def forward(x, x_own, wt, geo, last):
    w_cat, w_out, w_gu, w_down, gain_one, gain_two, kern, par = wt
    me, dsl, cos, sin, di = geo
    heads = di // P_SIZE
    tokens = dsl.shape[0]
    size, width = x_own.shape
    ff = w_down.shape[0]
    seqs = lax.axis_size("seq")
    wide = di + 2 * N
    low_parts = [sds((size, width), bf16)] * 3
    h, z, im, step, q, kv = call(
        partial(project_kernel, len(x), di),
        [
            Far(sds((tokens, width), bf16)),
            sds((tokens, di), f32),
            sds((tokens, wide), bf16),
            sds((tokens, LANES), f32),
            sds((tokens, LANES), bf16),
            sds((tokens, LANES), bf16),
        ],
        [me, *x, gain_one, Far(w_cat), cos, sin],
        [pltpu.VMEM((tokens, width), bf16)] if len(x) > 1 else [],
        name="project",
    )
    halo = from_shard(im[tokens - HALO :], 1)
    kvs = [kv] + from_shards(kv, 1)
    mix0, cmap, lfac, packet = call(
        partial(ssm_forward_kernel, heads),
        [
            sds((tokens, di), f32),
            sds((tokens, N), bf16),
            sds((tokens, LANES), f32),
            sds((di + HALO, N), bf16),
        ],
        [me, im, halo, step, dsl, kern, par],
        [pltpu.VMEM((tokens + HALO, wide), f32), pltpu.VMEM((di, N), f32)],
        name="ssm_forward",
    )
    packets = from_shards(packet, 1)
    attn, lse = call(
        partial(attention_kernel, seqs),
        [sds((tokens, LANES), f32), Far(sds((tokens, LANES), f32))],
        [me, q, dsl, *kvs],
        [pltpu.VMEM((seqs, tokens, LANES), bf16)] * 2,
        name="attention",
    )
    mixed, ga, state_in, own, *parts = call(
        partial(mix_kernel, heads, len(packets)),
        [
            Far(sds((tokens, di), f32)),
            Far(sds((tokens, di + LANES), bf16)),
            Far(sds((di, N), f32)),
            sds((size, width), f32),
            *low_parts,
        ],
        [me, *packets, mix0, cmap, lfac, z, attn, Far(w_out)],
        name="mix",
    )
    resid, h_own = call(
        norm_two_kernel,
        [sds((size, width), f32), sds((size, width), bf16)],
        [me, x_own, own, *trades(parts), gain_two],
        name="norm_two",
    )
    h_two, gate, up, hidden, *parts = call(
        mlp_kernel,
        [
            *[
                Far(o) if not last else o
                for o in [sds((tokens, width), bf16)] + [sds((tokens, ff), bf16)] * 3
            ],
            *([] if last else [sds((size, width), f32), *low_parts]),
        ],
        [me, h_own, *trades([h_own] * 3), *fars(w_gu, w_down)],
        name="mlp",
    )
    out = None if last else finish(me, resid, *parts)
    saved = (
        x_own, h, z, im, step, q, halo, kvs, cmap, lfac, packet, attn, lse, mixed, ga, state_in,
        resid, h_two, gate, up, hidden,
    )
    return out, saved


def products(*pairs, me, after):
    return call(
        partial(products_kernel, len(pairs)),
        [Far(sds((a.shape[1], b.shape[1]), bf16)) for a, b in pairs],
        [me, *[x for a, b in pairs for x in (Far(a), b)]],
        name="products",
        after=after,
    )


def last_products(me, h, d_is, d_mk, *small, after=()):
    size = h.shape[1] // 4 + HALO
    wide = d_mk.shape[1]
    own_is, own, *parts = call(
        last_products_kernel,
        [Far(sds((h.shape[1] + HALO, d_is.shape[1]), bf16)), sds((size, wide), f32)]
        + [sds((size, wide), bf16)] * 3,
        [me, Far(h), d_is, d_mk, *small],
        name="last_products",
        after=after,
    )
    (shared,) = call(
        share_sum_kernel,
        [sds((size, 2 * N + 2 * LANES), bf16)],
        [me, own, *trades(parts)],
        name="share_sum",
    )
    return own_is, shared


def both_sum(arrays, *axes):
    return list(lax.psum(tuple(arrays), axes))


def backward(g, g_own, saved, wt, geo, first=(), second=()):
    (
        x_own, h, z, im, step, q, halo, kvs, cmap, lfac, packet, attn, lse, mixed, ga, state_in,
        resid, h_two, gate, up, hidden,
    ) = saved
    w_cat, w_out, w_gu, w_down, gain_one, gain_two, kern, par = wt
    me, dsl, cos, sin, di = geo
    heads = di // P_SIZE
    tokens = dsl.shape[0]
    size, width = x_own.shape
    ff = w_down.shape[0]
    seqs = lax.axis_size("seq")
    wide = di + 2 * N
    low_parts = [sds((size, width), bf16)] * 3
    dgate, dup, g_cat, own, *parts = call(
        partial(mlp_back_kernel, len(g)),
        [
            sds((tokens, ff), bf16),
            sds((tokens, ff), bf16),
            sds((tokens, width), bf16),
            sds((size, width), f32),
            *low_parts,
        ],
        [me, *g, *(fars(gate, up) if len(g) > 1 else (gate, up)), *fars(w_gu, w_down)],
        name="mlp_back",
        after=first,
    )
    got = trades(parts)
    d_resid, d_own, grad_gain_two = call(
        norm_back_kernel,
        [sds((size, width), f32), sds((size, width), bf16), sds((8, width), f32)],
        [me, g_own, own, *got, Far(resid), gain_two],
        name="norm_two_back",
        after=second,
    )
    early = products((h_two, dgate), (h_two, dup), (hidden, g_cat), me=me, after=[d_own])
    d_branch, d_mixed, dz, d_attn, packet_back = call(
        partial(mixer_back_kernel, heads),
        [
            sds((tokens, width), bf16),
            sds((tokens, di), f32),
            sds((tokens, di), bf16),
            sds((tokens, LANES), bf16),
            sds((di + HALO, N), bf16),
        ],
        [me, d_own, *trades([d_own] * 3), *fars(w_out, z, mixed, cmap, lfac, packet)],
        name="mixer_back",
        after=early,
    )
    packets = from_shards(packet_back, -1)
    zq, *dkvs = call(
        partial(attention_back_kernel, seqs),
        [sds((tokens, di + LANES), bf16), sds((tokens, LANES), f32)]
        + [sds((tokens, LANES), bf16)] * (seqs - 1),
        [me, *fars(q, dsl, attn, lse), d_attn, dz, *fars(cos, sin, *kvs)],
        [pltpu.VMEM((seqs, tokens, LANES), bf16)] * 2
        + [pltpu.VMEM((seqs, tokens, LANES), f32)] * 2,
        name="attention_back",
    )
    got_kv = [from_shard(dkvs[d], -d) for d in range(1, seqs)]
    d_im, d_halo, d_step, grad_kern, grad_par = call(
        partial(ssm_back_kernel, heads, len(packets)),
        [
            sds((tokens, wide), bf16),
            sds((HALO, wide), f32),
            sds((tokens, LANES), bf16),
            sds((8, wide), f32),
            sds((8, LANES), f32),
        ],
        [me, *packets, *fars(im, halo, step, dsl), kern, par, d_mixed, Far(state_in)],
        [
            pltpu.VMEM((tokens + HALO, wide), f32),
            pltpu.VMEM((tokens + 2 * HALO, wide), f32),
            pltpu.VMEM((tokens + 2 * HALO, LANES), jnp.int32),
            pltpu.VMEM((tokens // CHUNK, di, N), f32),
            pltpu.VMEM((di, N), f32),
            pltpu.VMEM((LANES, LANES), f32),
        ],
        name="ssm_back",
    )
    back_halo = from_shard(d_halo, -1)
    d_is, d_mk, own, *parts = call(
        partial(project_back_kernel, len(got_kv)),
        [
            sds((tokens, di + LANES), bf16),
            sds((tokens, 2 * N + LANES), bf16),
            sds((size, width), f32),
            *low_parts,
        ],
        [me, *got_kv, zq, d_im, back_halo, dkvs[0], d_step, *fars(cos, sin, w_cat)],
        name="project_back",
    )
    got = trades(parts)
    middle = products((ga, d_branch), (h, zq), me=me, after=[d_is])
    dx_own, grad_gain_one = call(
        norm_back_kernel,
        [sds((size, width), bf16), sds((8, width), f32)],
        [me, d_resid, own, *got, Far(x_own), gain_one],
        name="norm_one_back",
        after=middle,
    )
    dx = [dx_own] + trades([dx_own] * 3)
    last = h, d_is, d_mk, grad_kern, grad_par, grad_gain_one, grad_gain_two
    return dx, early, middle, last


def in_order(pieces, me):
    size = pieces[0].shape[0]
    whole = jnp.zeros((size * len(pieces), pieces[0].shape[1]), pieces[0].dtype)
    for k, piece in enumerate(pieces):
        whole = lax.dynamic_update_slice_in_dim(whole, piece, (me ^ k) * size, 0)
    return whole


def body(
    inputs,
    cotangent,
    doc_lengths,
    norm_one,
    w_gate_z,
    w_inner_x,
    w_bc,
    w_step,
    conv_inner,
    conv_bc,
    step_bias,
    decay_log,
    skip_gain,
    w_mix_out,
    w_query,
    keyval_weight,
    w_attn_out,
    norm_two,
    w_gate_up,
    w_down,
):
    core = lax.axis_index("pipe")
    place = lax.axis_index("tensor")
    me = place.astype(jnp.int32).reshape(1)
    tokens, width = inputs.shape[1:]
    di = w_gate_z.shape[2]
    heads = di // P_SIZE
    size = tokens // lax.axis_size("tensor")

    keyval_head = place * (w_query.shape[2] // HEAD_WIDTH) // (QUERY_HEADS // KEY_HEADS)
    key_at = keyval_head * HEAD_WIDTH
    value_at = KEY_HEADS * HEAD_WIDTH + key_at
    own_cat = jnp.concatenate(
        [
            w_gate_z[0],
            w_query[0],
            w_inner_x[0],
            jnp.pad(w_step[0], ((0, 0), (0, LANES - heads))),
            w_bc[0],
            lax.dynamic_slice_in_dim(keyval_weight[0], key_at, HEAD_WIDTH, 1),
            lax.dynamic_slice_in_dim(keyval_weight[0], value_at, HEAD_WIDTH, 1),
        ],
        axis=1,
    )
    own_out = jnp.concatenate([w_mix_out[0], w_attn_out[0]], axis=0)
    wide = di + 2 * N
    own_kern = jnp.concatenate(
        [
            jnp.concatenate([conv_inner[0], conv_bc[0]], axis=1),
            jnp.pad(jnp.repeat(skip_gain, P_SIZE, axis=1), ((0, KC - 1), (0, 2 * N))),
        ],
        axis=0,
    )
    own_par = jnp.pad(
        jnp.concatenate([step_bias, jnp.exp(decay_log)], axis=0), ((0, 6), (0, LANES - heads))
    )
    own_small = jnp.concatenate(
        [
            jnp.pad(jnp.concatenate([norm_one, norm_two], axis=0), ((0, 6), (0, 0))),
            jnp.pad(
                jnp.concatenate([own_kern, own_par], axis=1),
                ((0, 0), (0, width - wide - LANES)),
            ),
        ],
        axis=0,
    )
    mine = (own_cat, own_out, w_gate_up[0], w_down[0], own_small)
    theirs = [other_core(w) for w in mine]

    def weights(layer):
        cat, out, gu, down, small = [
            jnp.where(core == layer, a, b) for a, b in zip(mine, theirs)
        ]
        return (
            cat, out, gu, down, small[0:1], small[1:2],
            small[8:, :wide], small[8:, wide : wide + LANES],
        )

    layers = [weights(0), weights(1)]

    x = lax.dynamic_index_in_dim(inputs, core, 0, keepdims=False)
    top = lax.dynamic_index_in_dim(cotangent, core, 0, keepdims=False)
    lengths = lax.dynamic_index_in_dim(doc_lengths, core, 0, keepdims=False)
    first = lax.axis_index("seq") * tokens
    spots = first + jnp.arange(tokens, dtype=jnp.int32)
    before = jnp.cumsum(lengths)[None, :] <= spots[:, None]
    starts = jnp.sum(jnp.where(before, lengths[None, :], 0), axis=1)
    dsl = jnp.broadcast_to((starts - first)[:, None], (tokens, LANES)).astype(jnp.int32)
    half = HEAD_WIDTH // 2
    frequency = rope_base ** (-2.0 * jnp.arange(half, dtype=f32) / HEAD_WIDTH)
    angles = (spots - starts).astype(f32)[:, None] * frequency[None, :]
    cos, sin = jnp.cos(angles), jnp.sin(angles)
    cos = jnp.concatenate([cos] * 4, axis=1)
    sin = jnp.concatenate([-sin, sin] * 2, axis=1)
    geo = (me, dsl, cos, sin, di)

    def share(whole):
        return lax.dynamic_slice_in_dim(whole, place * size, size, 0)

    out_0, saved_0 = forward([x], share(x), layers[0], geo, False)
    _, saved_1 = forward(out_0, out_0[0], layers[1], geo, True)
    dx_1, early_1, middle_1, last_1 = backward([top], share(top), saved_1, layers[1], geo)
    early_1 = both_sum(early_1, "pipe", "seq")
    last_1 = last_products(me, *last_1, after=[dx_1[0]])
    dx_0, early_0, middle_0, last_0 = backward(
        dx_1, dx_1[0], saved_0, layers[0], geo, [last_1[0]], early_1
    )
    late_1 = both_sum([*middle_1, last_1[0]], "seq", "pipe")
    last_0 = last_products(me, *last_0, after=[dx_0[0], *late_1])
    *sums_0, shared_0, shared_1 = both_sum(
        [*early_0, *middle_0, *last_0, last_1[1]], "pipe", "seq"
    )
    sums_0 = [*sums_0, shared_0]
    sums_1 = [*early_1, *late_1, shared_1]
    out_1 = last_out(saved_1, layers[1], me, [dx_0[0]])

    gate, up, down, out, zq, last, shared = [
        jnp.where(core == 0, a, b) for a, b in zip(sums_0, sums_1)
    ]
    quarter = shared[: width // 4]
    every = shared[width // 4 :].astype(f32)
    shared = in_order([quarter] + trades([quarter] * 3), place).astype(f32)
    gate, up, down, out, zq = [a.astype(f32) for a in (gate, up, down, out, zq)]
    own_small = last[width:].astype(f32)
    last = last[:width].astype(f32)
    step_128 = 2 * N + LANES
    count = -(-width // step_128)
    gain_one = every[:count, :step_128].reshape(-1)[:width]
    gain_two = every[count : 2 * count, :step_128].reshape(-1)[:width]
    taps = every[2 * count : 2 * count + KC, : 2 * N]
    skip = jnp.sum(own_small[KC, :di].reshape(heads, P_SIZE), axis=1)

    def both_micros(first_layer, second_layer):
        a, b = in_order(first_layer, place), in_order(second_layer, place)
        keep = jnp.where(core == 0, a, b)
        got = other_core(jnp.where(core == 0, b, a))
        return jnp.stack([jnp.where(core == 0, keep, got), jnp.where(core == 0, got, keep)])

    layer_out = both_micros(out_0, out_1)
    input_grad = both_micros(dx_0, dx_1)
    results = (
        layer_out,
        input_grad,
        gain_one,
        zq[:, :di],
        last[:, :di],
        shared[:, : 2 * N],
        last[:, di : di + heads],
        own_small[:KC, :di],
        taps,
        own_small[0, di : di + heads],
        own_small[1, di : di + heads],
        skip,
        out[:di],
        zq[:, di:],
        shared[:, 2 * N :],
        out[di:],
        gain_two,
        jnp.stack([gate, up]),
        down,
    )
    return tuple(r[None] for r in results)


def solution(mesh):
    token_spec = P(None, "seq", None)
    columns = P("pipe", None, "tensor")
    rows = P("pipe", "tensor", None)
    layer = P("pipe", None, None)
    vector = P("pipe", None)
    heads = P("pipe", "tensor")
    outs = P("pipe", None, "seq", None)
    gate_up = P("pipe", None, None, "tensor")
    return jax.shard_map(
        body,
        mesh=mesh,
        in_specs=(
            token_spec, token_spec, P(), vector, columns, columns, layer, columns, columns, layer,
            heads, heads, heads, rows, columns, layer, rows, vector, gate_up, rows,
        ),
        out_specs=(
            outs, outs, vector, columns, columns, layer, columns, columns, layer,
            heads, heads, heads, rows, columns, layer, rows, vector, gate_up, rows,
        ),
        check_vma=False,
    )
```

```python
from functools import partial

import jax
import jax.numpy as jnp
from jax import lax
from jax.experimental import pallas as pl
from jax.experimental.pallas import tpu as pltpu
from jax.sharding import PartitionSpec as P

P_SIZE = 64
N = 128
KC = 4
KEY_HEADS = 2
QUERY_HEADS = 8
HEAD_WIDTH = 64
CHUNK = 128
LANES = 128
HALO = 16

f32 = jnp.float32
bf16 = jnp.bfloat16
highest = lax.Precision.HIGHEST
eps_norm = 1e-05
rope_base = 100000000000.0
masked_score = -1e30
score_scale = HEAD_WIDTH ** (-0.5)


def nn(a, b, precision=None):
    return lax.dot_general(
        a, b, (((1,), (0,)), ((), ())), precision=precision, preferred_element_type=f32
    )


def nt(a, b, precision=None):
    return lax.dot_general(
        a, b, (((1,), (1,)), ((), ())), precision=precision, preferred_element_type=f32
    )


def tn(a, b, precision=None):
    return lax.dot_general(
        a, b, (((0,), (0,)), ((), ())), precision=precision, preferred_element_type=f32
    )


def iota(shape, axis):
    return lax.broadcasted_iota(jnp.int32, shape, axis)


def sds(shape, kind):
    return jax.ShapeDtypeStruct(shape, kind)


MICROSECONDS = {
    "project": 3.0,
    "ssm_forward": 3.8,
    "attention": 5.5,
    "mix": 1.6,
    "norm_two": 1.0,
    "mlp": 2.3,
    "layer_out": 1.0,
    "last_down": 1.0,
    "mlp_back": 0.46,
    "norm_two_back": 0.12,
    "mixer_back": 0.21,
    "attention_back": 0.82,
    "ssm_back": 1.38,
    "project_back": 0.39,
    "norm_one_back": 0.12,
    "products": 0.20,
    "last_products": 0.22,
    "share_sum": 0.09,
}


class Far:
    def __init__(self, value, other=None, layer=None):
        self.value, self.other, self.layer = value, other, layer


def fars(*values):
    return [value if isinstance(value, Far) else Far(value) for value in values]


class Arriving:
    def __init__(self, ref, copy):
        self.ref, self.copy, self.shape = ref, copy, ref.shape

    def ready(self):
        if self.copy is not None:
            self.copy.wait()
            self.copy = None

    def __getitem__(self, index):
        self.ready()
        return self.ref[index]


def in_hbm(array):
    return pltpu.with_memory_space_constraint(array, pltpu.HBM)


def call(kernel, outs, args, scratch=(), name=None, after=()):
    count = len(args)
    far_in = {i: a for i, a in enumerate(args) if isinstance(a, Far)}
    far_out = [i for i, o in enumerate(outs) if isinstance(o, Far)]
    args = [in_hbm(a.value) if isinstance(a, Far) else a for a in args]
    others = {i: k for k, i in enumerate(i for i, a in far_in.items() if a.other is not None)}
    after = [in_hbm(far_in[i].other) for i in others] + [in_hbm(a) for a in after]
    wait = len(after)
    outs = [pltpu.HBM(o.value.shape, o.value.dtype) if isinstance(o, Far) else o for o in outs]

    def run(*refs):
        ins = list(refs[:count])
        results = list(refs[count + wait : count + wait + len(outs)])
        rest = list(refs[count + wait + len(outs) :])
        own = rest[: len(scratch)]
        near = rest[len(scratch) : len(scratch) + len(far_in) + len(far_out)]
        for k, (i, far) in enumerate(far_in.items()):
            copy = pltpu.make_async_copy(ins[i], near[k], rest[-1].at[k])
            if i in others:
                other = pltpu.make_async_copy(refs[count + others[i]], near[k], rest[-1].at[k])
                mine = ins[0][1] == far.layer
                pl.when(mine)(copy.start)
                pl.when(jnp.logical_not(mine))(other.start)
            else:
                copy.start()
            ins[i] = Arriving(near[k], copy)
        copies = []
        for k, i in enumerate(far_out):
            k = k + len(far_in)
            copies.append(pltpu.make_async_copy(near[k], results[i], rest[-1].at[k]))
            results[i] = near[k]
        kernel(*ins, *results, *own)
        for i in far_in:
            ins[i].ready()
        for copy in copies:
            copy.start()
        for copy in copies:
            copy.wait()

    def spec(far):
        return pl.BlockSpec(memory_space=pltpu.HBM if far else pltpu.VMEM)

    specs = [pl.BlockSpec(memory_space=pltpu.SMEM)]
    specs += [spec(i in far_in) for i in range(1, count)]
    specs += [spec(True) for _ in after]
    scratch = list(scratch)
    extra = [pltpu.VMEM(args[i].shape, args[i].dtype) for i in far_in]
    extra += [pltpu.VMEM(outs[i].shape, outs[i].dtype) for i in far_out]
    if extra:
        extra.append(pltpu.SemaphoreType.DMA((len(extra),)))
    return pl.pallas_call(
        run,
        out_shape=outs,
        in_specs=specs,
        out_specs=[spec(i in far_out) for i in range(len(outs))],
        scratch_shapes=scratch + extra,
        compiler_params=pltpu.CompilerParams(
            vmem_limit_bytes=(14 + 2 * lax.axis_size("seq")) * 1024 * 1024
        ),
        cost_estimate=pl.CostEstimate(
            flops=int(MICROSECONDS[name] * 1.1e9), bytes_accessed=0, transcendentals=0
        ),
        name=name,
    )(*args, *after)


def block_rows(me_ref, k, size):
    return pl.ds(pl.multiple_of((me_ref[0] ^ k) * size, size), size)


def rms_scale(x):
    return lax.rsqrt(jnp.mean(x * x, axis=-1, keepdims=True) + eps_norm)


def swap_halves(x):
    lane = iota(x.shape, 1) % HEAD_WIDTH
    ahead = pltpu.roll(x, LANES - HEAD_WIDTH // 2, 1)
    behind = pltpu.roll(x, HEAD_WIDTH // 2, 1)
    return jnp.where(lane < HEAD_WIDTH // 2, ahead, behind)


def low_lanes(shape):
    return iota(shape, 1) < HEAD_WIDTH


def project_kernel(pieces, di, me_ref, *refs):
    xs = refs[:pieces]
    (gain_ref, w_ref, cos_ref, sin_ref,
     h_ref, z_ref, im_ref, step_ref, q_ref, kv_ref, *held) = refs[pieces:]
    tokens = h_ref.shape[0]
    size = tokens // 4
    source = xs[0]
    if pieces > 1:
        (source,) = held
        for k in range(4):
            source[block_rows(me_ref, k, size), :] = xs[k][...]
    w_ref.ready()

    def block(k, nothing):
        rows = pl.ds(pl.multiple_of(k * size, size), size)
        x = source[rows, :].astype(f32)
        h = (x * rms_scale(x) * gain_ref[...]).astype(bf16)
        h_ref[rows, :] = h
        p = nn(h, w_ref[...])
        z_ref[rows, :] = p[:, :di]
        cos, sin = cos_ref[rows, :], sin_ref[rows, :]
        q = p[:, di : di + LANES]
        q_ref[rows, :] = (q * cos + swap_halves(q) * sin).astype(bf16)
        im_ref[rows, :di] = p[:, di + LANES : 2 * di + LANES].astype(bf16)
        at = 2 * di
        step_ref[rows, :] = p[:, at + LANES : at + 2 * LANES]
        im_ref[rows, di:] = p[:, at + 2 * LANES : at + 4 * LANES].astype(bf16)
        kv = p[:, at + 4 * LANES :]
        turned = kv * cos + swap_halves(kv) * sin
        kv_ref[rows, :] = jnp.where(low_lanes(kv.shape), turned, kv).astype(bf16)
        return nothing

    lax.fori_loop(0, 4, block, 0)


def fill_ext(ext, halo_ref, im_ref):
    ext[:HALO, :] = halo_ref[...].astype(f32)
    ext[HALO:, :] = im_ref[...].astype(f32)


def triangle(lower):
    r, c = iota((CHUNK, CHUNK), 0), iota((CHUNK, CHUNK), 1)
    return jnp.where((c <= r) if lower else (c >= r), 1.0, 0.0).astype(f32)


def expand(cols, i):
    shape = (cols.shape[0], LANES)
    return jnp.where(
        low_lanes(shape),
        jnp.broadcast_to(cols[:, 2 * i : 2 * i + 1], shape),
        jnp.broadcast_to(cols[:, 2 * i + 1 : 2 * i + 2], shape),
    )


def expand_all(cols, tiles):
    return jnp.concatenate([expand(cols, i) for i in range(tiles)], axis=1)


def per_state_row(row, heads):
    return jnp.concatenate(
        [jnp.broadcast_to(row[:, h : h + 1], (P_SIZE, N)) for h in range(heads)], axis=0
    )


def chunk_steps(c, step_ref, dsl_ref, par_ref):
    r0 = c * CHUNK
    rows = slice(r0, r0 + CHUNK)
    raw = step_ref[rows, :] + par_ref[0:1, :]
    dt = jnp.maximum(raw, 0.0) + jnp.log1p(jnp.exp(-jnp.abs(raw)))
    ld = -dt * par_ref[1:2, :]
    cum = nn(triangle(True), ld, highest)
    dsl = dsl_ref[rows, :]
    place = r0 + iota((CHUNK, LANES), 0)
    end = cum[CHUNK - 1 : CHUNK, :]
    dsl_end = dsl[CHUNK - 1 : CHUNK, :]
    to_end = jnp.where(place >= dsl_end, jnp.exp(end - cum), 0.0)
    link = jnp.where(dsl < r0, jnp.exp(cum), 0.0)
    keep = jnp.where(dsl_end < r0, jnp.exp(end), 0.0)
    allowed = (iota((CHUNK, CHUNK), 1) <= iota((CHUNK, CHUNK), 0)) & (
        r0 + iota((CHUNK, CHUNK), 1) >= dsl
    )
    return raw, dt, ld, cum, dsl, place - dsl, end, to_end, link, keep, allowed


def chunk_conv(c, off, ext, kern_ref, tiles):
    r0 = c * CHUNK
    keeps = [jnp.where(off >= KC - 1 - j, 1.0, 0.0) for j in range(KC)]
    outs = []
    for i in range(tiles):
        cols = slice(i * LANES, (i + 1) * LANES)
        acc = None
        for j in range(KC):
            at = r0 + HALO - (KC - 1) + j
            term = ext[at : at + CHUNK, cols] * keeps[j] * kern_ref[j : j + 1, cols]
            acc = term if acc is None else acc + term
        outs.append(acc)
    return outs


def decays(cum, cum_t, allowed, h):
    gap = cum[:, h : h + 1] - cum_t[h : h + 1, :]
    return jnp.exp(jnp.where(allowed, gap, masked_score))


def both(a0, a1, axis):
    return jnp.concatenate([a0, a1], axis=axis)


def split_pair(x):
    low = low_lanes(x.shape)
    return both(jnp.where(low, x, 0.0), jnp.where(low, 0.0, x), 0)


def ssm_forward_kernel(
    heads, me_ref, im_ref, halo_ref, step_ref, dsl_ref, kern_ref, par_ref,
    mix_ref, cmap_ref, lfac_ref, packet_ref, ext, state,
):
    tokens = im_ref.shape[0]
    pairs = heads // 2
    fill_ext(ext, halo_ref, im_ref)
    state[...] = jnp.zeros_like(state)
    base = jnp.zeros((1, LANES), f32)
    for c in range(tokens // CHUNK):
        rows = slice(c * CHUNK, (c + 1) * CHUNK)
        raw, dt, ld, cum, dsl, off, end, to_end, link, keep, allowed = chunk_steps(
            c, step_ref, dsl_ref, par_ref
        )
        acts = [a * jax.nn.sigmoid(a) for a in chunk_conv(c, off, ext, kern_ref, pairs + 2)]
        bmap, cmap = acts[pairs].astype(bf16), acts[pairs + 1].astype(bf16)
        cum_t, dt_t = cum.T, dt.T
        cross = nt(cmap, bmap)
        carried = nt(cmap, state[...].astype(bf16)) if c else None
        ins = to_end * dt
        fed = []
        for i in range(pairs):
            u = acts[i]
            weights = [
                (decays(cum, cum_t, allowed, h) * cross * dt_t[h : h + 1, :]).astype(bf16)
                for h in (2 * i, 2 * i + 1)
            ]
            cols = slice(i * LANES, (i + 1) * LANES)
            y = nn(both(*weights, 1), split_pair(u).astype(bf16))
            if c:
                y = y + carried[:, cols] * expand(link, i)
            mix_ref[rows, cols] = y + kern_ref[KC : KC + 1, cols] * u
            fed.append((u * expand(ins, i)).astype(bf16))
        fresh = tn(jnp.concatenate(fed, axis=1), bmap)
        state[...] = per_state_row(keep, heads) * state[...] + fresh
        cmap_ref[rows, :] = cmap
        lfac = jnp.where(dsl < 0, jnp.exp(base + cum), 0.0)
        lfac_ref[rows, :] = lfac
        base = base + end
    packet_ref[: heads * P_SIZE, :] = state[...].astype(bf16)
    packet_ref[heads * P_SIZE :, :] = jnp.broadcast_to(
        lfac[CHUNK - 1 : CHUNK, :], (HALO, LANES)
    ).astype(bf16)


def arriving(packets, heads):
    total = None
    for ref in packets[::-1]:
        own = ref[: heads * P_SIZE, :].astype(f32)
        if total is not None:
            row = ref[heads * P_SIZE : heads * P_SIZE + 1, :].astype(f32)
            own = own + per_state_row(row, heads) * total
        total = own
    return total


def mix_kernel(heads, packets, me_ref, *refs):
    ins = refs[:packets]
    (mix_ref, cmap_ref, lfac_ref, z_ref, attn_ref, w_ref,
     mixed_ref, ga_ref, state_ref, own_ref, *part_refs) = refs[packets:]
    tokens = mix_ref.shape[0]
    size = tokens // 4
    pairs = heads // 2
    di = heads * P_SIZE
    if packets:
        state = arriving(ins, heads)
    else:
        state = jnp.zeros(state_ref.shape, f32)
    state_ref[...] = state
    state = state.astype(bf16)
    for k in (1, 2, 3, 0):
        rows = block_rows(me_ref, k, size)
        carried = nt(cmap_ref[rows, :], state)
        mixed = mix_ref[rows, :] + carried * expand_all(lfac_ref[rows, :], pairs)
        mixed_ref[rows, :] = mixed
        z = z_ref[rows, :]
        ga_ref[rows, :di] = (mixed * z * jax.nn.sigmoid(z)).astype(bf16)
        ga_ref[rows, di:] = attn_ref[rows, :].astype(bf16)
        part = nn(ga_ref[rows, :], w_ref[...])
        if k:
            part_refs[k - 1][...] = part.astype(bf16)
        else:
            own_ref[...] = part


def spread_keyval(ref):
    kv = ref[...].astype(f32)
    other = pltpu.roll(kv, HEAD_WIDTH, 1)
    low = low_lanes(kv.shape)
    return (
        jnp.where(low, kv, other).astype(bf16),
        jnp.where(low, other, kv).astype(bf16),
    )


def pair_mask(r0, d, tokens, dsl):
    shape = (CHUNK, tokens)
    key = iota(shape, 1) - d * tokens
    ok = key >= jnp.broadcast_to(dsl[:, 0:1], shape)
    if d == 0:
        ok = ok & (key <= r0 + iota(shape, 0))
    return both(ok, ok, 0)


def attention_kernel(blocks, me_ref, q_ref, dsl_ref, *refs):
    kvs = refs[:blocks]
    attn_ref, lse_ref, keys, values = refs[blocks:]
    tokens = q_ref.shape[0]
    for d in range(blocks):
        keys[d], values[d] = spread_keyval(kvs[d])
    for c in range(tokens // CHUNK):
        r0 = c * CHUNK
        rows = slice(r0, r0 + CHUNK)
        q = split_pair(q_ref[rows, :].astype(f32)).astype(bf16)
        dsl = dsl_ref[rows, :]
        top = total = acc = None
        for d in range(blocks):
            ok = pair_mask(r0, d, tokens, dsl)
            scores = jnp.where(ok, nt(q, keys[d]) * score_scale, masked_score)
            block_top = jnp.max(scores, axis=1, keepdims=True)
            if d == 0:
                top = block_top
                weights = jnp.exp(scores - top)
                total = jnp.sum(weights, axis=1, keepdims=True)
                acc = nn(weights.astype(bf16), values[d])
            else:
                new_top = jnp.maximum(top, block_top)
                factor = jnp.exp(top - new_top)
                weights = jnp.exp(scores - new_top)
                total = total * factor + jnp.sum(weights, axis=1, keepdims=True)
                acc = acc * factor + nn(weights.astype(bf16), values[d])
                top = new_top
        out = acc / total
        low = low_lanes((CHUNK, LANES))
        attn_ref[rows, :] = jnp.where(low, out[:CHUNK], out[CHUNK:])
        lse = jnp.broadcast_to(top + jnp.log(total), (2 * CHUNK, LANES))
        lse_ref[rows, :] = jnp.where(low, lse[:CHUNK], lse[CHUNK:])


def attention_back_kernel(
    blocks, me_ref, q_ref, dsl_ref, attn_ref, lse_ref, dattn_ref, dz_ref, cos_ref, sin_ref, *refs
):
    kvs = refs[:blocks]
    zq_ref = refs[blocks]
    outs = refs[blocks + 1 : 2 * blocks + 1]
    keys, values, dkeys, dvalues = refs[2 * blocks + 1 :]
    tokens = q_ref.shape[0]
    low = low_lanes((CHUNK, LANES))
    zq_ref[:, : dz_ref.shape[1]] = dz_ref[...]
    for d in range(blocks):
        keys[d], values[d] = spread_keyval(kvs[d])
    for c in range(tokens // CHUNK):
        r0 = c * CHUNK
        rows = slice(r0, r0 + CHUNK)
        q = split_pair(q_ref[rows, :].astype(f32)).astype(bf16)
        dout = dattn_ref[rows, :].astype(f32)
        prod = split_pair(dout * attn_ref[rows, :])
        delta = jnp.sum(prod, axis=1, keepdims=True)
        dout = split_pair(dout).astype(bf16)
        lse = lse_ref[rows, :]
        lse = both(lse[:, 0:1], lse[:, HEAD_WIDTH : HEAD_WIDTH + 1], 0)
        dsl = dsl_ref[rows, :]
        dq = None
        for d in range(blocks):
            ok = pair_mask(r0, d, tokens, dsl)
            scores = jnp.where(ok, nt(q, keys[d]) * score_scale - lse, masked_score)
            probs = jnp.exp(scores)
            dprobs = nt(dout, values[d])
            dscores = (probs * (dprobs - delta) * score_scale).astype(bf16)
            probs = probs.astype(bf16)
            part = nn(dscores, keys[d])
            dq = part if dq is None else dq + part
            dk, dv = tn(dscores, q), tn(probs, dout)
            if c:
                dkeys[d] += dk
                dvalues[d] += dv
            else:
                dkeys[d] = dk
                dvalues[d] = dv
        dq = jnp.where(low, dq[:CHUNK], dq[CHUNK:])
        dq = dq * cos_ref[rows, :] - swap_halves(dq) * sin_ref[rows, :]
        zq_ref[rows, dz_ref.shape[1] :] = dq.astype(bf16)
    wide = low_lanes((tokens, LANES))
    for d in range(blocks):
        dk, dv = dkeys[d], dvalues[d]
        dk = dk + pltpu.roll(dk, HEAD_WIDTH, 1)
        dv = dv + pltpu.roll(dv, HEAD_WIDTH, 1)
        outs[d][...] = jnp.where(wide, dk, dv).astype(outs[d].dtype)


def norm_two_kernel(me_ref, x_ref, own_ref, r1, r2, r3, gain_ref, resid_ref, h_ref):
    resid = x_ref[...].astype(f32) + own_ref[...]
    for r in (r1, r2, r3):
        resid = resid + r[...].astype(f32)
    resid_ref[...] = resid
    h_ref[...] = (resid * rms_scale(resid) * gain_ref[...]).astype(bf16)


def mlp_kernel(
    me_ref, h0, h1, h2, h3, gu_ref, down_ref, h_ref, gate_ref, up_ref, hid_ref, *rest
):
    size = h0.shape[0]
    for k, ref in ((1, h1), (2, h2), (3, h3), (0, h0)):
        rows = slice(k * size, (k + 1) * size)
        h = ref[...]
        h_ref[rows, :] = h
        gate = nn(h, gu_ref[0])
        up = nn(h, gu_ref[1])
        gate_ref[rows, :] = gate.astype(bf16)
        up_ref[rows, :] = up.astype(bf16)
        hidden = (gate * jax.nn.sigmoid(gate) * up).astype(bf16)
        hid_ref[rows, :] = hidden
        if rest:
            own_ref, *parts = rest
            part = nn(hidden, down_ref[...])
            if k:
                parts[k - 1][...] = part.astype(bf16)
            else:
                own_ref[...] = part


def down_kernel(me_ref, hid_ref, down_ref, own_ref, *parts):
    size = own_ref.shape[0]
    for k in (1, 2, 3, 0):
        part = nn(hid_ref[k * size : (k + 1) * size, :], down_ref[...])
        if k:
            parts[k - 1][...] = part.astype(bf16)
        else:
            own_ref[...] = part


def out_kernel(me_ref, resid_ref, own_ref, r1, r2, r3, out_ref):
    out = resid_ref[...] + own_ref[...]
    for r in (r1, r2, r3):
        out = out + r[...].astype(f32)
    out_ref[...] = out.astype(bf16)


def mlp_back_kernel(pieces, me_ref, *refs):
    gs = refs[:pieces]
    gate_ref, up_ref, gu_ref, down_ref, dgate_ref, dup_ref, g_ref, own_ref, *parts = refs[pieces:]
    size = gate_ref.shape[0] // 4
    for k in (1, 2, 3, 0):
        rows = slice(k * size, (k + 1) * size)
        g = gs[0][block_rows(me_ref, k, size), :] if pieces == 1 else gs[k][...]
        g_ref[rows, :] = g
        dhid = nt(g, down_ref[...])
        gate, up = gate_ref[rows, :].astype(f32), up_ref[rows, :].astype(f32)
        sig = jax.nn.sigmoid(gate)
        dgate = (dhid * up * sig * (1.0 + gate * (1.0 - sig))).astype(bf16)
        dup = (dhid * gate * sig).astype(bf16)
        dgate_ref[rows, :] = dgate
        dup_ref[rows, :] = dup
        part = nt(dgate, gu_ref[0]) + nt(dup, gu_ref[1])
        if k:
            parts[k - 1][...] = part.astype(bf16)
        else:
            own_ref[...] = part


def norm_back_kernel(me_ref, base_ref, own_ref, r1, r2, r3, x_ref, gain_ref, *outs):
    low_ref, gain_grad_ref = outs[-2:]
    dh = own_ref[...]
    for r in (r1, r2, r3):
        dh = dh + r[...].astype(f32)
    x = x_ref[...].astype(f32)
    r = rms_scale(x)
    n = x * r
    gain_grad_ref[...] = jnp.broadcast_to(
        jnp.sum(dh * n, axis=0, keepdims=True), gain_grad_ref.shape
    )
    dn = dh * gain_ref[...]
    dx = base_ref[...].astype(f32) + r * (dn - n * jnp.mean(dn * n, axis=-1, keepdims=True))
    if len(outs) == 3:
        outs[0][...] = dx
    low_ref[...] = dx.astype(bf16)


def mixer_back_kernel(
    heads, me_ref, d0, d1, d2, d3, w_ref, z_ref, mixed_ref, cmap_ref, lfac_ref, passing_ref,
    dbr_ref, dmixed_ref, dz_ref, dattn_ref, packet_ref,
):
    size = d0.shape[0]
    di = heads * P_SIZE
    pairs = heads // 2
    own = None
    for k, ref in ((0, d0), (1, d1), (2, d2), (3, d3)):
        rows = block_rows(me_ref, k, size)
        d = ref[...]
        dbr_ref[rows, :] = d
        p = nt(d, w_ref[...])
        dgated = p[:, :di]
        z = z_ref[rows, :]
        sig = jax.nn.sigmoid(z)
        act = z * sig
        dmixed = dgated * act
        dmixed_ref[rows, :] = dmixed
        dz_ref[rows, :] = (dgated * mixed_ref[rows, :] * sig * (1.0 + z * (1.0 - sig))).astype(bf16)
        dattn_ref[rows, :] = p[:, di:].astype(bf16)
        linked = (dmixed * expand_all(lfac_ref[rows, :], pairs)).astype(bf16)
        part = tn(linked, cmap_ref[rows, :])
        own = part if own is None else own + part
    packet_ref[:di, :] = own.astype(bf16)
    packet_ref[di:, :] = passing_ref[di:, :]


def ssm_back_kernel(heads, packets, me_ref, *refs):
    ins = refs[:packets]
    (im_ref, halo_ref, step_ref, dsl_ref, kern_ref, par_ref, dmixed_ref, state_in_ref,
     dim_ref, dhalo_ref, dstep_ref, dkern_ref, dpar_ref,
     ext, dcs, dsl_pad, states, dstate, rows_acc) = refs[packets:]
    tokens = im_ref.shape[0]
    chunks = tokens // CHUNK
    pairs = heads // 2
    di = heads * P_SIZE
    tiles = pairs + 2
    fill_ext(ext, halo_ref, im_ref)
    pick = jnp.where(
        iota((di, LANES), 0) // P_SIZE == iota((di, LANES), 1), 1.0, 0.0
    ).astype(f32)

    states[0] = state_in_ref[...]
    for c in range(chunks - 1):
        raw, dt, ld, cum, dsl, off, end, to_end, link, keep, allowed = chunk_steps(
            c, step_ref, dsl_ref, par_ref
        )
        acts = [a * jax.nn.sigmoid(a) for a in chunk_conv(c, off, ext, kern_ref, pairs + 1)]
        ins_ = to_end * dt
        fed = jnp.concatenate([(acts[i] * expand(ins_, i)).astype(bf16) for i in range(pairs)], 1)
        states[c + 1] = per_state_row(keep, heads) * states[c] + tn(fed, acts[pairs].astype(bf16))

    if packets:
        dstate[...] = arriving(ins, heads)
    else:
        dstate[...] = jnp.zeros_like(dstate)
    dcs[:HALO, :] = jnp.zeros((HALO, tiles * LANES), f32)
    dcs[HALO + tokens :, :] = jnp.zeros((HALO, tiles * LANES), f32)
    drate = jnp.zeros((1, LANES), f32)
    dbias = jnp.zeros((1, LANES), f32)
    dskip = [jnp.zeros((1, LANES), f32) for _ in range(pairs)]
    dkern = [[jnp.zeros((1, LANES), f32) for _ in range(tiles)] for _ in range(KC)]
    rows_acc[...] = jnp.zeros_like(rows_acc)
    lane = iota((CHUNK, LANES), 1)
    for c in range(chunks - 1, -1, -1):
        r0 = c * CHUNK
        rows = slice(r0, r0 + CHUNK)
        raw, dt, ld, cum, dsl, off, end, to_end, link, keep, allowed = chunk_steps(
            c, step_ref, dsl_ref, par_ref
        )
        pre = chunk_conv(c, off, ext, kern_ref, tiles)
        sigs = [jax.nn.sigmoid(a) for a in pre]
        acts = [a * s for a, s in zip(pre, sigs)]
        bmap, cmap = acts[pairs].astype(bf16), acts[pairs + 1].astype(bf16)
        cum_t, dt_t = cum.T, dt.T
        cross = nt(cmap, bmap)
        state = states[c]
        state_low = state.astype(bf16)
        ds = dstate[...]
        ds_low = ds.astype(bf16)
        carried = nt(cmap, state_low)
        towards = nt(bmap, ds_low)
        ins_ = to_end * dt
        cross_grad = jnp.zeros((CHUNK, CHUNK), f32)
        row_sums = jnp.zeros((CHUNK, LANES), f32)
        linked, fed, link_prod, end_prod, dus = [], [], [], [], []
        for i in range(pairs):
            cols = slice(i * LANES, (i + 1) * LANES)
            u = acts[i]
            dy = dmixed_ref[rows, cols]
            dy2 = split_pair(dy).astype(bf16)
            dw2 = nt(dy2, u.astype(bf16))
            weights = []
            for s in range(2):
                h = 2 * i + s
                dw = dw2[s * CHUNK : (s + 1) * CHUNK]
                low = decays(cum, cum_t, allowed, h)
                dt_row = dt_t[h : h + 1, :]
                scaled = low * dt_row
                cross_grad = cross_grad + dw * scaled
                g = low * cross
                weights.append((g * dt_row).astype(bf16))
                r = dw * g
                rows_acc[h : h + 1, :] = jnp.sum(r, axis=0, keepdims=True)
                row_sums = jnp.where(
                    lane == h, jnp.sum(r * dt_row, axis=1, keepdims=True), row_sums
                )
            du = tn(both(*weights, 0), dy2)
            x_link = dy * expand(link, i)
            linked.append(x_link.astype(bf16))
            link_prod.append(x_link * carried[:, cols])
            x_in = expand(ins_, i)
            fed.append((u * x_in).astype(bf16))
            x_to = towards[:, cols]
            end_prod.append(u * x_to * expand(to_end, i))
            skip = kern_ref[KC : KC + 1, cols]
            du = du + x_in * x_to + skip * dy
            dskip[i] = dskip[i] + jnp.sum(dy * u, axis=0, keepdims=True)
            dus.append(du)
        linked = jnp.concatenate(linked, axis=1)
        fed = jnp.concatenate(fed, axis=1)
        cross_low = cross_grad.astype(bf16)
        dc_map = nn(linked, state_low) + nn(cross_low, bmap)
        db_map = nn(fed, ds_low) + tn(cross_low, cmap)
        y_sum = nn(jnp.concatenate(link_prod, axis=1), pick, highest)
        v = nn(jnp.concatenate(end_prod, axis=1), pick, highest)
        col_sums = rows_acc[...].T
        keep_sum = nn(nt(jnp.ones((8, N), f32), ds * state, highest), pick, highest)[0:1, :]
        d_end = keep * keep_sum + jnp.sum(v * dt, axis=0, keepdims=True)
        dcum = row_sums - col_sums * dt + y_sum - v * dt
        dcum = dcum + jnp.where(iota((CHUNK, LANES), 0) == CHUNK - 1, d_end, 0.0)
        dld = nn(triangle(False), dcum, highest)
        ddt = col_sums + v - dld * par_ref[1:2, :]
        dstep = ddt * jax.nn.sigmoid(raw)
        dstep_ref[rows, :] = dstep.astype(bf16)
        dbias = dbias + jnp.sum(dstep, axis=0, keepdims=True)
        drate = drate + jnp.sum(dld * ld, axis=0, keepdims=True)
        dstate[...] = per_state_row(keep, heads) * ds + tn(linked, cmap)
        grads = dus + [db_map, dc_map]
        for i in range(tiles):
            cols = slice(i * LANES, (i + 1) * LANES)
            dpre = grads[i] * sigs[i] * (1.0 + pre[i] * (1.0 - sigs[i]))
            dcs[HALO + r0 : HALO + r0 + CHUNK, cols] = dpre
            for j in range(KC):
                at = r0 + HALO - (KC - 1) + j
                term = jnp.where(off >= KC - 1 - j, ext[at : at + CHUNK, cols] * dpre, 0.0)
                dkern[j][i] = dkern[j][i] + jnp.sum(term, axis=0, keepdims=True)
    for i in range(tiles):
        cols = slice(i * LANES, (i + 1) * LANES)
        for j in range(KC):
            dkern_ref[j : j + 1, cols] = dkern[j][i]
        dkern_ref[KC : KC + 1, cols] = dskip[i] if i < pairs else jnp.zeros((1, LANES), f32)
        dkern_ref[KC + 1 :, cols] = jnp.zeros((8 - KC - 1, LANES), f32)
    dpar_ref[...] = jnp.zeros_like(dpar_ref)
    dpar_ref[0:1, :] = dbias
    dpar_ref[1:2, :] = drate

    dsl_pad[:HALO, :] = jnp.full((HALO, LANES), 1 << 20, jnp.int32)
    dsl_pad[HALO : HALO + tokens, :] = dsl_ref[...]
    dsl_pad[HALO + tokens :, :] = jnp.full((HALO, LANES), 1 << 20, jnp.int32)
    for start, count in [(-HALO, HALO)] + [(c * CHUNK, CHUNK) for c in range(chunks)]:
        keeps = []
        for q in range(KC):
            at = start + q
            place = at + iota((count, LANES), 0)
            reach = place - dsl_pad[HALO + at : HALO + at + count, :]
            keeps.append(jnp.where(reach >= q, 1.0, 0.0))
        for i in range(tiles):
            cols = slice(i * LANES, (i + 1) * LANES)
            acc = None
            for q in range(KC):
                at = HALO + start + q
                term = dcs[at : at + count, cols] * keeps[q] * kern_ref[KC - 1 - q : KC - q, cols]
                acc = term if acc is None else acc + term
            if start < 0:
                dhalo_ref[:, cols] = acc
            else:
                dim_ref[start : start + count, cols] = acc.astype(bf16)


def project_back_kernel(received, me_ref, *refs):
    gots = refs[:received]
    (zq_ref, dim_ref, dhalo_ref, dkv_ref, dstep_ref, cos_ref, sin_ref, w_ref,
     dis_ref, dmk_ref, own_ref, *parts) = refs[received:]
    tokens = zq_ref.shape[0]
    di = zq_ref.shape[1] - LANES
    size = tokens // 4
    tail = slice(tokens - HALO, tokens)
    dis_ref[:, :di] = dim_ref[:, :di]
    dis_ref[tail, :di] = (dim_ref[tail, :di].astype(f32) + dhalo_ref[:, :di]).astype(bf16)
    dis_ref[:, di:] = dstep_ref[...]
    dmk_ref[:, : 2 * N] = dim_ref[:, di:]
    dmk_ref[tail, : 2 * N] = (dim_ref[tail, di:].astype(f32) + dhalo_ref[:, di:]).astype(bf16)
    dkv = dkv_ref[...]
    for got in gots:
        dkv = dkv + got[...].astype(f32)
    turned = dkv * cos_ref[...] - swap_halves(dkv) * sin_ref[...]
    dmk_ref[:, 2 * N :] = jnp.where(low_lanes(dkv.shape), turned, dkv).astype(bf16)
    first, second = di + LANES, 2 * di + 2 * LANES
    for k in (1, 2, 3, 0):
        rows = block_rows(me_ref, k, size)
        part = nt(zq_ref[rows, :], w_ref[:, :first])
        part = part + nt(dis_ref[rows, :], w_ref[:, first:second])
        part = part + nt(dmk_ref[rows, :], w_ref[:, second:])
        if k:
            parts[k - 1][...] = part.astype(bf16)
        else:
            own_ref[...] = part


def products_kernel(count, me_ref, *refs):
    for i in range(count):
        refs[2 * count + i][...] = tn(refs[2 * i][...], refs[2 * i + 1][...]).astype(bf16)


def last_products_kernel(
    me_ref, h_ref, dis_ref, dmk_ref, kern_ref, par_ref, one_ref, two_ref, is_ref, own_ref, *parts
):
    di = dis_ref.shape[1] - LANES
    rows = h_ref.shape[1]
    size = rows // 4
    width = one_ref.shape[1]
    wide = dmk_ref.shape[1]
    is_ref[:rows, :] = tn(h_ref[...], dis_ref[...]).astype(bf16)
    small = jnp.concatenate([kern_ref[:, :di], par_ref[...]], axis=1)
    is_ref[rows:, :] = both(small, jnp.zeros_like(small), 0).astype(bf16)
    pieces = []
    for ref in (one_ref, two_ref):
        for at in range(0, width, wide):
            piece = ref[0:1, at : at + wide]
            if piece.shape[1] < wide:
                piece = both(piece, jnp.zeros((1, wide - piece.shape[1]), f32), 1)
            pieces.append(piece)
    taps = both(kern_ref[:KC, di:], jnp.zeros((KC, wide - 2 * N), f32), 1)
    pieces.append(taps)
    pieces.append(jnp.zeros((HALO - KC - len(pieces) + 1, wide), f32))
    extra = jnp.concatenate(pieces, axis=0)
    for k in range(4):
        at = pl.ds(pl.multiple_of((me_ref[0] ^ k) * size, size), size)
        block = tn(h_ref[:, at], dmk_ref[...])
        out = parts[k - 1] if k else own_ref
        out[:size, :] = block.astype(out.dtype)
        out[size:, :] = extra.astype(out.dtype)


def share_sum_kernel(me_ref, own_ref, r1, r2, r3, out_ref):
    size = own_ref.shape[0] - HALO
    wide = own_ref.shape[1]
    near = own_ref[...] + r1[...].astype(f32)
    far = r2[...].astype(f32) + r3[...].astype(f32)
    total = near + far
    out_ref[:, : 2 * N] = total[:, : 2 * N].astype(bf16)
    first = me_ref[0] // 2 == 0
    mine, other = near[:size, 2 * N :], far[:size, 2 * N :]
    a, b = jnp.where(first, mine, other), jnp.where(first, other, mine)
    low = low_lanes(a.shape)
    out_ref[:size, 2 * N : 2 * N + LANES] = jnp.where(low, a, pltpu.roll(b, HEAD_WIDTH, 1)).astype(bf16)
    out_ref[:size, 2 * N + LANES :] = jnp.where(low, pltpu.roll(a, HEAD_WIDTH, 1), b).astype(bf16)
    out_ref[size:, 2 * N : wide] = total[size:, 2 * N :].astype(bf16)
    out_ref[size:, wide:] = jnp.zeros((HALO, out_ref.shape[1] - wide), bf16)


def trade(array, k):
    places = range(lax.axis_size("tensor"))
    return lax.ppermute(array, "tensor", [(i, i ^ k) for i in places])


def trades(arrays):
    return [trade(array, k + 1) for k, array in enumerate(arrays)]


def from_shard(array, distance):
    places = range(lax.axis_size("seq"))
    route = [(i - distance, i) for i in places if i - distance in places]
    return lax.ppermute(array, "seq", route)


def from_shards(array, sign):
    return [from_shard(array, sign * d) for d in range(1, lax.axis_size("seq"))]


def other_core(array):
    return lax.ppermute(array, "pipe", [(0, 1), (1, 0)])


def finish(me, resid, own, *parts):
    (out_own,) = call(
        out_kernel, [sds(resid.shape, bf16)], [me, resid, own, *trades(parts)], name="layer_out"
    )
    return [out_own] + trades([out_own] * 3)


def last_out(saved, wt, me, after):
    resid, hidden = saved[-5], saved[-1]
    parts = call(
        down_kernel,
        [sds(resid.shape, f32)] + [sds(resid.shape, bf16)] * 3,
        [me, *fars(hidden, wt[3])],
        name="last_down",
        after=after,
    )
    return finish(me, resid, *parts)


def forward(x, x_own, wt, geo, last):
    w_cat, w_out, w_gu, w_down, gain_one, gain_two, kern, par = wt
    me, dsl, cos, sin, di = geo
    heads = di // P_SIZE
    tokens = dsl.shape[0]
    size, width = x_own.shape
    ff = w_down.value.shape[0]
    seqs = lax.axis_size("seq")
    wide = di + 2 * N
    low_parts = [sds((size, width), bf16)] * 3
    h, z, im, step, q, kv = call(
        partial(project_kernel, len(x), di),
        [
            Far(sds((tokens, width), bf16)),
            sds((tokens, di), f32),
            sds((tokens, wide), bf16),
            sds((tokens, LANES), f32),
            sds((tokens, LANES), bf16),
            sds((tokens, LANES), bf16),
        ],
        [me, *x, gain_one, w_cat, cos, sin],
        [pltpu.VMEM((tokens, width), bf16)] if len(x) > 1 else [],
        name="project",
    )
    halo = from_shard(im[tokens - HALO :], 1)
    kvs = [kv] + from_shards(kv, 1)
    mix0, cmap, lfac, packet = call(
        partial(ssm_forward_kernel, heads),
        [
            sds((tokens, di), f32),
            sds((tokens, N), bf16),
            sds((tokens, LANES), f32),
            sds((di + HALO, N), bf16),
        ],
        [me, im, halo, step, dsl, kern, par],
        [pltpu.VMEM((tokens + HALO, wide), f32), pltpu.VMEM((di, N), f32)],
        name="ssm_forward",
    )
    packets = from_shards(packet, 1)
    attn, lse = call(
        partial(attention_kernel, seqs),
        [sds((tokens, LANES), f32), Far(sds((tokens, LANES), f32))],
        [me, q, dsl, *kvs],
        [pltpu.VMEM((seqs, tokens, LANES), bf16)] * 2,
        name="attention",
    )
    mixed, ga, state_in, own, *parts = call(
        partial(mix_kernel, heads, len(packets)),
        [
            Far(sds((tokens, di), f32)),
            Far(sds((tokens, di + LANES), bf16)),
            Far(sds((di, N), f32)),
            sds((size, width), f32),
            *low_parts,
        ],
        [me, *packets, mix0, cmap, lfac, z, attn, w_out],
        name="mix",
    )
    resid, h_own = call(
        norm_two_kernel,
        [sds((size, width), f32), sds((size, width), bf16)],
        [me, x_own, own, *trades(parts), gain_two],
        name="norm_two",
    )
    h_two, gate, up, hidden, *parts = call(
        mlp_kernel,
        [
            *[
                Far(o) if not last else o
                for o in [sds((tokens, width), bf16)] + [sds((tokens, ff), bf16)] * 3
            ],
            *([] if last else [sds((size, width), f32), *low_parts]),
        ],
        [me, h_own, *trades([h_own] * 3), *fars(w_gu, w_down)],
        name="mlp",
    )
    out = None if last else finish(me, resid, *parts)
    saved = (
        x_own, h, z, im, step, q, halo, kvs, cmap, lfac, packet, attn, lse, mixed, ga, state_in,
        resid, h_two, gate, up, hidden,
    )
    return out, saved


def products(*pairs, me, after):
    return call(
        partial(products_kernel, len(pairs)),
        [Far(sds((a.shape[1], b.shape[1]), bf16)) for a, b in pairs],
        [me, *[x for a, b in pairs for x in (Far(a), b)]],
        name="products",
        after=after,
    )


def last_products(me, h, d_is, d_mk, *small, after=()):
    size = h.shape[1] // 4 + HALO
    wide = d_mk.shape[1]
    own_is, own, *parts = call(
        last_products_kernel,
        [Far(sds((h.shape[1] + HALO, d_is.shape[1]), bf16)), sds((size, wide), f32)]
        + [sds((size, wide), bf16)] * 3,
        [me, Far(h), d_is, d_mk, *small],
        name="last_products",
        after=after,
    )
    (shared,) = call(
        share_sum_kernel,
        [sds((size, 2 * N + 2 * LANES), bf16)],
        [me, own, *trades(parts)],
        name="share_sum",
    )
    return own_is, shared


def line_sum(x, cores):
    n = lax.axis_size("seq")
    here = lax.axis_index("seq")
    half = n // 2

    def send(x, route):
        route = [(c * n + a, c * n + b) for c in cores for a, b in route]
        return lax.ppermute(x, ("pipe", "seq"), route)

    for r in range(1, half):
        x = add(x, send(x, [(r - 1, r), (n - r, n - 1 - r)]))
    if n > 1:
        x = add(x, send(x, [(half - 1, half), (half, half - 1)]))
    for r in range(half - 1, 0, -1):
        got = send(x, [(r, r - 1), (n - 1 - r, n - r)])
        x = jnp.where((here == r - 1) | (here == n - r), got, x)
    return x


def add(a, b):
    return (a.astype(f32) + b.astype(f32)).astype(bf16)


def own_core_sum(first, second):
    core = lax.axis_index("pipe")
    keep = jnp.where(core == 0, first, second)
    return line_sum(add(keep, other_core(jnp.where(core == 0, second, first))), [0, 1])


def both_sum(arrays, *axes):
    return list(lax.psum(tuple(arrays), axes))


def backward(g, g_own, saved, wt, geo, first=(), second=()):
    (
        x_own, h, z, im, step, q, halo, kvs, cmap, lfac, packet, attn, lse, mixed, ga, state_in,
        resid, h_two, gate, up, hidden,
    ) = saved
    w_cat, w_out, w_gu, w_down, gain_one, gain_two, kern, par = wt
    me, dsl, cos, sin, di = geo
    heads = di // P_SIZE
    tokens = dsl.shape[0]
    size, width = x_own.shape
    ff = w_down.value.shape[0]
    seqs = lax.axis_size("seq")
    wide = di + 2 * N
    low_parts = [sds((size, width), bf16)] * 3
    dgate, dup, g_cat, own, *parts = call(
        partial(mlp_back_kernel, len(g)),
        [
            sds((tokens, ff), bf16),
            sds((tokens, ff), bf16),
            sds((tokens, width), bf16),
            sds((size, width), f32),
            *low_parts,
        ],
        [me, *g, *(fars(gate, up) if len(g) > 1 else (gate, up)), *fars(w_gu, w_down)],
        name="mlp_back",
        after=first,
    )
    got = trades(parts)
    d_resid, d_own, grad_gain_two = call(
        norm_back_kernel,
        [sds((size, width), f32), sds((size, width), bf16), sds((8, width), f32)],
        [me, g_own, own, *got, Far(resid), gain_two],
        name="norm_two_back",
        after=second,
    )
    early = products((h_two, dgate), (h_two, dup), (hidden, g_cat), me=me, after=[d_own])
    d_branch, d_mixed, dz, d_attn, packet_back = call(
        partial(mixer_back_kernel, heads),
        [
            sds((tokens, width), bf16),
            sds((tokens, di), f32),
            sds((tokens, di), bf16),
            sds((tokens, LANES), bf16),
            sds((di + HALO, N), bf16),
        ],
        [me, d_own, *trades([d_own] * 3), *fars(w_out, z, mixed, cmap, lfac, packet)],
        name="mixer_back",
        after=early,
    )
    packets = from_shards(packet_back, -1)
    zq, *dkvs = call(
        partial(attention_back_kernel, seqs),
        [sds((tokens, di + LANES), bf16), sds((tokens, LANES), f32)]
        + [sds((tokens, LANES), bf16)] * (seqs - 1),
        [me, *fars(q, dsl, attn, lse), d_attn, dz, *fars(cos, sin, *kvs)],
        [pltpu.VMEM((seqs, tokens, LANES), bf16)] * 2
        + [pltpu.VMEM((seqs, tokens, LANES), f32)] * 2,
        name="attention_back",
    )
    got_kv = [from_shard(dkvs[d], -d) for d in range(1, seqs)]
    d_im, d_halo, d_step, grad_kern, grad_par = call(
        partial(ssm_back_kernel, heads, len(packets)),
        [
            sds((tokens, wide), bf16),
            sds((HALO, wide), f32),
            sds((tokens, LANES), bf16),
            sds((8, wide), f32),
            sds((8, LANES), f32),
        ],
        [me, *packets, *fars(im, halo, step, dsl), kern, par, d_mixed, Far(state_in)],
        [
            pltpu.VMEM((tokens + HALO, wide), f32),
            pltpu.VMEM((tokens + 2 * HALO, wide), f32),
            pltpu.VMEM((tokens + 2 * HALO, LANES), jnp.int32),
            pltpu.VMEM((tokens // CHUNK, di, N), f32),
            pltpu.VMEM((di, N), f32),
            pltpu.VMEM((LANES, LANES), f32),
        ],
        name="ssm_back",
    )
    back_halo = from_shard(d_halo, -1)
    d_is, d_mk, own, *parts = call(
        partial(project_back_kernel, len(got_kv)),
        [
            sds((tokens, di + LANES), bf16),
            sds((tokens, 2 * N + LANES), bf16),
            sds((size, width), f32),
            *low_parts,
        ],
        [me, *got_kv, zq, d_im, back_halo, dkvs[0], d_step, *fars(cos, sin, w_cat)],
        name="project_back",
    )
    got = trades(parts)
    middle = products((ga, d_branch), (h, zq), me=me, after=[d_is])
    dx_own, grad_gain_one = call(
        norm_back_kernel,
        [sds((size, width), bf16), sds((8, width), f32)],
        [me, d_resid, own, *got, Far(x_own), gain_one],
        name="norm_one_back",
        after=middle,
    )
    dx = [dx_own] + trades([dx_own] * 3)
    last = h, d_is, d_mk, grad_kern, grad_par, grad_gain_one, grad_gain_two
    return dx, early, middle, last


def in_order(pieces, me):
    size = pieces[0].shape[0]
    whole = jnp.zeros((size * len(pieces), pieces[0].shape[1]), pieces[0].dtype)
    for k, piece in enumerate(pieces):
        whole = lax.dynamic_update_slice_in_dim(whole, piece, (me ^ k) * size, 0)
    return whole


def body(
    inputs,
    cotangent,
    doc_lengths,
    norm_one,
    w_gate_z,
    w_inner_x,
    w_bc,
    w_step,
    conv_inner,
    conv_bc,
    step_bias,
    decay_log,
    skip_gain,
    w_mix_out,
    w_query,
    keyval_weight,
    w_attn_out,
    norm_two,
    w_gate_up,
    w_down,
):
    core = lax.axis_index("pipe")
    place = lax.axis_index("tensor")
    me = jnp.stack([place, core]).astype(jnp.int32)
    tokens, width = inputs.shape[1:]
    di = w_gate_z.shape[2]
    heads = di // P_SIZE
    size = tokens // lax.axis_size("tensor")

    keyval_head = place * (w_query.shape[2] // HEAD_WIDTH) // (QUERY_HEADS // KEY_HEADS)
    key_at = keyval_head * HEAD_WIDTH
    value_at = KEY_HEADS * HEAD_WIDTH + key_at
    own_cat = jnp.concatenate(
        [
            w_gate_z[0],
            w_query[0],
            w_inner_x[0],
            jnp.pad(w_step[0], ((0, 0), (0, LANES - heads))),
            w_bc[0],
            lax.dynamic_slice_in_dim(keyval_weight[0], key_at, HEAD_WIDTH, 1),
            lax.dynamic_slice_in_dim(keyval_weight[0], value_at, HEAD_WIDTH, 1),
        ],
        axis=1,
    )
    own_out = jnp.concatenate([w_mix_out[0], w_attn_out[0]], axis=0)
    wide = di + 2 * N
    own_kern = jnp.concatenate(
        [
            jnp.concatenate([conv_inner[0], conv_bc[0]], axis=1),
            jnp.pad(jnp.repeat(skip_gain, P_SIZE, axis=1), ((0, KC - 1), (0, 2 * N))),
        ],
        axis=0,
    )
    own_par = jnp.pad(
        jnp.concatenate([step_bias, jnp.exp(decay_log)], axis=0), ((0, 6), (0, LANES - heads))
    )
    own_small = jnp.concatenate(
        [
            jnp.pad(jnp.concatenate([norm_one, norm_two], axis=0), ((0, 6), (0, 0))),
            jnp.pad(
                jnp.concatenate([own_kern, own_par], axis=1),
                ((0, 0), (0, width - wide - LANES)),
            ),
        ],
        axis=0,
    )
    mine = (own_cat, own_out, w_gate_up[0], w_down[0], own_small)
    theirs = [other_core(w) for w in mine]

    def weights(layer):
        small = jnp.where(core == layer, mine[-1], theirs[-1])
        return (
            *[Far(a, b, layer) for a, b in zip(mine[:-1], theirs[:-1])],
            small[0:1], small[1:2], small[8:, :wide], small[8:, wide : wide + LANES],
        )

    layers = [weights(0), weights(1)]

    x = lax.dynamic_index_in_dim(inputs, core, 0, keepdims=False)
    top = lax.dynamic_index_in_dim(cotangent, core, 0, keepdims=False)
    lengths = lax.dynamic_index_in_dim(doc_lengths, core, 0, keepdims=False)
    first = lax.axis_index("seq") * tokens
    spots = first + jnp.arange(tokens, dtype=jnp.int32)
    before = jnp.cumsum(lengths)[None, :] <= spots[:, None]
    starts = jnp.sum(jnp.where(before, lengths[None, :], 0), axis=1)
    dsl = jnp.broadcast_to((starts - first)[:, None], (tokens, LANES)).astype(jnp.int32)
    half = HEAD_WIDTH // 2
    frequency = rope_base ** (-2.0 * jnp.arange(half, dtype=f32) / HEAD_WIDTH)
    angles = (spots - starts).astype(f32)[:, None] * frequency[None, :]
    cos, sin = jnp.cos(angles), jnp.sin(angles)
    cos = jnp.concatenate([cos] * 4, axis=1)
    sin = jnp.concatenate([-sin, sin] * 2, axis=1)
    geo = (me, dsl, cos, sin, di)

    def share(whole):
        return lax.dynamic_slice_in_dim(whole, place * size, size, 0)

    out_0, saved_0 = forward([x], share(x), layers[0], geo, False)
    _, saved_1 = forward(out_0, out_0[0], layers[1], geo, True)
    dx_1, early_1, middle_1, last_1 = backward([top], share(top), saved_1, layers[1], geo)
    early_1 = both_sum(early_1, "pipe", "seq")
    last_1 = last_products(me, *last_1, after=[dx_1[0]])
    dx_0, early_0, middle_0, last_0 = backward(
        dx_1, dx_1[0], saved_0, layers[0], geo, [last_1[0]], early_1
    )
    late_1 = both_sum([*middle_1, last_1[0]], "seq", "pipe")
    *last_0, shared_0 = last_products(me, *last_0, after=late_1)
    sums_0 = both_sum([*early_0, *middle_0, *last_0], "pipe", "seq")
    sums_1 = [*early_1, *late_1]
    shared = own_core_sum(shared_0, last_1[1])
    out_1 = last_out(saved_1, layers[1], me, [dx_0[0]])

    gate, up, down, out, zq, last = [
        jnp.where(core == 0, a, b) for a, b in zip(sums_0, sums_1)
    ]
    quarter = shared[: width // 4]
    every = shared[width // 4 :].astype(f32)
    shared = in_order([quarter] + trades([quarter] * 3), place).astype(f32)
    gate, up, down, out, zq = [a.astype(f32) for a in (gate, up, down, out, zq)]
    own_small = last[width:].astype(f32)
    last = last[:width].astype(f32)
    step_128 = 2 * N + LANES
    count = -(-width // step_128)
    gain_one = every[:count, :step_128].reshape(-1)[:width]
    gain_two = every[count : 2 * count, :step_128].reshape(-1)[:width]
    taps = every[2 * count : 2 * count + KC, : 2 * N]
    skip = jnp.sum(own_small[KC, :di].reshape(heads, P_SIZE), axis=1)

    def both_micros(first_layer, second_layer):
        a, b = in_order(first_layer, place), in_order(second_layer, place)
        keep = jnp.where(core == 0, a, b)
        got = other_core(jnp.where(core == 0, b, a))
        return jnp.stack([jnp.where(core == 0, keep, got), jnp.where(core == 0, got, keep)])

    layer_out = both_micros(out_0, out_1)
    input_grad = both_micros(dx_0, dx_1)
    results = (
        layer_out,
        input_grad,
        gain_one,
        zq[:, :di],
        last[:, :di],
        shared[:, : 2 * N],
        last[:, di : di + heads],
        own_small[:KC, :di],
        taps,
        own_small[0, di : di + heads],
        own_small[1, di : di + heads],
        skip,
        out[:di],
        zq[:, di:],
        shared[:, 2 * N :],
        out[di:],
        gain_two,
        jnp.stack([gate, up]),
        down,
    )
    return tuple(r[None] for r in results)


def solution(mesh):
    token_spec = P(None, "seq", None)
    columns = P("pipe", None, "tensor")
    rows = P("pipe", "tensor", None)
    layer = P("pipe", None, None)
    vector = P("pipe", None)
    heads = P("pipe", "tensor")
    outs = P("pipe", None, "seq", None)
    gate_up = P("pipe", None, None, "tensor")
    return jax.shard_map(
        body,
        mesh=mesh,
        in_specs=(
            token_spec, token_spec, P(), vector, columns, columns, layer, columns, columns, layer,
            heads, heads, heads, rows, columns, layer, rows, vector, gate_up, rows,
        ),
        out_specs=(
            outs, outs, vector, columns, columns, layer, columns, columns, layer,
            heads, heads, heads, rows, columns, layer, rows, vector, gate_up, rows,
        ),
        check_vma=False,
    )
```

```python
from functools import partial

import jax
import jax.numpy as jnp
from jax import lax
from jax.experimental import pallas as pl
from jax.experimental.pallas import tpu as pltpu
from jax.sharding import PartitionSpec as P

P_SIZE = 64
N = 128
KC = 4
KEY_HEADS = 2
QUERY_HEADS = 8
HEAD_WIDTH = 64
CHUNK = 128
LANES = 128
HALO = 16

f32 = jnp.float32
bf16 = jnp.bfloat16
highest = lax.Precision.HIGHEST
eps_norm = 1e-05
rope_base = 100000000000.0
masked_score = -1e30
score_scale = HEAD_WIDTH ** (-0.5)


def nn(a, b, precision=None):
    return lax.dot_general(
        a, b, (((1,), (0,)), ((), ())), precision=precision, preferred_element_type=f32
    )


def nt(a, b, precision=None):
    return lax.dot_general(
        a, b, (((1,), (1,)), ((), ())), precision=precision, preferred_element_type=f32
    )


def tn(a, b, precision=None):
    return lax.dot_general(
        a, b, (((0,), (0,)), ((), ())), precision=precision, preferred_element_type=f32
    )


def iota(shape, axis):
    return lax.broadcasted_iota(jnp.int32, shape, axis)


def sds(shape, kind):
    return jax.ShapeDtypeStruct(shape, kind)


MICROSECONDS = {
    "project": 3.0,
    "ssm_forward": 3.8,
    "attention": 5.5,
    "mix": 1.6,
    "norm_two": 1.0,
    "mlp": 2.3,
    "layer_out": 1.0,
    "last_down": 1.0,
    "mlp_back": 0.46,
    "norm_two_back": 0.12,
    "mixer_back": 0.21,
    "attention_back": 0.82,
    "ssm_back": 1.38,
    "project_back": 0.39,
    "norm_one_back": 0.12,
    "products": 0.20,
    "last_products": 0.22,
    "share_sum": 0.09,
}


class Far:
    def __init__(self, value, other=None, layer=None):
        self.value, self.other, self.layer = value, other, layer


def fars(*values):
    return [value if isinstance(value, Far) else Far(value) for value in values]


class Arriving:
    def __init__(self, ref, copy):
        self.ref, self.copy, self.shape = ref, copy, ref.shape

    def ready(self):
        if self.copy is not None:
            self.copy.wait()
            self.copy = None

    def __getitem__(self, index):
        self.ready()
        return self.ref[index]


def in_hbm(array):
    return pltpu.with_memory_space_constraint(array, pltpu.HBM)


def call(kernel, outs, args, scratch=(), name=None, after=()):
    count = len(args)
    far_in = {i: a for i, a in enumerate(args) if isinstance(a, Far)}
    far_out = [i for i, o in enumerate(outs) if isinstance(o, Far)]
    args = [in_hbm(a.value) if isinstance(a, Far) else a for a in args]
    others = {i: k for k, i in enumerate(i for i, a in far_in.items() if a.other is not None)}
    after = [in_hbm(far_in[i].other) for i in others] + [in_hbm(a) for a in after]
    wait = len(after)
    outs = [pltpu.HBM(o.value.shape, o.value.dtype) if isinstance(o, Far) else o for o in outs]

    def run(*refs):
        ins = list(refs[:count])
        results = list(refs[count + wait : count + wait + len(outs)])
        rest = list(refs[count + wait + len(outs) :])
        own = rest[: len(scratch)]
        near = rest[len(scratch) : len(scratch) + len(far_in) + len(far_out)]
        for k, (i, far) in enumerate(far_in.items()):
            copy = pltpu.make_async_copy(ins[i], near[k], rest[-1].at[k])
            if i in others:
                other = pltpu.make_async_copy(refs[count + others[i]], near[k], rest[-1].at[k])
                mine = ins[0][1] == far.layer
                pl.when(mine)(copy.start)
                pl.when(jnp.logical_not(mine))(other.start)
            else:
                copy.start()
            ins[i] = Arriving(near[k], copy)
        copies = []
        for k, i in enumerate(far_out):
            k = k + len(far_in)
            copies.append(pltpu.make_async_copy(near[k], results[i], rest[-1].at[k]))
            results[i] = near[k]
        kernel(*ins, *results, *own)
        for i in far_in:
            ins[i].ready()
        for copy in copies:
            copy.start()
        for copy in copies:
            copy.wait()

    def spec(far):
        return pl.BlockSpec(memory_space=pltpu.HBM if far else pltpu.VMEM)

    specs = [pl.BlockSpec(memory_space=pltpu.SMEM)]
    specs += [spec(i in far_in) for i in range(1, count)]
    specs += [spec(True) for _ in after]
    scratch = list(scratch)
    extra = [pltpu.VMEM(args[i].shape, args[i].dtype) for i in far_in]
    extra += [pltpu.VMEM(outs[i].shape, outs[i].dtype) for i in far_out]
    if extra:
        extra.append(pltpu.SemaphoreType.DMA((len(extra),)))
    return pl.pallas_call(
        run,
        out_shape=outs,
        in_specs=specs,
        out_specs=[spec(i in far_out) for i in range(len(outs))],
        scratch_shapes=scratch + extra,
        compiler_params=pltpu.CompilerParams(
            vmem_limit_bytes=(14 + 2 * lax.axis_size("seq")) * 1024 * 1024
        ),
        cost_estimate=pl.CostEstimate(
            flops=int(MICROSECONDS[name] * 1.1e9), bytes_accessed=0, transcendentals=0
        ),
        name=name,
    )(*args, *after)


def block_rows(me_ref, k, size):
    return pl.ds(pl.multiple_of((me_ref[0] ^ k) * size, size), size)


def rms_scale(x):
    return lax.rsqrt(jnp.mean(x * x, axis=-1, keepdims=True) + eps_norm)


def swap_halves(x):
    lane = iota(x.shape, 1) % HEAD_WIDTH
    ahead = pltpu.roll(x, LANES - HEAD_WIDTH // 2, 1)
    behind = pltpu.roll(x, HEAD_WIDTH // 2, 1)
    return jnp.where(lane < HEAD_WIDTH // 2, ahead, behind)


def low_lanes(shape):
    return iota(shape, 1) < HEAD_WIDTH


def project_kernel(pieces, di, me_ref, *refs):
    xs = refs[:pieces]
    (gain_ref, w_ref, cos_ref, sin_ref,
     h_ref, z_ref, im_ref, step_ref, q_ref, kv_ref, *held) = refs[pieces:]
    tokens = h_ref.shape[0]
    size = tokens // 4
    source = xs[0]
    if pieces > 1:
        (source,) = held
        for k in range(4):
            source[block_rows(me_ref, k, size), :] = xs[k][...]
    w_ref.ready()

    def block(k, nothing):
        rows = pl.ds(pl.multiple_of(k * size, size), size)
        x = source[rows, :].astype(f32)
        h = (x * rms_scale(x) * gain_ref[...]).astype(bf16)
        h_ref[rows, :] = h
        p = nn(h, w_ref[...])
        z_ref[rows, :] = p[:, :di]
        cos, sin = cos_ref[rows, :], sin_ref[rows, :]
        q = p[:, di : di + LANES]
        q_ref[rows, :] = (q * cos + swap_halves(q) * sin).astype(bf16)
        im_ref[rows, :di] = p[:, di + LANES : 2 * di + LANES].astype(bf16)
        at = 2 * di
        step_ref[rows, :] = p[:, at + LANES : at + 2 * LANES]
        im_ref[rows, di:] = p[:, at + 2 * LANES : at + 4 * LANES].astype(bf16)
        kv = p[:, at + 4 * LANES :]
        turned = kv * cos + swap_halves(kv) * sin
        kv_ref[rows, :] = jnp.where(low_lanes(kv.shape), turned, kv).astype(bf16)
        return nothing

    lax.fori_loop(0, 4, block, 0)


def fill_ext(ext, halo_ref, im_ref):
    ext[:HALO, :] = halo_ref[...].astype(f32)
    ext[HALO:, :] = im_ref[...].astype(f32)


def triangle(lower):
    r, c = iota((CHUNK, CHUNK), 0), iota((CHUNK, CHUNK), 1)
    return jnp.where((c <= r) if lower else (c >= r), 1.0, 0.0).astype(f32)


def expand(cols, i):
    shape = (cols.shape[0], LANES)
    return jnp.where(
        low_lanes(shape),
        jnp.broadcast_to(cols[:, 2 * i : 2 * i + 1], shape),
        jnp.broadcast_to(cols[:, 2 * i + 1 : 2 * i + 2], shape),
    )


def expand_all(cols, tiles):
    return jnp.concatenate([expand(cols, i) for i in range(tiles)], axis=1)


def per_state_row(row, heads):
    return jnp.concatenate(
        [jnp.broadcast_to(row[:, h : h + 1], (P_SIZE, N)) for h in range(heads)], axis=0
    )


def chunk_steps(c, step_ref, dsl_ref, par_ref):
    r0 = c * CHUNK
    rows = slice(r0, r0 + CHUNK)
    raw = step_ref[rows, :] + par_ref[0:1, :]
    dt = jnp.maximum(raw, 0.0) + jnp.log1p(jnp.exp(-jnp.abs(raw)))
    ld = -dt * par_ref[1:2, :]
    cum = nn(triangle(True), ld, highest)
    dsl = dsl_ref[rows, :]
    place = r0 + iota((CHUNK, LANES), 0)
    end = cum[CHUNK - 1 : CHUNK, :]
    dsl_end = dsl[CHUNK - 1 : CHUNK, :]
    to_end = jnp.where(place >= dsl_end, jnp.exp(end - cum), 0.0)
    link = jnp.where(dsl < r0, jnp.exp(cum), 0.0)
    keep = jnp.where(dsl_end < r0, jnp.exp(end), 0.0)
    allowed = (iota((CHUNK, CHUNK), 1) <= iota((CHUNK, CHUNK), 0)) & (
        r0 + iota((CHUNK, CHUNK), 1) >= dsl
    )
    return raw, dt, ld, cum, dsl, place - dsl, end, to_end, link, keep, allowed


def chunk_conv(c, off, ext, kern_ref, tiles):
    r0 = c * CHUNK
    keeps = [jnp.where(off >= KC - 1 - j, 1.0, 0.0) for j in range(KC)]
    outs = []
    for i in range(tiles):
        cols = slice(i * LANES, (i + 1) * LANES)
        acc = None
        for j in range(KC):
            at = r0 + HALO - (KC - 1) + j
            term = ext[at : at + CHUNK, cols] * keeps[j] * kern_ref[j : j + 1, cols]
            acc = term if acc is None else acc + term
        outs.append(acc)
    return outs


def decays(cum, cum_t, allowed, h):
    gap = cum[:, h : h + 1] - cum_t[h : h + 1, :]
    return jnp.exp(jnp.where(allowed, gap, masked_score))


def both(a0, a1, axis):
    return jnp.concatenate([a0, a1], axis=axis)


def split_pair(x):
    low = low_lanes(x.shape)
    return both(jnp.where(low, x, 0.0), jnp.where(low, 0.0, x), 0)


def ssm_forward_kernel(
    heads, me_ref, im_ref, halo_ref, step_ref, dsl_ref, kern_ref, par_ref,
    mix_ref, cmap_ref, lfac_ref, packet_ref, ext, state,
):
    tokens = im_ref.shape[0]
    pairs = heads // 2
    fill_ext(ext, halo_ref, im_ref)
    state[...] = jnp.zeros_like(state)
    base = jnp.zeros((1, LANES), f32)
    for c in range(tokens // CHUNK):
        rows = slice(c * CHUNK, (c + 1) * CHUNK)
        raw, dt, ld, cum, dsl, off, end, to_end, link, keep, allowed = chunk_steps(
            c, step_ref, dsl_ref, par_ref
        )
        acts = [a * jax.nn.sigmoid(a) for a in chunk_conv(c, off, ext, kern_ref, pairs + 2)]
        bmap, cmap = acts[pairs].astype(bf16), acts[pairs + 1].astype(bf16)
        cum_t, dt_t = cum.T, dt.T
        cross = nt(cmap, bmap)
        carried = nt(cmap, state[...].astype(bf16)) if c else None
        ins = to_end * dt
        fed = []
        for i in range(pairs):
            u = acts[i]
            weights = [
                (decays(cum, cum_t, allowed, h) * cross * dt_t[h : h + 1, :]).astype(bf16)
                for h in (2 * i, 2 * i + 1)
            ]
            cols = slice(i * LANES, (i + 1) * LANES)
            y = nn(both(*weights, 1), split_pair(u).astype(bf16))
            if c:
                y = y + carried[:, cols] * expand(link, i)
            mix_ref[rows, cols] = y + kern_ref[KC : KC + 1, cols] * u
            fed.append((u * expand(ins, i)).astype(bf16))
        fresh = tn(jnp.concatenate(fed, axis=1), bmap)
        state[...] = per_state_row(keep, heads) * state[...] + fresh
        cmap_ref[rows, :] = cmap
        lfac = jnp.where(dsl < 0, jnp.exp(base + cum), 0.0)
        lfac_ref[rows, :] = lfac
        base = base + end
    packet_ref[: heads * P_SIZE, :] = state[...].astype(bf16)
    packet_ref[heads * P_SIZE :, :] = jnp.broadcast_to(
        lfac[CHUNK - 1 : CHUNK, :], (HALO, LANES)
    ).astype(bf16)


def arriving(packets, heads):
    total = None
    for ref in packets[::-1]:
        own = ref[: heads * P_SIZE, :].astype(f32)
        if total is not None:
            row = ref[heads * P_SIZE : heads * P_SIZE + 1, :].astype(f32)
            own = own + per_state_row(row, heads) * total
        total = own
    return total


def mix_kernel(heads, packets, me_ref, *refs):
    ins = refs[:packets]
    (mix_ref, cmap_ref, lfac_ref, z_ref, attn_ref, w_ref,
     mixed_ref, ga_ref, state_ref, own_ref, *part_refs) = refs[packets:]
    tokens = mix_ref.shape[0]
    size = tokens // 4
    pairs = heads // 2
    di = heads * P_SIZE
    if packets:
        state = arriving(ins, heads)
    else:
        state = jnp.zeros(state_ref.shape, f32)
    state_ref[...] = state
    state = state.astype(bf16)
    for k in (1, 2, 3, 0):
        rows = block_rows(me_ref, k, size)
        carried = nt(cmap_ref[rows, :], state)
        mixed = mix_ref[rows, :] + carried * expand_all(lfac_ref[rows, :], pairs)
        mixed_ref[rows, :] = mixed
        z = z_ref[rows, :]
        ga_ref[rows, :di] = (mixed * z * jax.nn.sigmoid(z)).astype(bf16)
        ga_ref[rows, di:] = attn_ref[rows, :].astype(bf16)
        part = nn(ga_ref[rows, :], w_ref[...])
        if k:
            part_refs[k - 1][...] = part.astype(bf16)
        else:
            own_ref[...] = part


def spread_keyval(ref):
    kv = ref[...].astype(f32)
    other = pltpu.roll(kv, HEAD_WIDTH, 1)
    low = low_lanes(kv.shape)
    return (
        jnp.where(low, kv, other).astype(bf16),
        jnp.where(low, other, kv).astype(bf16),
    )


def pair_mask(r0, d, tokens, dsl):
    shape = (CHUNK, tokens)
    key = iota(shape, 1) - d * tokens
    ok = key >= jnp.broadcast_to(dsl[:, 0:1], shape)
    if d == 0:
        ok = ok & (key <= r0 + iota(shape, 0))
    return both(ok, ok, 0)


def attention_kernel(blocks, me_ref, q_ref, dsl_ref, *refs):
    kvs = refs[:blocks]
    attn_ref, lse_ref, keys, values = refs[blocks:]
    tokens = q_ref.shape[0]
    for d in range(blocks):
        keys[d], values[d] = spread_keyval(kvs[d])
    for c in range(tokens // CHUNK):
        r0 = c * CHUNK
        rows = slice(r0, r0 + CHUNK)
        q = split_pair(q_ref[rows, :].astype(f32)).astype(bf16)
        dsl = dsl_ref[rows, :]
        top = total = acc = None
        for d in range(blocks):
            ok = pair_mask(r0, d, tokens, dsl)
            scores = jnp.where(ok, nt(q, keys[d]) * score_scale, masked_score)
            block_top = jnp.max(scores, axis=1, keepdims=True)
            if d == 0:
                top = block_top
                weights = jnp.exp(scores - top)
                total = jnp.sum(weights, axis=1, keepdims=True)
                acc = nn(weights.astype(bf16), values[d])
            else:
                new_top = jnp.maximum(top, block_top)
                factor = jnp.exp(top - new_top)
                weights = jnp.exp(scores - new_top)
                total = total * factor + jnp.sum(weights, axis=1, keepdims=True)
                acc = acc * factor + nn(weights.astype(bf16), values[d])
                top = new_top
        out = acc / total
        low = low_lanes((CHUNK, LANES))
        attn_ref[rows, :] = jnp.where(low, out[:CHUNK], out[CHUNK:])
        lse = jnp.broadcast_to(top + jnp.log(total), (2 * CHUNK, LANES))
        lse_ref[rows, :] = jnp.where(low, lse[:CHUNK], lse[CHUNK:])


def attention_back_kernel(
    blocks, me_ref, q_ref, dsl_ref, attn_ref, lse_ref, dattn_ref, dz_ref, cos_ref, sin_ref, *refs
):
    kvs = refs[:blocks]
    zq_ref = refs[blocks]
    outs = refs[blocks + 1 : 2 * blocks + 1]
    keys, values, dkeys, dvalues = refs[2 * blocks + 1 :]
    tokens = q_ref.shape[0]
    low = low_lanes((CHUNK, LANES))
    zq_ref[:, : dz_ref.shape[1]] = dz_ref[...]
    for d in range(blocks):
        keys[d], values[d] = spread_keyval(kvs[d])
    for c in range(tokens // CHUNK):
        r0 = c * CHUNK
        rows = slice(r0, r0 + CHUNK)
        q = split_pair(q_ref[rows, :].astype(f32)).astype(bf16)
        dout = dattn_ref[rows, :].astype(f32)
        prod = split_pair(dout * attn_ref[rows, :])
        delta = jnp.sum(prod, axis=1, keepdims=True)
        dout = split_pair(dout).astype(bf16)
        lse = lse_ref[rows, :]
        lse = both(lse[:, 0:1], lse[:, HEAD_WIDTH : HEAD_WIDTH + 1], 0)
        dsl = dsl_ref[rows, :]
        dq = None
        for d in range(blocks):
            ok = pair_mask(r0, d, tokens, dsl)
            scores = jnp.where(ok, nt(q, keys[d]) * score_scale - lse, masked_score)
            probs = jnp.exp(scores)
            dprobs = nt(dout, values[d])
            dscores = (probs * (dprobs - delta) * score_scale).astype(bf16)
            probs = probs.astype(bf16)
            part = nn(dscores, keys[d])
            dq = part if dq is None else dq + part
            dk, dv = tn(dscores, q), tn(probs, dout)
            if c:
                dkeys[d] += dk
                dvalues[d] += dv
            else:
                dkeys[d] = dk
                dvalues[d] = dv
        dq = jnp.where(low, dq[:CHUNK], dq[CHUNK:])
        dq = dq * cos_ref[rows, :] - swap_halves(dq) * sin_ref[rows, :]
        zq_ref[rows, dz_ref.shape[1] :] = dq.astype(bf16)
    wide = low_lanes((tokens, LANES))
    for d in range(blocks):
        dk, dv = dkeys[d], dvalues[d]
        dk = dk + pltpu.roll(dk, HEAD_WIDTH, 1)
        dv = dv + pltpu.roll(dv, HEAD_WIDTH, 1)
        outs[d][...] = jnp.where(wide, dk, dv).astype(outs[d].dtype)


def norm_two_kernel(me_ref, x_ref, own_ref, r1, r2, r3, gain_ref, resid_ref, h_ref):
    resid = x_ref[...].astype(f32) + own_ref[...]
    for r in (r1, r2, r3):
        resid = resid + r[...].astype(f32)
    resid_ref[...] = resid
    h_ref[...] = (resid * rms_scale(resid) * gain_ref[...]).astype(bf16)


def mlp_kernel(
    me_ref, h0, h1, h2, h3, gu_ref, down_ref, h_ref, gate_ref, up_ref, hid_ref, *rest
):
    size = h0.shape[0]
    for k, ref in ((1, h1), (2, h2), (3, h3), (0, h0)):
        rows = slice(k * size, (k + 1) * size)
        h = ref[...]
        h_ref[rows, :] = h
        gate = nn(h, gu_ref[0])
        up = nn(h, gu_ref[1])
        gate_ref[rows, :] = gate.astype(bf16)
        up_ref[rows, :] = up.astype(bf16)
        hidden = (gate * jax.nn.sigmoid(gate) * up).astype(bf16)
        hid_ref[rows, :] = hidden
        if rest:
            own_ref, *parts = rest
            part = nn(hidden, down_ref[...])
            if k:
                parts[k - 1][...] = part.astype(bf16)
            else:
                own_ref[...] = part


def down_kernel(me_ref, hid_ref, down_ref, own_ref, *parts):
    size = own_ref.shape[0]
    for k in (1, 2, 3, 0):
        part = nn(hid_ref[k * size : (k + 1) * size, :], down_ref[...])
        if k:
            parts[k - 1][...] = part.astype(bf16)
        else:
            own_ref[...] = part


def out_kernel(me_ref, resid_ref, own_ref, r1, r2, r3, out_ref):
    out = resid_ref[...] + own_ref[...]
    for r in (r1, r2, r3):
        out = out + r[...].astype(f32)
    out_ref[...] = out.astype(bf16)


def mlp_back_kernel(pieces, me_ref, *refs):
    gs = refs[:pieces]
    gate_ref, up_ref, gu_ref, down_ref, dgate_ref, dup_ref, g_ref, own_ref, *parts = refs[pieces:]
    size = gate_ref.shape[0] // 4
    for k in (1, 2, 3, 0):
        rows = slice(k * size, (k + 1) * size)
        g = gs[0][block_rows(me_ref, k, size), :] if pieces == 1 else gs[k][...]
        g_ref[rows, :] = g
        dhid = nt(g, down_ref[...])
        gate, up = gate_ref[rows, :].astype(f32), up_ref[rows, :].astype(f32)
        sig = jax.nn.sigmoid(gate)
        dgate = (dhid * up * sig * (1.0 + gate * (1.0 - sig))).astype(bf16)
        dup = (dhid * gate * sig).astype(bf16)
        dgate_ref[rows, :] = dgate
        dup_ref[rows, :] = dup
        part = nt(dgate, gu_ref[0]) + nt(dup, gu_ref[1])
        if k:
            parts[k - 1][...] = part.astype(bf16)
        else:
            own_ref[...] = part


def norm_back_kernel(me_ref, base_ref, own_ref, r1, r2, r3, x_ref, gain_ref, *outs):
    low_ref, gain_grad_ref = outs[-2:]
    dh = own_ref[...]
    for r in (r1, r2, r3):
        dh = dh + r[...].astype(f32)
    x = x_ref[...].astype(f32)
    r = rms_scale(x)
    n = x * r
    gain_grad_ref[...] = jnp.broadcast_to(
        jnp.sum(dh * n, axis=0, keepdims=True), gain_grad_ref.shape
    )
    dn = dh * gain_ref[...]
    dx = base_ref[...].astype(f32) + r * (dn - n * jnp.mean(dn * n, axis=-1, keepdims=True))
    if len(outs) == 3:
        outs[0][...] = dx
    low_ref[...] = dx.astype(bf16)


def mixer_back_kernel(
    heads, me_ref, d0, d1, d2, d3, w_ref, z_ref, mixed_ref, cmap_ref, lfac_ref, passing_ref,
    dbr_ref, dmixed_ref, dz_ref, dattn_ref, packet_ref,
):
    size = d0.shape[0]
    di = heads * P_SIZE
    pairs = heads // 2
    own = None
    for k, ref in ((0, d0), (1, d1), (2, d2), (3, d3)):
        rows = block_rows(me_ref, k, size)
        d = ref[...]
        dbr_ref[rows, :] = d
        p = nt(d, w_ref[...])
        dgated = p[:, :di]
        z = z_ref[rows, :]
        sig = jax.nn.sigmoid(z)
        act = z * sig
        dmixed = dgated * act
        dmixed_ref[rows, :] = dmixed
        dz_ref[rows, :] = (dgated * mixed_ref[rows, :] * sig * (1.0 + z * (1.0 - sig))).astype(bf16)
        dattn_ref[rows, :] = p[:, di:].astype(bf16)
        linked = (dmixed * expand_all(lfac_ref[rows, :], pairs)).astype(bf16)
        part = tn(linked, cmap_ref[rows, :])
        own = part if own is None else own + part
    packet_ref[:di, :] = own.astype(bf16)
    packet_ref[di:, :] = passing_ref[di:, :]


def ssm_back_kernel(heads, packets, me_ref, *refs):
    ins = refs[:packets]
    (im_ref, halo_ref, step_ref, dsl_ref, kern_ref, par_ref, dmixed_ref, state_in_ref,
     dim_ref, dhalo_ref, dstep_ref, dkern_ref, dpar_ref,
     ext, dcs, dsl_pad, states, dstate, rows_acc) = refs[packets:]
    tokens = im_ref.shape[0]
    chunks = tokens // CHUNK
    pairs = heads // 2
    di = heads * P_SIZE
    tiles = pairs + 2
    fill_ext(ext, halo_ref, im_ref)
    pick = jnp.where(
        iota((di, LANES), 0) // P_SIZE == iota((di, LANES), 1), 1.0, 0.0
    ).astype(f32)

    states[0] = state_in_ref[...]
    for c in range(chunks - 1):
        raw, dt, ld, cum, dsl, off, end, to_end, link, keep, allowed = chunk_steps(
            c, step_ref, dsl_ref, par_ref
        )
        acts = [a * jax.nn.sigmoid(a) for a in chunk_conv(c, off, ext, kern_ref, pairs + 1)]
        ins_ = to_end * dt
        fed = jnp.concatenate([(acts[i] * expand(ins_, i)).astype(bf16) for i in range(pairs)], 1)
        states[c + 1] = per_state_row(keep, heads) * states[c] + tn(fed, acts[pairs].astype(bf16))

    if packets:
        dstate[...] = arriving(ins, heads)
    else:
        dstate[...] = jnp.zeros_like(dstate)
    dcs[:HALO, :] = jnp.zeros((HALO, tiles * LANES), f32)
    dcs[HALO + tokens :, :] = jnp.zeros((HALO, tiles * LANES), f32)
    drate = jnp.zeros((1, LANES), f32)
    dbias = jnp.zeros((1, LANES), f32)
    dskip = [jnp.zeros((1, LANES), f32) for _ in range(pairs)]
    dkern = [[jnp.zeros((1, LANES), f32) for _ in range(tiles)] for _ in range(KC)]
    rows_acc[...] = jnp.zeros_like(rows_acc)
    lane = iota((CHUNK, LANES), 1)
    for c in range(chunks - 1, -1, -1):
        r0 = c * CHUNK
        rows = slice(r0, r0 + CHUNK)
        raw, dt, ld, cum, dsl, off, end, to_end, link, keep, allowed = chunk_steps(
            c, step_ref, dsl_ref, par_ref
        )
        pre = chunk_conv(c, off, ext, kern_ref, tiles)
        sigs = [jax.nn.sigmoid(a) for a in pre]
        acts = [a * s for a, s in zip(pre, sigs)]
        bmap, cmap = acts[pairs].astype(bf16), acts[pairs + 1].astype(bf16)
        cum_t, dt_t = cum.T, dt.T
        cross = nt(cmap, bmap)
        state = states[c]
        state_low = state.astype(bf16)
        ds = dstate[...]
        ds_low = ds.astype(bf16)
        carried = nt(cmap, state_low)
        towards = nt(bmap, ds_low)
        ins_ = to_end * dt
        cross_grad = jnp.zeros((CHUNK, CHUNK), f32)
        row_sums = jnp.zeros((CHUNK, LANES), f32)
        linked, fed, link_prod, end_prod, dus = [], [], [], [], []
        for i in range(pairs):
            cols = slice(i * LANES, (i + 1) * LANES)
            u = acts[i]
            dy = dmixed_ref[rows, cols]
            dy2 = split_pair(dy).astype(bf16)
            dw2 = nt(dy2, u.astype(bf16))
            weights = []
            for s in range(2):
                h = 2 * i + s
                dw = dw2[s * CHUNK : (s + 1) * CHUNK]
                low = decays(cum, cum_t, allowed, h)
                dt_row = dt_t[h : h + 1, :]
                scaled = low * dt_row
                cross_grad = cross_grad + dw * scaled
                g = low * cross
                weights.append((g * dt_row).astype(bf16))
                r = dw * g
                rows_acc[h : h + 1, :] = jnp.sum(r, axis=0, keepdims=True)
                row_sums = jnp.where(
                    lane == h, jnp.sum(r * dt_row, axis=1, keepdims=True), row_sums
                )
            du = tn(both(*weights, 0), dy2)
            x_link = dy * expand(link, i)
            linked.append(x_link.astype(bf16))
            link_prod.append(x_link * carried[:, cols])
            x_in = expand(ins_, i)
            fed.append((u * x_in).astype(bf16))
            x_to = towards[:, cols]
            end_prod.append(u * x_to * expand(to_end, i))
            skip = kern_ref[KC : KC + 1, cols]
            du = du + x_in * x_to + skip * dy
            dskip[i] = dskip[i] + jnp.sum(dy * u, axis=0, keepdims=True)
            dus.append(du)
        linked = jnp.concatenate(linked, axis=1)
        fed = jnp.concatenate(fed, axis=1)
        cross_low = cross_grad.astype(bf16)
        dc_map = nn(linked, state_low) + nn(cross_low, bmap)
        db_map = nn(fed, ds_low) + tn(cross_low, cmap)
        y_sum = nn(jnp.concatenate(link_prod, axis=1), pick, highest)
        v = nn(jnp.concatenate(end_prod, axis=1), pick, highest)
        col_sums = rows_acc[...].T
        keep_sum = nn(nt(jnp.ones((8, N), f32), ds * state, highest), pick, highest)[0:1, :]
        d_end = keep * keep_sum + jnp.sum(v * dt, axis=0, keepdims=True)
        dcum = row_sums - col_sums * dt + y_sum - v * dt
        dcum = dcum + jnp.where(iota((CHUNK, LANES), 0) == CHUNK - 1, d_end, 0.0)
        dld = nn(triangle(False), dcum, highest)
        ddt = col_sums + v - dld * par_ref[1:2, :]
        dstep = ddt * jax.nn.sigmoid(raw)
        dstep_ref[rows, :] = dstep.astype(bf16)
        dbias = dbias + jnp.sum(dstep, axis=0, keepdims=True)
        drate = drate + jnp.sum(dld * ld, axis=0, keepdims=True)
        dstate[...] = per_state_row(keep, heads) * ds + tn(linked, cmap)
        grads = dus + [db_map, dc_map]
        for i in range(tiles):
            cols = slice(i * LANES, (i + 1) * LANES)
            dpre = grads[i] * sigs[i] * (1.0 + pre[i] * (1.0 - sigs[i]))
            dcs[HALO + r0 : HALO + r0 + CHUNK, cols] = dpre
            for j in range(KC):
                at = r0 + HALO - (KC - 1) + j
                term = jnp.where(off >= KC - 1 - j, ext[at : at + CHUNK, cols] * dpre, 0.0)
                dkern[j][i] = dkern[j][i] + jnp.sum(term, axis=0, keepdims=True)
    for i in range(tiles):
        cols = slice(i * LANES, (i + 1) * LANES)
        for j in range(KC):
            dkern_ref[j : j + 1, cols] = dkern[j][i]
        dkern_ref[KC : KC + 1, cols] = dskip[i] if i < pairs else jnp.zeros((1, LANES), f32)
        dkern_ref[KC + 1 :, cols] = jnp.zeros((8 - KC - 1, LANES), f32)
    dpar_ref[...] = jnp.zeros_like(dpar_ref)
    dpar_ref[0:1, :] = dbias
    dpar_ref[1:2, :] = drate

    dsl_pad[:HALO, :] = jnp.full((HALO, LANES), 1 << 20, jnp.int32)
    dsl_pad[HALO : HALO + tokens, :] = dsl_ref[...]
    dsl_pad[HALO + tokens :, :] = jnp.full((HALO, LANES), 1 << 20, jnp.int32)
    for start, count in [(-HALO, HALO)] + [(c * CHUNK, CHUNK) for c in range(chunks)]:
        keeps = []
        for q in range(KC):
            at = start + q
            place = at + iota((count, LANES), 0)
            reach = place - dsl_pad[HALO + at : HALO + at + count, :]
            keeps.append(jnp.where(reach >= q, 1.0, 0.0))
        for i in range(tiles):
            cols = slice(i * LANES, (i + 1) * LANES)
            acc = None
            for q in range(KC):
                at = HALO + start + q
                term = dcs[at : at + count, cols] * keeps[q] * kern_ref[KC - 1 - q : KC - q, cols]
                acc = term if acc is None else acc + term
            if start < 0:
                dhalo_ref[:, cols] = acc
            else:
                dim_ref[start : start + count, cols] = acc.astype(bf16)


def project_back_kernel(received, me_ref, *refs):
    gots = refs[:received]
    (zq_ref, dim_ref, dhalo_ref, dkv_ref, dstep_ref, cos_ref, sin_ref, w_ref,
     dis_ref, dmk_ref, own_ref, *parts) = refs[received:]
    tokens = zq_ref.shape[0]
    di = zq_ref.shape[1] - LANES
    size = tokens // 4
    tail = slice(tokens - HALO, tokens)
    dis_ref[:, :di] = dim_ref[:, :di]
    dis_ref[tail, :di] = (dim_ref[tail, :di].astype(f32) + dhalo_ref[:, :di]).astype(bf16)
    dis_ref[:, di:] = dstep_ref[...]
    dmk_ref[:, : 2 * N] = dim_ref[:, di:]
    dmk_ref[tail, : 2 * N] = (dim_ref[tail, di:].astype(f32) + dhalo_ref[:, di:]).astype(bf16)
    dkv = dkv_ref[...]
    for got in gots:
        dkv = dkv + got[...].astype(f32)
    turned = dkv * cos_ref[...] - swap_halves(dkv) * sin_ref[...]
    dmk_ref[:, 2 * N :] = jnp.where(low_lanes(dkv.shape), turned, dkv).astype(bf16)
    first, second = di + LANES, 2 * di + 2 * LANES
    for k in (1, 2, 3, 0):
        rows = block_rows(me_ref, k, size)
        part = nt(zq_ref[rows, :], w_ref[:, :first])
        part = part + nt(dis_ref[rows, :], w_ref[:, first:second])
        part = part + nt(dmk_ref[rows, :], w_ref[:, second:])
        if k:
            parts[k - 1][...] = part.astype(bf16)
        else:
            own_ref[...] = part


def products_kernel(count, me_ref, *refs):
    for i in range(count):
        refs[2 * count + i][...] = tn(refs[2 * i][...], refs[2 * i + 1][...]).astype(bf16)


def last_products_kernel(
    me_ref, h_ref, dis_ref, dmk_ref, kern_ref, par_ref, one_ref, two_ref, is_ref, own_ref, *parts
):
    di = dis_ref.shape[1] - LANES
    rows = h_ref.shape[1]
    size = rows // 4
    width = one_ref.shape[1]
    wide = dmk_ref.shape[1]
    is_ref[:rows, :] = tn(h_ref[...], dis_ref[...]).astype(bf16)
    small = jnp.concatenate([kern_ref[:, :di], par_ref[...]], axis=1)
    is_ref[rows:, :] = both(small, jnp.zeros_like(small), 0).astype(bf16)
    pieces = []
    for ref in (one_ref, two_ref):
        for at in range(0, width, wide):
            piece = ref[0:1, at : at + wide]
            if piece.shape[1] < wide:
                piece = both(piece, jnp.zeros((1, wide - piece.shape[1]), f32), 1)
            pieces.append(piece)
    taps = both(kern_ref[:KC, di:], jnp.zeros((KC, wide - 2 * N), f32), 1)
    pieces.append(taps)
    pieces.append(jnp.zeros((HALO - KC - len(pieces) + 1, wide), f32))
    extra = jnp.concatenate(pieces, axis=0)
    for k in range(4):
        at = pl.ds(pl.multiple_of((me_ref[0] ^ k) * size, size), size)
        block = tn(h_ref[:, at], dmk_ref[...])
        out = parts[k - 1] if k else own_ref
        out[:size, :] = block.astype(out.dtype)
        out[size:, :] = extra.astype(out.dtype)


def share_sum_kernel(me_ref, own_ref, r1, r2, r3, out_ref):
    size = own_ref.shape[0] - HALO
    wide = own_ref.shape[1]
    near = own_ref[...] + r1[...].astype(f32)
    far = r2[...].astype(f32) + r3[...].astype(f32)
    total = near + far
    out_ref[:, : 2 * N] = total[:, : 2 * N].astype(bf16)
    first = me_ref[0] // 2 == 0
    mine, other = near[:size, 2 * N :], far[:size, 2 * N :]
    a, b = jnp.where(first, mine, other), jnp.where(first, other, mine)
    low = low_lanes(a.shape)
    out_ref[:size, 2 * N : 2 * N + LANES] = jnp.where(low, a, pltpu.roll(b, HEAD_WIDTH, 1)).astype(bf16)
    out_ref[:size, 2 * N + LANES :] = jnp.where(low, pltpu.roll(a, HEAD_WIDTH, 1), b).astype(bf16)
    out_ref[size:, 2 * N : wide] = total[size:, 2 * N :].astype(bf16)
    out_ref[size:, wide:] = jnp.zeros((HALO, out_ref.shape[1] - wide), bf16)


def trade(array, k):
    places = range(lax.axis_size("tensor"))
    return lax.ppermute(array, "tensor", [(i, i ^ k) for i in places])


def trades(arrays):
    return [trade(array, k + 1) for k, array in enumerate(arrays)]


def from_shard(array, distance):
    places = range(lax.axis_size("seq"))
    route = [(i - distance, i) for i in places if i - distance in places]
    return lax.ppermute(array, "seq", route)


def from_shards(array, sign):
    return [from_shard(array, sign * d) for d in range(1, lax.axis_size("seq"))]


def other_core(array):
    return lax.ppermute(array, "pipe", [(0, 1), (1, 0)])


def finish(me, resid, own, *parts):
    (out_own,) = call(
        out_kernel, [sds(resid.shape, bf16)], [me, resid, own, *trades(parts)], name="layer_out"
    )
    return [out_own] + trades([out_own] * 3)


def last_out(saved, wt, me, after):
    resid, hidden = saved[-5], saved[-1]
    parts = call(
        down_kernel,
        [sds(resid.shape, f32)] + [sds(resid.shape, bf16)] * 3,
        [me, *fars(hidden, wt[3])],
        name="last_down",
        after=after,
    )
    return finish(me, resid, *parts)


def forward(x, x_own, wt, geo, last):
    w_cat, w_out, w_gu, w_down, gain_one, gain_two, kern, par = wt
    me, dsl, cos, sin, di = geo
    heads = di // P_SIZE
    tokens = dsl.shape[0]
    size, width = x_own.shape
    ff = w_down.value.shape[0]
    seqs = lax.axis_size("seq")
    wide = di + 2 * N
    low_parts = [sds((size, width), bf16)] * 3
    h, z, im, step, q, kv = call(
        partial(project_kernel, len(x), di),
        [
            Far(sds((tokens, width), bf16)),
            sds((tokens, di), f32),
            sds((tokens, wide), bf16),
            sds((tokens, LANES), f32),
            sds((tokens, LANES), bf16),
            sds((tokens, LANES), bf16),
        ],
        [me, *x, gain_one, w_cat, cos, sin],
        [pltpu.VMEM((tokens, width), bf16)] if len(x) > 1 else [],
        name="project",
    )
    halo = from_shard(im[tokens - HALO :], 1)
    kvs = [kv] + from_shards(kv, 1)
    mix0, cmap, lfac, packet = call(
        partial(ssm_forward_kernel, heads),
        [
            sds((tokens, di), f32),
            sds((tokens, N), bf16),
            sds((tokens, LANES), f32),
            sds((di + HALO, N), bf16),
        ],
        [me, im, halo, step, dsl, kern, par],
        [pltpu.VMEM((tokens + HALO, wide), f32), pltpu.VMEM((di, N), f32)],
        name="ssm_forward",
    )
    packets = from_shards(packet, 1)
    attn, lse = call(
        partial(attention_kernel, seqs),
        [sds((tokens, LANES), f32), Far(sds((tokens, LANES), f32))],
        [me, q, dsl, *kvs],
        [pltpu.VMEM((seqs, tokens, LANES), bf16)] * 2,
        name="attention",
    )
    mixed, ga, state_in, own, *parts = call(
        partial(mix_kernel, heads, len(packets)),
        [
            Far(sds((tokens, di), f32)),
            Far(sds((tokens, di + LANES), bf16)),
            Far(sds((di, N), f32)),
            sds((size, width), f32),
            *low_parts,
        ],
        [me, *packets, mix0, cmap, lfac, z, attn, w_out],
        name="mix",
    )
    resid, h_own = call(
        norm_two_kernel,
        [sds((size, width), f32), sds((size, width), bf16)],
        [me, x_own, own, *trades(parts), gain_two],
        name="norm_two",
    )
    h_two, gate, up, hidden, *parts = call(
        mlp_kernel,
        [
            *[
                Far(o) if not last else o
                for o in [sds((tokens, width), bf16)] + [sds((tokens, ff), bf16)] * 3
            ],
            *([] if last else [sds((size, width), f32), *low_parts]),
        ],
        [me, h_own, *trades([h_own] * 3), *fars(w_gu, w_down)],
        name="mlp",
    )
    out = None if last else finish(me, resid, *parts)
    saved = (
        x_own, h, z, im, step, q, halo, kvs, cmap, lfac, packet, attn, lse, mixed, ga, state_in,
        resid, h_two, gate, up, hidden,
    )
    return out, saved


def products(*pairs, me, after):
    return call(
        partial(products_kernel, len(pairs)),
        [Far(sds((a.shape[1], b.shape[1]), bf16)) for a, b in pairs],
        [me, *[x for a, b in pairs for x in (Far(a), b)]],
        name="products",
        after=after,
    )


def last_products(me, h, d_is, d_mk, *small, after=()):
    size = h.shape[1] // 4 + HALO
    wide = d_mk.shape[1]
    own_is, own, *parts = call(
        last_products_kernel,
        [Far(sds((h.shape[1] + HALO, d_is.shape[1]), bf16)), sds((size, wide), f32)]
        + [sds((size, wide), bf16)] * 3,
        [me, Far(h), d_is, d_mk, *small],
        name="last_products",
        after=after,
    )
    (shared,) = call(
        share_sum_kernel,
        [sds((size, 2 * N + 2 * LANES), bf16)],
        [me, own, *trades(parts)],
        name="share_sum",
    )
    return own_is, shared


def line_sum(x, cores):
    n = lax.axis_size("seq")
    here = lax.axis_index("seq")
    half = n // 2

    def send(x, route):
        route = [(c * n + a, c * n + b) for c in cores for a, b in route]
        return lax.ppermute(x, ("pipe", "seq"), route)

    for r in range(1, half):
        x = add(x, send(x, [(r - 1, r), (n - r, n - 1 - r)]))
    if n > 1:
        x = add(x, send(x, [(half - 1, half), (half, half - 1)]))
    for r in range(half - 1, 0, -1):
        got = send(x, [(r, r - 1), (n - 1 - r, n - r)])
        x = jnp.where((here == r - 1) | (here == n - r), got, x)
    return x


def add(a, b):
    return (a.astype(f32) + b.astype(f32)).astype(bf16)


def own_core_sum(first, second):
    core = lax.axis_index("pipe")
    keep = jnp.where(core == 0, first, second)
    return line_sum(add(keep, other_core(jnp.where(core == 0, second, first))), [0, 1])


def both_sum(arrays, *axes):
    return list(lax.psum(tuple(arrays), axes))


def backward(g, g_own, saved, wt, geo, first=(), second=(), third=()):
    (
        x_own, h, z, im, step, q, halo, kvs, cmap, lfac, packet, attn, lse, mixed, ga, state_in,
        resid, h_two, gate, up, hidden,
    ) = saved
    w_cat, w_out, w_gu, w_down, gain_one, gain_two, kern, par = wt
    me, dsl, cos, sin, di = geo
    heads = di // P_SIZE
    tokens = dsl.shape[0]
    size, width = x_own.shape
    ff = w_down.value.shape[0]
    seqs = lax.axis_size("seq")
    wide = di + 2 * N
    low_parts = [sds((size, width), bf16)] * 3
    dgate, dup, g_cat, own, *parts = call(
        partial(mlp_back_kernel, len(g)),
        [
            sds((tokens, ff), bf16),
            sds((tokens, ff), bf16),
            sds((tokens, width), bf16),
            sds((size, width), f32),
            *low_parts,
        ],
        [me, *g, *(fars(gate, up) if len(g) > 1 else (gate, up)), *fars(w_gu, w_down)],
        name="mlp_back",
        after=first,
    )
    got = trades(parts)
    d_resid, d_own, grad_gain_two = call(
        norm_back_kernel,
        [sds((size, width), f32), sds((size, width), bf16), sds((8, width), f32)],
        [me, g_own, own, *got, Far(resid), gain_two],
        name="norm_two_back",
        after=second,
    )
    early = products((h_two, dgate), (h_two, dup), (hidden, g_cat), me=me, after=[d_own])
    d_branch, d_mixed, dz, d_attn, packet_back = call(
        partial(mixer_back_kernel, heads),
        [
            sds((tokens, width), bf16),
            sds((tokens, di), f32),
            sds((tokens, di), bf16),
            sds((tokens, LANES), bf16),
            sds((di + HALO, N), bf16),
        ],
        [me, d_own, *trades([d_own] * 3), *fars(w_out, z, mixed, cmap, lfac, packet)],
        name="mixer_back",
        after=early,
    )
    packets = from_shards(packet_back, -1)
    zq, *dkvs = call(
        partial(attention_back_kernel, seqs),
        [sds((tokens, di + LANES), bf16), sds((tokens, LANES), f32)]
        + [sds((tokens, LANES), bf16)] * (seqs - 1),
        [me, *fars(q, dsl, attn, lse), d_attn, dz, *fars(cos, sin, *kvs)],
        [pltpu.VMEM((seqs, tokens, LANES), bf16)] * 2
        + [pltpu.VMEM((seqs, tokens, LANES), f32)] * 2,
        name="attention_back",
    )
    got_kv = [from_shard(dkvs[d], -d) for d in range(1, seqs)]
    d_im, d_halo, d_step, grad_kern, grad_par = call(
        partial(ssm_back_kernel, heads, len(packets)),
        [
            sds((tokens, wide), bf16),
            sds((HALO, wide), f32),
            sds((tokens, LANES), bf16),
            sds((8, wide), f32),
            sds((8, LANES), f32),
        ],
        [me, *packets, *fars(im, halo, step, dsl), kern, par, d_mixed, Far(state_in)],
        [
            pltpu.VMEM((tokens + HALO, wide), f32),
            pltpu.VMEM((tokens + 2 * HALO, wide), f32),
            pltpu.VMEM((tokens + 2 * HALO, LANES), jnp.int32),
            pltpu.VMEM((tokens // CHUNK, di, N), f32),
            pltpu.VMEM((di, N), f32),
            pltpu.VMEM((LANES, LANES), f32),
        ],
        name="ssm_back",
    )
    back_halo = from_shard(d_halo, -1)
    d_is, d_mk, own, *parts = call(
        partial(project_back_kernel, len(got_kv)),
        [
            sds((tokens, di + LANES), bf16),
            sds((tokens, 2 * N + LANES), bf16),
            sds((size, width), f32),
            *low_parts,
        ],
        [me, *got_kv, zq, d_im, back_halo, dkvs[0], d_step, *fars(cos, sin, w_cat)],
        name="project_back",
    )
    got = trades(parts)
    middle = products((ga, d_branch), (h, zq), me=me, after=[d_is, *third])
    dx_own, grad_gain_one = call(
        norm_back_kernel,
        [sds((size, width), bf16), sds((8, width), f32)],
        [me, d_resid, own, *got, Far(x_own), gain_one],
        name="norm_one_back",
        after=middle,
    )
    dx = [dx_own] + trades([dx_own] * 3)
    last = h, d_is, d_mk, grad_kern, grad_par, grad_gain_one, grad_gain_two
    return dx, early, middle, last


def in_order(pieces, me):
    size = pieces[0].shape[0]
    whole = jnp.zeros((size * len(pieces), pieces[0].shape[1]), pieces[0].dtype)
    for k, piece in enumerate(pieces):
        whole = lax.dynamic_update_slice_in_dim(whole, piece, (me ^ k) * size, 0)
    return whole


def body(
    inputs,
    cotangent,
    doc_lengths,
    norm_one,
    w_gate_z,
    w_inner_x,
    w_bc,
    w_step,
    conv_inner,
    conv_bc,
    step_bias,
    decay_log,
    skip_gain,
    w_mix_out,
    w_query,
    keyval_weight,
    w_attn_out,
    norm_two,
    w_gate_up,
    w_down,
):
    core = lax.axis_index("pipe")
    place = lax.axis_index("tensor")
    me = jnp.stack([place, core]).astype(jnp.int32)
    tokens, width = inputs.shape[1:]
    di = w_gate_z.shape[2]
    heads = di // P_SIZE
    size = tokens // lax.axis_size("tensor")

    keyval_head = place * (w_query.shape[2] // HEAD_WIDTH) // (QUERY_HEADS // KEY_HEADS)
    key_at = keyval_head * HEAD_WIDTH
    value_at = KEY_HEADS * HEAD_WIDTH + key_at
    own_cat = jnp.concatenate(
        [
            w_gate_z[0],
            w_query[0],
            w_inner_x[0],
            jnp.pad(w_step[0], ((0, 0), (0, LANES - heads))),
            w_bc[0],
            lax.dynamic_slice_in_dim(keyval_weight[0], key_at, HEAD_WIDTH, 1),
            lax.dynamic_slice_in_dim(keyval_weight[0], value_at, HEAD_WIDTH, 1),
        ],
        axis=1,
    )
    own_out = jnp.concatenate([w_mix_out[0], w_attn_out[0]], axis=0)
    wide = di + 2 * N
    own_kern = jnp.concatenate(
        [
            jnp.concatenate([conv_inner[0], conv_bc[0]], axis=1),
            jnp.pad(jnp.repeat(skip_gain, P_SIZE, axis=1), ((0, KC - 1), (0, 2 * N))),
        ],
        axis=0,
    )
    own_par = jnp.pad(
        jnp.concatenate([step_bias, jnp.exp(decay_log)], axis=0), ((0, 6), (0, LANES - heads))
    )
    own_small = jnp.concatenate(
        [
            jnp.pad(jnp.concatenate([norm_one, norm_two], axis=0), ((0, 6), (0, 0))),
            jnp.pad(
                jnp.concatenate([own_kern, own_par], axis=1),
                ((0, 0), (0, width - wide - LANES)),
            ),
        ],
        axis=0,
    )
    mine = (own_cat, own_out, w_gate_up[0], w_down[0], own_small)
    theirs = [other_core(w) for w in mine]

    def weights(layer):
        small = jnp.where(core == layer, mine[-1], theirs[-1])
        return (
            *[Far(a, b, layer) for a, b in zip(mine[:-1], theirs[:-1])],
            small[0:1], small[1:2], small[8:, :wide], small[8:, wide : wide + LANES],
        )

    layers = [weights(0), weights(1)]

    x = lax.dynamic_index_in_dim(inputs, core, 0, keepdims=False)
    top = lax.dynamic_index_in_dim(cotangent, core, 0, keepdims=False)
    lengths = lax.dynamic_index_in_dim(doc_lengths, core, 0, keepdims=False)
    first = lax.axis_index("seq") * tokens
    spots = first + jnp.arange(tokens, dtype=jnp.int32)
    before = jnp.cumsum(lengths)[None, :] <= spots[:, None]
    starts = jnp.sum(jnp.where(before, lengths[None, :], 0), axis=1)
    dsl = jnp.broadcast_to((starts - first)[:, None], (tokens, LANES)).astype(jnp.int32)
    half = HEAD_WIDTH // 2
    frequency = rope_base ** (-2.0 * jnp.arange(half, dtype=f32) / HEAD_WIDTH)
    angles = (spots - starts).astype(f32)[:, None] * frequency[None, :]
    cos, sin = jnp.cos(angles), jnp.sin(angles)
    cos = jnp.concatenate([cos] * 4, axis=1)
    sin = jnp.concatenate([-sin, sin] * 2, axis=1)
    geo = (me, dsl, cos, sin, di)

    def share(whole):
        return lax.dynamic_slice_in_dim(whole, place * size, size, 0)

    out_0, saved_0 = forward([x], share(x), layers[0], geo, False)
    _, saved_1 = forward(out_0, out_0[0], layers[1], geo, True)
    dx_1, early_1, middle_1, last_1 = backward([top], share(top), saved_1, layers[1], geo)
    early_1 = both_sum(early_1, "pipe", "seq")
    last_1 = last_products(me, *last_1, after=[dx_1[0]])
    late_1 = both_sum([*middle_1, last_1[0]], "seq", "pipe")
    dx_0, early_0, middle_0, last_0 = backward(
        dx_1, dx_1[0], saved_0, layers[0], geo, [last_1[0]], early_1, late_1
    )
    *last_0, shared_0 = last_products(me, *last_0)
    sums_0 = both_sum([*early_0, *middle_0, *last_0], "pipe", "seq")
    sums_1 = [*early_1, *late_1]
    shared = own_core_sum(shared_0, last_1[1])
    out_1 = last_out(saved_1, layers[1], me, [dx_0[0]])

    gate, up, down, out, zq, last = [
        jnp.where(core == 0, a, b) for a, b in zip(sums_0, sums_1)
    ]
    quarter = shared[: width // 4]
    every = shared[width // 4 :].astype(f32)
    shared = in_order([quarter] + trades([quarter] * 3), place).astype(f32)
    gate, up, down, out, zq = [a.astype(f32) for a in (gate, up, down, out, zq)]
    own_small = last[width:].astype(f32)
    last = last[:width].astype(f32)
    step_128 = 2 * N + LANES
    count = -(-width // step_128)
    gain_one = every[:count, :step_128].reshape(-1)[:width]
    gain_two = every[count : 2 * count, :step_128].reshape(-1)[:width]
    taps = every[2 * count : 2 * count + KC, : 2 * N]
    skip = jnp.sum(own_small[KC, :di].reshape(heads, P_SIZE), axis=1)

    def both_micros(first_layer, second_layer):
        a, b = in_order(first_layer, place), in_order(second_layer, place)
        keep = jnp.where(core == 0, a, b)
        got = other_core(jnp.where(core == 0, b, a))
        return jnp.stack([jnp.where(core == 0, keep, got), jnp.where(core == 0, got, keep)])

    layer_out = both_micros(out_0, out_1)
    input_grad = both_micros(dx_0, dx_1)
    results = (
        layer_out,
        input_grad,
        gain_one,
        zq[:, :di],
        last[:, :di],
        shared[:, : 2 * N],
        last[:, di : di + heads],
        own_small[:KC, :di],
        taps,
        own_small[0, di : di + heads],
        own_small[1, di : di + heads],
        skip,
        out[:di],
        zq[:, di:],
        shared[:, 2 * N :],
        out[di:],
        gain_two,
        jnp.stack([gate, up]),
        down,
    )
    return tuple(r[None] for r in results)


def solution(mesh):
    token_spec = P(None, "seq", None)
    columns = P("pipe", None, "tensor")
    rows = P("pipe", "tensor", None)
    layer = P("pipe", None, None)
    vector = P("pipe", None)
    heads = P("pipe", "tensor")
    outs = P("pipe", None, "seq", None)
    gate_up = P("pipe", None, None, "tensor")
    return jax.shard_map(
        body,
        mesh=mesh,
        in_specs=(
            token_spec, token_spec, P(), vector, columns, columns, layer, columns, columns, layer,
            heads, heads, heads, rows, columns, layer, rows, vector, gate_up, rows,
        ),
        out_specs=(
            outs, outs, vector, columns, columns, layer, columns, columns, layer,
            heads, heads, heads, rows, columns, layer, rows, vector, gate_up, rows,
        ),
        check_vma=False,
    )
```
